512 devices in a mesh: basin: 64 (over z, x), reach: 8 (over y, core).
Axes of the slice: x: 4, y: 4, z: 16, core: 2. Of those that a mesh axis runs over, the one named last changes fastest.
Arguments:
- reach_residual: float32 [384, 24, 128], P('basin', 'reach'), may hold values from -4 to 4
- chain_inv: float32 [384, 24, 128, 128], P('basin', 'reach'), may hold values from -1 to 2
- chain_link: float32 [384, 24, 128, 128], P('basin', 'reach'), may hold values from -1 to 1
- outlet_link: float32 [384, 128, 128], P('basin'), may hold values from -0.5 to 0.5
- junction_inv: float32 [384, 128, 128], P('basin'), may hold values from -1 to 1
- junction_residual: float32 [384, 128], P('basin'), may hold values from -6 to 6
- upper_junction: int32 [384], P('basin'), may hold values from 0 to 383
- lower_junction: int32 [384], P('basin'), may hold values from 0 to 383
- cell_cotangent: float32 [384, 24, 128], P('basin', 'reach'), may hold values from -4 to 4
- junction_cotangent: float32 [384, 128], P('basin'), may hold values from -6 to 6
Outputs:
- cell_update: float32 [384, 24, 128], P('basin', 'reach')
- section_update: float32 [384, 128], P('basin')
- cell_adjoint: float32 [384, 24, 128], P('basin', 'reach')
- junction_adjoint: float32 [384, 128], P('basin')
The draws below stay inside these ranges and needn't reach their ends.
Inputs may be any that keep to these rules, and one draw needn't show every extreme that they name: `upper_junction`: junction ids. `lower_junction`: junction ids.
All inputs are finite; a program needn't handle non-finite values.
Results may differ from the reference program's by a relative error of at most 0.00014.
Values sent between devices are 32-bit elements; how exact they have to be, the bound alone decides.
No kernel may reach another device: no remote copies, remote signals or barrier semaphores. Data moves between devices by JAX's collectives and lax.ppermute only.
A program may use at most 64 MiB of HBM per device.

```python
import math
import jax
import jax.numpy as jnp
from jax import lax

C = 128
SWEEPS = 4
REACH_BLOCKS = 24
SUBBASIN_COUNT = 384
JUN = 384


def with_diagonal(diagonal, spread, factor):
    eye_block = jnp.eye(C, dtype=jnp.float32)
    return eye_block * diagonal[..., None] + (1.0 - eye_block) * spread * factor


def draw_chain_inv(key, part):
    key = jax.random.fold_in(key, 11)
    first, second = jax.random.split(key)
    diagonal = jnp.exp(jax.random.uniform(first, (SUBBASIN_COUNT, REACH_BLOCKS, C), jnp.float32, -0.15, 0.15))
    spread = jnp.clip(jax.random.normal(second, (SUBBASIN_COUNT, REACH_BLOCKS, C, C), jnp.float32), -4.0, 4.0)
    return with_diagonal(diagonal, spread, 0.2 / math.sqrt(C))


def draw_chain_link(key, part):
    key = jax.random.fold_in(key, 12)
    random_keys = jax.random.split(key, 4)
    top_rate = 0.8
    flow_rates = jnp.exp(jax.random.uniform(random_keys[0], (SUBBASIN_COUNT, 1, C), jnp.float32, math.log(0.3 / REACH_BLOCKS), math.log(top_rate)))
    storm_pulses = jax.random.bernoulli(random_keys[1], 0.08, (SUBBASIN_COUNT, REACH_BLOCKS, 1))
    seepage_losses = jax.random.uniform(random_keys[2], (SUBBASIN_COUNT, REACH_BLOCKS, 1), jnp.float32, 0.5, 0.8)
    recession_factor = jnp.exp(-flow_rates) * jnp.where(storm_pulses, seepage_losses, 1.0)
    spread = jnp.clip(jax.random.normal(random_keys[3], (SUBBASIN_COUNT, REACH_BLOCKS, C, C), jnp.float32), -4.0, 4.0)
    return with_diagonal(recession_factor, spread, 0.15 / math.sqrt(C))


def draw_junction_inv(key, part):
    key = jax.random.fold_in(key, 13)
    first, second = jax.random.split(key)
    diagonal = jax.random.uniform(first, (JUN, C), jnp.float32, 0.3, 0.55)
    spread = jnp.clip(jax.random.normal(second, (JUN, C, C), jnp.float32), -4.0, 4.0)
    return with_diagonal(diagonal, spread, 0.1 / math.sqrt(C))


def place_ends(result, own_key, low, top_value):
    spot = [jax.random.randint(jax.random.fold_in(own_key, axis), (), 0, length) for axis, length in enumerate(result.shape)]
    main_axis = result.shape.index(max(result.shape))
    next_to = spot[:main_axis] + [(spot[main_axis] + 1) % result.shape[main_axis]] + spot[main_axis + 1:]
    return result.at[tuple(spot)].set(low).at[tuple(next_to)].set(top_value)


def level_of(own_key, extent, cuts, least, top_value):
    level = 1.0
    for dim, shards_of in cuts:
        draws = jax.random.uniform(jax.random.fold_in(jax.random.fold_in(own_key, 6), dim), (shards_of,), jnp.float32, least / len(cuts), top_value / len(cuts))
        level = level * jnp.repeat(jnp.exp(draws), extent[dim] // shards_of).reshape((-1,) + (1,) * (len(extent) - 1 - dim))
    return level


def bell_draw(own_key, extent, width, bound, shards=(), kind=jnp.bfloat16):
    loudness = level_of(own_key, extent, shards, -0.22, 0.18) if shards else 1.0
    array = jax.random.normal(own_key, extent, jnp.float32) * width * loudness
    return jnp.minimum(jnp.maximum(array, -bound), bound).astype(kind)


def setup_inputs(seed: int = 0) -> dict:
    streams_of = jax.random.split(jax.random.key(seed), 11)
    reach_residual = bell_draw(streams_of[0], (SUBBASIN_COUNT, REACH_BLOCKS, C), 0.5, 4.0, ((0, 64), (1, 8)), jnp.float32)
    chain_inv = draw_chain_inv(jax.random.fold_in(streams_of[10], 71), 0)
    chain_link = draw_chain_link(jax.random.fold_in(streams_of[10], 71), 0)
    outlet_link = bell_draw(streams_of[3], (SUBBASIN_COUNT, C, C), C ** -0.5, 0.5, ((0, 64),), jnp.float32)
    junction_inv = draw_junction_inv(jax.random.fold_in(streams_of[10], 71), 0)
    junction_residual = bell_draw(streams_of[5], (JUN, C), 1.0, 6.0, ((0, 64),), jnp.float32)
    upper_junction = place_ends(jax.random.randint(streams_of[6], (SUBBASIN_COUNT,), 0, JUN), jax.random.fold_in(streams_of[6], 1), 0, JUN - 1).astype(jnp.int32)
    lower_junction = place_ends(jax.random.randint(streams_of[7], (SUBBASIN_COUNT,), 0, JUN), jax.random.fold_in(streams_of[7], 1), 0, JUN - 1).astype(jnp.int32)
    cell_cotangent = bell_draw(streams_of[8], (SUBBASIN_COUNT, REACH_BLOCKS, C), 0.5, 4.0, ((0, 64), (1, 8)), jnp.float32)
    junction_cotangent = bell_draw(streams_of[9], (JUN, C), 1.0, 6.0, ((0, 64),), jnp.float32)
    return dict(reach_residual=reach_residual, chain_inv=chain_inv, chain_link=chain_link, outlet_link=outlet_link, junction_inv=junction_inv, junction_residual=junction_residual, upper_junction=upper_junction, lower_junction=lower_junction, cell_cotangent=cell_cotangent, junction_cotangent=junction_cotangent)


precise = lax.Precision.HIGHEST


def product(former, latter):
    return jnp.einsum("sij,sjk->sik", former, latter, precision=precise)


def applied(matrix, vector):
    return jnp.einsum("sij,sj->si", matrix, vector, precision=precise)


def applied_transposed(matrix, vector):
    return jnp.einsum("sji,sj->si", matrix, vector, precision=precise)


def reference(reach_residual, chain_inv, chain_link, outlet_link, junction_inv, junction_residual, upper_junction, lower_junction, cell_cotangent, junction_cotangent):
    blocks = reach_residual.shape[1]
    tile_width = reach_residual.shape[2]
    junctions = junction_residual.shape[0]
    multiplier = jnp.einsum("slij,sljk->slik", chain_inv, chain_link, precision=precise)
    forced = jnp.einsum("slij,slj->sli", chain_inv, reach_residual, precision=precise)
    transfer = multiplier[:, 0]
    outflow = forced[:, 0]
    for number in range(1, blocks):
        transfer = product(multiplier[:, number], transfer)
        outflow = applied(multiplier[:, number], outflow) + forced[:, number]
    schur_tile = product(outlet_link, transfer)
    outlet_push = applied(outlet_link, outflow)
    junction_rows = jnp.arange(junctions)[:, None]
    lower_onehot = (junction_rows == lower_junction[None, :]).astype(jnp.float32)
    upper_onehot = (junction_rows == upper_junction[None, :]).astype(jnp.float32)
    sections = jnp.zeros((junctions, tile_width), jnp.float32)
    for sweep_index in range(SWEEPS):
        inflow_terms = outlet_push + applied(schur_tile, sections[upper_junction])
        inflow = jnp.dot(lower_onehot, inflow_terms, precision=precise)
        sections = applied(junction_inv, junction_residual + inflow)
    carried = sections[upper_junction]
    cell_rows = []
    for number in range(blocks):
        carried = applied(multiplier[:, number], carried) + forced[:, number]
        cell_rows.append(carried)
    cell_update = jnp.stack(cell_rows, axis=1)
    backward = cell_cotangent[:, blocks - 1]
    for number in range(blocks - 2, -1, -1):
        backward = cell_cotangent[:, number] + applied_transposed(multiplier[:, number + 1], backward)
    upward = applied_transposed(multiplier[:, 0], backward)
    adjoint = jnp.zeros((junctions, tile_width), jnp.float32)
    for sweep_index in range(SWEEPS):
        relief = applied_transposed(junction_inv, adjoint)
        adjoint_terms = upward + applied_transposed(schur_tile, relief[lower_junction])
        adjoint = junction_cotangent + jnp.dot(upper_onehot, adjoint_terms, precision=precise)
    relief = applied_transposed(junction_inv, adjoint)
    carried = cell_cotangent[:, blocks - 1] + applied_transposed(outlet_link, relief[lower_junction])
    collected = [carried]
    for number in range(blocks - 2, -1, -1):
        carried = cell_cotangent[:, number] + applied_transposed(multiplier[:, number + 1], carried)
        collected.append(carried)
    cell_adjoint = jnp.stack(collected[::-1], axis=1)
    return (cell_update, sections, cell_adjoint, adjoint)
```

```python
import jax
import jax.numpy as jnp
from jax import lax
from jax.experimental import pallas as pl
from jax.experimental.pallas import tpu as pltpu
from jax.sharding import Mesh, PartitionSpec as P

SWEEPS = 4

precise = lax.Precision.HIGHEST


def product(left, right):
    return jnp.einsum("sij,sjk->sik", left, right, precision=precise)


def applied(matrix, vector):
    return jnp.einsum("sij,sj->si", matrix, vector, precision=precise)


def applied_transposed(matrix, vector):
    return jnp.einsum("sji,sj->si", matrix, vector, precision=precise)


def everyone(values, axis):
    count = lax.axis_size(axis)
    spread = jnp.broadcast_to(values[None], (count,) + values.shape)
    return lax.all_to_all(spread, axis, 0, 0, tiled=False)


def all_basins(rows):
    along_z = everyone(rows, "z")
    along_x = everyone(along_z, "x")
    return jnp.swapaxes(along_x, 0, 1).reshape((-1,) + rows.shape)


def packed(matrix, *vectors):
    members, _, width = matrix.shape
    rows = [matrix] + [v[:, None, :] for v in vectors]
    pad = -len(vectors) % 8
    return jnp.concatenate(rows + [jnp.zeros((members, pad, width), matrix.dtype)], axis=1)


def pick(table, rows, keep):
    count = rows.shape[0]

    def kernel(rows_ref, keep_ref, table_ref, out_ref):
        for k in range(count):
            out_ref[k] = jnp.where(keep_ref[k] > 0, table_ref[rows_ref[k]], 0.0)

    smem = pl.BlockSpec(memory_space=pltpu.SMEM)
    vmem = pl.BlockSpec(memory_space=pltpu.VMEM)
    return pl.pallas_call(
        kernel,
        out_shape=jax.ShapeDtypeStruct((count,) + table.shape[1:], table.dtype),
        in_specs=[smem, smem, vmem],
        out_specs=vmem,
    )(rows, keep, table)


def shards(
    reach_residual,
    chain_inv,
    chain_link,
    outlet_link,
    junction_inv,
    junction_residual,
    upper_junction,
    lower_junction,
    cell_cotangent,
    junction_cotangent,
):
    members, blocks, width = reach_residual.shape
    owned = junction_inv.shape[0]
    zs, xs, ys = lax.axis_size("z"), lax.axis_size("x"), lax.axis_size("y")
    z, x, y, c = (lax.axis_index(a) for a in ("z", "x", "y", "c"))
    half = members // 2
    piece = width // ys

    def mine(array):
        return lax.dynamic_slice_in_dim(array, c * half, half, 0)

    part = lax.dynamic_slice_in_dim(junction_inv, y * piece, piece, 1)
    table = lax.all_gather(packed(part, junction_residual, junction_cotangent), "z")
    table = table.reshape((zs * owned,) + table.shape[2:])

    multiplier = jnp.einsum("skij,skjl->skil", chain_inv, chain_link, precision=precise)
    forced = jnp.einsum("skij,skj->ski", chain_inv, reach_residual, precision=precise)
    local_map = multiplier[:, 0]
    local_vector = forced[:, 0]
    for number in range(1, blocks):
        local_map = product(multiplier[:, number], local_map)
        local_vector = applied(multiplier[:, number], local_vector) + forced[:, number]
    backward = cell_cotangent[:, blocks - 1]
    for number in range(blocks - 2, -1, -1):
        backward = cell_cotangent[:, number] + applied_transposed(
            multiplier[:, number + 1], backward
        )
    local_back = applied_transposed(multiplier[:, 0], backward)

    pair = lax.all_gather(packed(local_map, local_vector, local_back), "c")
    first, second = mine(pair[0]), mine(pair[1])
    first_map, second_map = first[:, :width], second[:, :width]
    chip_map = product(second_map, first_map)
    chip_vector = applied(second_map, first[:, width]) + second[:, width]
    chip_back = applied_transposed(first_map, second[:, width + 1]) + first[:, width + 1]

    chips = lax.all_gather(packed(chip_map, chip_vector, chip_back), "y")
    maps, vectors, backs = chips[:, :, :width], chips[:, :, width], chips[:, :, width + 1]
    eye = jnp.broadcast_to(jnp.eye(width, dtype=jnp.float32), (half, width, width))
    before, before_vector = eye, jnp.zeros((half, width), jnp.float32)
    reached, reached_vector = before, before_vector
    for k in range(ys):
        reached_vector = applied(maps[k], reached_vector) + vectors[k] if k else vectors[0]
        if k < ys - 1:
            reached = product(maps[k], reached) if k else maps[0]
            before = jnp.where(y == k + 1, reached, before)
            before_vector = jnp.where(y == k + 1, reached_vector, before_vector)
    outlet = mine(outlet_link)
    schur, after = outlet, outlet
    upward = jnp.zeros((half, width), jnp.float32)
    after_vector = upward
    for k in range(ys - 1, -1, -1):
        after = jnp.where(y == k, schur, after)
        after_vector = jnp.where(y == k, upward, after_vector)
        schur = product(schur, maps[k])
        upward = applied_transposed(maps[k], upward) + backs[k]
    push = applied(outlet, reached_vector)

    ends = lax.all_gather(jnp.stack([push, upward]), "c")
    push_all = jnp.concatenate([ends[0, 0], ends[1, 0]])
    upward_all = jnp.concatenate([ends[0, 1], ends[1, 1]])

    lanes = jnp.zeros((width - 2 * members,), jnp.float32)
    ids = jnp.concatenate(
        [lower_junction.astype(jnp.float32), upper_junction.astype(jnp.float32), lanes]
    )[None]
    pad = jnp.zeros((-(2 * members + 1) % 8, width), jnp.float32)
    terms = all_basins(jnp.concatenate([push_all, upward_all, ids, pad]))
    lower_all = terms[:, 2 * members, :members].reshape(-1).astype(jnp.int32)
    upper_all = terms[:, 2 * members, members : 2 * members].reshape(-1).astype(jnp.int32)

    def meeting(ids_here, ids_all):
        return (ids_here[:, None] == ids_all[None, :]).astype(jnp.float32)

    into_head = meeting(upper_junction, lower_all)
    into_tail = meeting(lower_junction, upper_all)

    plane = lax.dynamic_slice_in_dim(
        jnp.stack([upper_all, lower_all]).reshape(2, zs, xs, members), z, 1, 1
    )[:, 0]
    plane = lax.dynamic_slice_in_dim(plane, c * half, half, 2)
    wanted = jnp.transpose(plane, (1, 0, 2))
    basin, place = wanted // owned, wanted % owned
    here = (basin % xs == x).astype(jnp.int32)
    rows = (basin // xs) * owned + place
    picked = pick(table, rows.reshape(-1), here.reshape(-1))
    picked = picked.reshape(rows.shape + table.shape[1:])
    arrived = lax.all_to_all(picked, "x", 0, 0, tiled=False).sum(0)
    ends_of = lax.all_gather(arrived, "y")
    tiles = jnp.transpose(ends_of[:, :, :, :piece], (1, 2, 0, 3, 4)).reshape(2, half, width, width)
    head_inv, tail_inv = tiles[0], tiles[1]
    head_residual, tail_cotangent = ends_of[0, 0, :, piece], ends_of[0, 1, :, piece + 1]

    down = product(schur, head_inv)
    up = product(tail_inv, schur)
    push_base = push + applied(down, head_residual)
    up_base = upward + applied_transposed(up, tail_cotangent)
    both = lax.all_gather(jnp.stack([packed(down, push_base), packed(up, up_base)]), "c")
    both = jnp.concatenate([both[0], both[1]], axis=1)
    down_all, push_base = both[0, :, :width], both[0, :, width]
    up_all, up_base = both[1, :, :width], both[1, :, width]

    def split(gathered):
        return (
            gathered[:, :members].reshape(-1, width),
            gathered[:, members : 2 * members].reshape(-1, width),
        )

    for sweep in range(1, SWEEPS):
        t_all, a_all = split(terms)
        inflow = jnp.dot(into_head, t_all, precision=precise)
        outflow = jnp.dot(into_tail, a_all, precision=precise)
        t = push_base + applied(down_all, inflow)
        a = up_base + applied_transposed(up_all, outflow)
        pad = jnp.zeros((-2 * members % 8, width), jnp.float32)
        terms = all_basins(jnp.concatenate([t, a, pad]))
    t_all, a_all = split(terms)

    owned_ids = (z * xs + x) * owned + jnp.arange(owned, dtype=jnp.int32)
    sections = applied(
        junction_inv,
        junction_residual + jnp.dot(meeting(owned_ids, lower_all), t_all, precision=precise),
    )
    adjoint = junction_cotangent + jnp.dot(
        meeting(owned_ids, upper_all), a_all, precision=precise
    )

    head = applied(head_inv, head_residual + jnp.dot(mine(into_head), t_all, precision=precise))
    relief = applied_transposed(
        tail_inv, tail_cotangent + jnp.dot(mine(into_tail), a_all, precision=precise)
    )
    enter = applied(before, head) + before_vector
    leave = applied_transposed(after, relief) + after_vector
    shared = lax.all_gather(jnp.stack([enter, leave]), "c")
    enter = jnp.concatenate([shared[0, 0], shared[1, 0]])
    leave = jnp.concatenate([shared[0, 1], shared[1, 1]])
    enter = jnp.where(c == 1, applied(pair[0, :, :width], enter) + pair[0, :, width], enter)
    leave = jnp.where(
        c == 0, applied_transposed(pair[1, :, :width], leave) + pair[1, :, width + 1], leave
    )

    cell_rows = []
    for number in range(blocks):
        enter = applied(multiplier[:, number], enter) + forced[:, number]
        cell_rows.append(enter)
    cell_update = jnp.stack(cell_rows, axis=1)
    carried = cell_cotangent[:, blocks - 1] + leave
    collected = [carried]
    for number in range(blocks - 2, -1, -1):
        carried = cell_cotangent[:, number] + applied_transposed(multiplier[:, number + 1], carried)
        collected.append(carried)
    cell_adjoint = jnp.stack(collected[::-1], axis=1)
    return (cell_update, sections, cell_adjoint, adjoint)


def solution(mesh):
    basins = mesh.shape["basin"]
    grid = Mesh(mesh.devices.reshape(basins // 4, 4, 4, 2), ("z", "x", "y", "c"))
    b, r = ("z", "x"), ("y", "c")
    return jax.shard_map(
        shards,
        mesh=grid,
        in_specs=(
            P(b, r, None),
            P(b, r, None, None),
            P(b, r, None, None),
            P(b, None, None),
            P(b, None, None),
            P(b, None),
            P(b),
            P(b),
            P(b, r, None),
            P(b, None),
        ),
        out_specs=(P(b, r, None), P(b, None), P(b, r, None), P(b, None)),
        check_vma=False,
    )
```

```python
import jax
import jax.numpy as jnp
from jax import lax
from jax.experimental import pallas as pl
from jax.experimental.pallas import tpu as pltpu
from jax.sharding import Mesh, PartitionSpec as P

SWEEPS = 4
WIDTH = 128
PACK = WIDTH + 8
F32 = jnp.float32

smem = pl.BlockSpec(memory_space=pltpu.SMEM)
vmem = pl.BlockSpec(memory_space=pltpu.VMEM)


def run(kernel, outs, *args, scalars=0):
    single = not isinstance(outs, list)
    shapes = [jax.ShapeDtypeStruct(o, F32) if isinstance(o, tuple) else o for o in ([outs] if single else outs)]
    result = pl.pallas_call(
        kernel,
        out_shape=shapes,
        in_specs=[smem] * scalars + [vmem] * (len(args) - scalars),
        out_specs=[vmem] * len(shapes),
        compiler_params=pltpu.CompilerParams(vmem_limit_bytes=40 * 1024 * 1024),
    )(*args)
    return result[0] if single else result


def two_parts(a):
    high = a.astype(jnp.bfloat16)
    return high, (a - high.astype(F32)).astype(jnp.bfloat16)


def dot(a, b, transposed=False):
    dims = (((1,), (1 if transposed else 0,)), ((), ()))
    return lax.dot_general(a, b, dims, preferred_element_type=F32)


def product(a, b):
    (ah, al), (bh, bl) = two_parts(a), two_parts(b)
    return dot(ah, bh) + (dot(ah, bl) + dot(al, bh))


def along(vector, matrix, transposed):
    vh, vl = two_parts(vector)
    mh, ml = two_parts(matrix)
    return dot(vh, mh, transposed) + (dot(vl, mh, transposed) + dot(vh, ml, transposed))


def applied(matrix, row):
    return along(row, matrix, True)


def applied_transposed(matrix, row):
    return along(row, matrix, False)


def table_kernel(inv_ref, residual_ref, cotangent_ref, out_ref):
    piece = out_ref.shape[1] - 8
    start = pl.multiple_of(lax.axis_index("y") * piece, 8)
    for k in range(inv_ref.shape[0]):
        out_ref[k, :piece] = inv_ref[k, pl.ds(start, piece)]
        out_ref[k, piece : piece + 1] = residual_ref[k : k + 1]
        out_ref[k, piece + 1 : piece + 2] = cotangent_ref[k : k + 1]
        out_ref[k, piece + 2 :] = jnp.zeros((6, WIDTH), F32)


def local_kernel(inv_ref, link_ref, residual_ref, cotangent_ref, mult_ref, forced_ref, out_ref):
    members, blocks = inv_ref.shape[:2]
    for s in range(members):
        m = []
        for i in range(blocks):
            m.append(product(inv_ref[s, i], link_ref[s, i]))
            mult_ref[s, i] = m[i]
        f = [applied(inv_ref[s, i], residual_ref[s, i : i + 1]) for i in range(blocks)]
        total, vector = m[0], f[0]
        forced_ref[s, 0:1] = f[0]
        for i in range(1, blocks):
            forced_ref[s, i : i + 1] = f[i]
            total = product(m[i], total)
            vector = applied(m[i], vector) + f[i]
        back = cotangent_ref[s, blocks - 1 : blocks]
        for i in range(blocks - 2, -1, -1):
            back = cotangent_ref[s, i : i + 1] + applied_transposed(m[i + 1], back)
        out_ref[s, :WIDTH] = total
        out_ref[s, WIDTH : WIDTH + 1] = vector
        out_ref[s, WIDTH + 1 : WIDTH + 2] = applied_transposed(m[0], back)
        out_ref[s, WIDTH + 2 :] = jnp.zeros((6, WIDTH), F32)


def pair_kernel(pair_ref, out_ref):
    half = out_ref.shape[0]
    first_s = lax.axis_index("c") * half
    for k in range(half):
        first, second = pair_ref[0, first_s + k], pair_ref[1, first_s + k]
        one, two = first[:WIDTH], second[:WIDTH]
        out_ref[k, :WIDTH] = product(two, one)
        out_ref[k, WIDTH : WIDTH + 1] = (
            applied(two, first[WIDTH : WIDTH + 1]) + second[WIDTH : WIDTH + 1]
        )
        out_ref[k, WIDTH + 1 : WIDTH + 2] = (
            applied_transposed(one, second[WIDTH + 1 : WIDTH + 2]) + first[WIDTH + 1 : WIDTH + 2]
        )
        out_ref[k, WIDTH + 2 :] = jnp.zeros((6, WIDTH), F32)


def chain_kernel(lower_ref, upper_ref, chips_ref, outlet_ref, schur_ref, before_ref, after_ref, rows_ref, spread_ref):
    chips, half = chips_ref.shape[:2]
    first_s = lax.axis_index("c") * half
    y = lax.axis_index("y")
    row = lax.broadcasted_iota(jnp.int32, (8, WIDTH), 0)
    lane = lax.broadcasted_iota(jnp.int32, (8, WIDTH), 1)
    eye = (
        lax.broadcasted_iota(jnp.int32, (WIDTH, WIDTH), 0)
        == lax.broadcasted_iota(jnp.int32, (WIDTH, WIDTH), 1)
    ).astype(F32)
    nothing = jnp.zeros((1, WIDTH), F32)
    ids = jnp.zeros((8, WIDTH), jnp.int32)
    payload = [nothing] * 8
    for k in range(half):
        ids = jnp.where(lane == k, lower_ref[first_s + k], ids)
        ids = jnp.where(lane == half + k, upper_ref[first_s + k], ids)
        maps = [chips_ref[i, k, :WIDTH] for i in range(chips)]
        before, before_row = eye, nothing
        reached, reached_row = maps[0], chips_ref[0, k, WIDTH : WIDTH + 1]
        for i in range(1, chips):
            before = jnp.where(y == i, reached, before)
            before_row = jnp.where(y == i, reached_row, before_row)
            if i < chips - 1:
                reached = product(maps[i], reached)
            reached_row = applied(maps[i], reached_row) + chips_ref[i, k, WIDTH : WIDTH + 1]
        outlet = outlet_ref[first_s + k]
        schur, after = outlet, outlet
        upward, after_row = nothing, nothing
        for i in range(chips - 1, -1, -1):
            after = jnp.where(y == i, schur, after)
            after_row = jnp.where(y == i, upward, after_row)
            schur = product(schur, maps[i])
            upward = applied_transposed(maps[i], upward) + chips_ref[i, k, WIDTH + 1 : WIDTH + 2]
        schur_ref[k] = schur
        before_ref[k] = before
        after_ref[k] = after
        rows_ref[k : k + 1] = before_row
        rows_ref[half + k : half + k + 1] = after_row
        payload[k] = applied(outlet, reached_row)
        payload[half + k] = upward
    rows_ref[2 * half :] = jnp.zeros((2, WIDTH), F32)
    full = jnp.where(row == 2 * half, ids.astype(F32), jnp.concatenate(payload))
    for i in range(spread_ref.shape[0]):
        spread_ref[i] = full


def pick_kernel(ids_ref, table_ref, out_ref):
    dests, tiles = out_ref.shape[:2]
    half = tiles // 2
    owned = 2 * half
    x = lax.axis_index("x")
    for d in range(dests):
        for k in range(tiles):
            junction = ids_ref[d, (k + half) % tiles]
            basin = lax.div(junction, owned)
            line = lax.div(basin, dests)
            at = line * owned + (junction - basin * owned)
            here = basin - line * dests == x
            out_ref[d, k] = jnp.where(here, table_ref[at], 0.0)


def merge_kernel(picked_ref, out_ref):
    total = picked_ref[0]
    for d in range(1, picked_ref.shape[0]):
        total = total + picked_ref[d]
    for i in range(out_ref.shape[0]):
        out_ref[i] = total


def rule(above, below, half):
    row = lax.broadcasted_iota(jnp.int32, (8, WIDTH), 0)
    return jnp.where(row < half, above, jnp.where(row < 2 * half, below, -2))


def gathered(ids, values, pattern, half):
    total = jnp.sum(jnp.where(ids == pattern[None], values, 0.0), axis=0)
    inflow, outflow = total[0:1], total[half : half + 1]
    for k in range(1, half):
        inflow = inflow + total[k : k + 1]
        outflow = outflow + total[half + k : half + k + 1]
    return inflow, outflow


def step(lower_ref, upper_ref, ids, values, tiles, schur_ref, ends, base, spread_ref):
    half = schur_ref.shape[0]
    first_s = lax.axis_index("c") * half
    payload = [jnp.zeros((1, WIDTH), F32)] * 8
    for k in range(half):
        pattern = rule(upper_ref[first_s + k], lower_ref[first_s + k], half)
        inflow, outflow = gathered(ids, values, pattern, half)
        head = applied(tiles[k], ends[k : k + 1] + inflow)
        relief = applied_transposed(tiles[half + k], ends[half + k : half + k + 1] + outflow)
        schur = schur_ref[k]
        payload[k] = base[k : k + 1] + applied(schur, head)
        payload[half + k] = base[half + k : half + k + 1] + applied_transposed(schur, relief)
    full = jnp.concatenate(payload)
    for i in range(spread_ref.shape[0]):
        spread_ref[i] = full


def first_step_kernel(
    lower_ref, upper_ref, terms_ref, ends_ref, schur_ref, base_ref, tiles_ref, ids_ref, rows_ref, spread_ref
):
    half = schur_ref.shape[0]
    piece = ends_ref.shape[2] - 8
    row = lax.broadcasted_iota(jnp.int32, (8, WIDTH), 0)
    lane = lax.broadcasted_iota(jnp.int32, (8, WIDTH), 1)
    values = terms_ref[...].reshape(-1, 8, WIDTH)
    chosen = jnp.where((row == lane) & (row < 2 * half), values[:, 2 * half : 2 * half + 1], 0.0)
    ids = jnp.sum(chosen, axis=2, keepdims=True).astype(jnp.int32)
    ids = jnp.broadcast_to(ids, values.shape)
    ids_ref[...] = ids
    for k in range(2 * half):
        for i in range(ends_ref.shape[0]):
            tiles_ref[k, i * piece : (i + 1) * piece] = ends_ref[i, k, :piece]
    ends = [ends_ref[0, k, piece : piece + 1] for k in range(half)]
    ends += [ends_ref[0, half + k, piece + 1 : piece + 2] for k in range(half)]
    ends = jnp.concatenate(ends + [jnp.zeros((2, WIDTH), F32)])
    rows_ref[...] = ends
    tiles = [tiles_ref[k] for k in range(2 * half)]
    step(lower_ref, upper_ref, ids, values, tiles, schur_ref, ends, base_ref[0], spread_ref)


def step_kernel(
    lower_ref, upper_ref, terms_ref, ids_ref, tiles_ref, schur_ref, rows_ref, base_ref, spread_ref
):
    values = terms_ref[...].reshape(-1, 8, WIDTH)
    tiles = [tiles_ref[k] for k in range(tiles_ref.shape[0])]
    step(lower_ref, upper_ref, ids_ref[...], values, tiles, schur_ref, rows_ref[...], base_ref[0], spread_ref)


def last_kernel(
    lower_ref, upper_ref, terms_ref, ids_ref, tiles_ref, rows_ref, before_ref, after_ref, passing_ref,
    inv_ref, residual_ref, cotangent_ref, sections_ref, adjoint_ref, shared_ref,
):
    half = before_ref.shape[0]
    owned = inv_ref.shape[0]
    first_s = lax.axis_index("c") * half
    first_j = (lax.axis_index("z") * lax.axis_size("x") + lax.axis_index("x")) * owned
    values = terms_ref[...].reshape(-1, 8, WIDTH)
    ids = ids_ref[...]
    shared_ref[2 * half :] = jnp.zeros((2, WIDTH), F32)
    for k in range(half):
        pattern = rule(upper_ref[first_s + k], lower_ref[first_s + k], half)
        inflow, outflow = gathered(ids, values, pattern, half)
        head = applied(tiles_ref[k], rows_ref[k : k + 1] + inflow)
        relief = applied_transposed(
            tiles_ref[half + k], rows_ref[half + k : half + k + 1] + outflow
        )
        shared_ref[k : k + 1] = applied(before_ref[k], head) + passing_ref[k : k + 1]
        shared_ref[half + k : half + k + 1] = (
            applied_transposed(after_ref[k], relief) + passing_ref[half + k : half + k + 1]
        )
    for k in range(owned):
        inflow, outflow = gathered(ids, values, rule(first_j + k, first_j + k, half), half)
        sections_ref[k : k + 1] = applied(inv_ref[k], residual_ref[k : k + 1] + inflow)
        adjoint_ref[k : k + 1] = cotangent_ref[k : k + 1] + outflow


def cells_kernel(shared_ref, pair_ref, mult_ref, forced_ref, cotangent_ref, update_ref, adjoint_ref):
    members, blocks = mult_ref.shape[:2]
    half = members // 2
    c = lax.axis_index("c")
    for s in range(members):
        core, k = s // half, s % half
        enter = shared_ref[core, k : k + 1]
        leave = shared_ref[core, half + k : half + k + 1]
        other = pair_ref[1 - c, s]
        matrix = other[:WIDTH]
        further = applied(matrix, enter) + other[WIDTH : WIDTH + 1]
        nearer = applied_transposed(matrix, leave) + other[WIDTH + 1 : WIDTH + 2]
        enter = jnp.where(c == 1, further, enter)
        leave = jnp.where(c == 0, nearer, leave)
        for i in range(blocks):
            enter = applied(mult_ref[s, i], enter) + forced_ref[s, i : i + 1]
            update_ref[s, i : i + 1] = enter
        carried = cotangent_ref[s, blocks - 1 : blocks] + leave
        adjoint_ref[s, blocks - 1 : blocks] = carried
        for i in range(blocks - 2, -1, -1):
            carried = cotangent_ref[s, i : i + 1] + applied_transposed(mult_ref[s, i + 1], carried)
            adjoint_ref[s, i : i + 1] = carried


def swap(spread, axis):
    return lax.all_to_all(spread, axis, 0, 0, tiled=False)


def exchanged(spread):
    along_z = swap(spread, "z")
    sides = ("x", "c")
    return swap(jnp.broadcast_to(along_z[None], (lax.axis_size(sides),) + along_z.shape), sides)


def shards(
    reach_residual,
    chain_inv,
    chain_link,
    outlet_link,
    junction_inv,
    junction_residual,
    upper_junction,
    lower_junction,
    cell_cotangent,
    junction_cotangent,
):
    members, blocks, width = reach_residual.shape
    owned = junction_inv.shape[0]
    zs, xs, ys = lax.axis_size("z"), lax.axis_size("x"), lax.axis_size("y")
    half = members // 2
    piece = width // ys
    square = (width, width)
    lower, upper = lower_junction, upper_junction

    part = run(table_kernel, (owned, piece + 8, width), junction_inv, junction_residual, junction_cotangent)
    table = lax.all_gather(part, "z").reshape(zs * owned, piece + 8, width)

    multiplier, forced, local = run(
        local_kernel,
        [(members, blocks) + square, (members, blocks, width), (members, PACK, width)],
        chain_inv, chain_link, reach_residual, cell_cotangent,
    )
    pair = lax.all_gather(local, "c")
    chips = lax.all_gather(run(pair_kernel, (half, PACK, width), pair), "y")
    schur, before, after, passing, spread = run(
        chain_kernel,
        [(half,) + square, (half,) + square, (half,) + square, (8, width), (zs, 8, width)],
        lower, upper, chips, outlet_link, scalars=2,
    )
    terms = exchanged(spread)

    plane = lax.dynamic_slice(
        terms.reshape(xs, 2, zs, 8, width),
        (0, lax.axis_index("c"), lax.axis_index("z"), 2 * half, 0),
        (xs, 1, 1, 1, 2 * half),
    ).reshape(xs, 2 * half).astype(jnp.int32)
    picked = run(pick_kernel, (xs, 2 * half, piece + 8, width), plane, table, scalars=1)
    merged = run(merge_kernel, (ys, 2 * half, piece + 8, width), swap(picked, "x"))
    ends = swap(merged, "y")
    first = spread
    tiles, ids, rows, spread = run(
        first_step_kernel,
        [(2 * half,) + square, jax.ShapeDtypeStruct((zs * xs * 2, 8, width), jnp.int32), (8, width), (zs, 8, width)],
        lower, upper, terms, ends, schur, first, scalars=2,
    )
    terms = exchanged(spread)
    for sweep in range(2, SWEEPS):
        spread = run(
            step_kernel, (zs, 8, width), lower, upper, terms, ids, tiles, schur, rows, first, scalars=2
        )
        terms = exchanged(spread)
    sections, adjoint, shared = run(
        last_kernel,
        [(owned, width), (owned, width), (8, width)],
        lower, upper, terms, ids, tiles, rows, before, after, passing,
        junction_inv, junction_residual, junction_cotangent, scalars=2,
    )
    cell_update, cell_adjoint = run(
        cells_kernel,
        [(members, blocks, width), (members, blocks, width)],
        lax.all_gather(shared, "c"), pair, multiplier, forced, cell_cotangent,
    )
    return (cell_update, sections, cell_adjoint, adjoint)


def solution(mesh):
    basins = mesh.shape["basin"]
    grid = Mesh(mesh.devices.reshape(basins // 4, 4, 4, 2), ("z", "x", "y", "c"))
    b, r = ("z", "x"), ("y", "c")
    return jax.shard_map(
        shards,
        mesh=grid,
        in_specs=(
            P(b, r, None),
            P(b, r, None, None),
            P(b, r, None, None),
            P(b, None, None),
            P(b, None, None),
            P(b, None),
            P(b),
            P(b),
            P(b, r, None),
            P(b, None),
        ),
        out_specs=(P(b, r, None), P(b, None), P(b, r, None), P(b, None)),
        check_vma=False,
    )
```

```python
import jax
import jax.numpy as jnp
from jax import lax
from jax.experimental import pallas as pl
from jax.experimental.pallas import tpu as pltpu
from jax.sharding import Mesh, PartitionSpec as P

SWEEPS = 4
WIDTH = 128
PACK = WIDTH + 8
F32 = jnp.float32

smem = pl.BlockSpec(memory_space=pltpu.SMEM)
vmem = pl.BlockSpec(memory_space=pltpu.VMEM)
hbm = pl.BlockSpec(memory_space=pltpu.HBM)


def array(*shape, dtype=F32):
    return jax.ShapeDtypeStruct(shape, dtype)


def run(kernel, outs, *args, scalars=0, where=vmem, scratch=(), limit=40, flops=0):
    single = not isinstance(outs, list)
    shapes = [outs] if single else outs
    result = pl.pallas_call(
        kernel,
        out_shape=shapes,
        in_specs=[smem] * scalars + [where] * (len(args) - scalars),
        out_specs=[vmem] * len(shapes),
        scratch_shapes=scratch,
        compiler_params=pltpu.CompilerParams(vmem_limit_bytes=limit * 1024 * 1024),
        cost_estimate=pl.CostEstimate(flops=flops, bytes_accessed=flops // 100, transcendentals=0) if flops else None,
    )(*args)
    return result[0] if single else result


def two_parts(a):
    high = a.astype(jnp.bfloat16)
    return high, (a - high.astype(F32)).astype(jnp.bfloat16)


def dot(a, b, transposed=False):
    dims = (((1,), (1 if transposed else 0,)), ((), ()))
    return lax.dot_general(a, b, dims, preferred_element_type=F32)


def parts_of(a):
    return a if isinstance(a, tuple) else two_parts(a)


def product(a, b):
    (ah, al), (bh, bl) = parts_of(a), parts_of(b)
    return dot(ah, bh) + (dot(ah, bl) + dot(al, bh))


def along(vector, matrix, transposed):
    vh, vl = two_parts(vector)
    mh, ml = parts_of(matrix)
    return dot(vh, mh, transposed) + (dot(vl, mh, transposed) + dot(vh, ml, transposed))


def applied(matrix, row):
    return along(row, matrix, True)


def applied_transposed(matrix, row):
    return along(row, matrix, False)


def fetch(pairs, sems):
    copies = [pltpu.make_async_copy(src, dst, sems.at[i]) for i, (src, dst) in enumerate(pairs)]
    for copy in copies:
        copy.start()
    return copies


def table_kernel(inv_ref, residual_ref, cotangent_ref, out_ref, inv, residual, cotangent, sems):
    piece = inv.shape[1]
    start = (lax.axis_index("y") * lax.axis_size("c") + lax.axis_index("c")) * piece
    start = pl.multiple_of(start, 8)
    copies = fetch(
        [
            (inv_ref.at[:, pl.ds(start, piece)], inv),
            (residual_ref, residual),
            (cotangent_ref, cotangent),
        ],
        sems,
    )
    for copy in copies:
        copy.wait()
    out_ref[:, :piece] = inv[...]
    for k in range(out_ref.shape[0]):
        out_ref[k, piece:] = jnp.concatenate(
            [residual[k : k + 1], cotangent[k : k + 1], jnp.zeros((6, WIDTH), F32)]
        )


def local_kernel(
    inv_hbm, link_hbm, residual_hbm, cotangent_hbm, high_ref, low_ref, forced_ref, out_ref,
    inv_ref, link_ref, residual_ref, cotangent_ref, sems,
):
    members, blocks = inv_ref.shape[:2]
    pairs = [(residual_hbm, residual_ref), (cotangent_hbm, cotangent_ref)]
    for s in range(members):
        pairs += [(inv_hbm.at[s], inv_ref.at[s]), (link_hbm.at[s], link_ref.at[s])]
    copies = fetch(pairs, sems)
    copies[0].wait()
    copies[1].wait()
    for s in range(members):
        copies[2 + 2 * s].wait()
        copies[3 + 2 * s].wait()
        m, f = [], []
        for i in range(blocks):
            inverse = two_parts(inv_ref[s, i])
            m.append(two_parts(product(inverse, two_parts(link_ref[s, i]))))
            high_ref[s, i], low_ref[s, i] = m[i]
            f.append(applied(inverse, residual_ref[s, i : i + 1]))
            forced_ref[s, i : i + 1] = f[i]
        total, vector = m[0], f[0]
        for i in range(1, blocks):
            total = product(m[i], total if i == 1 else two_parts(total))
            vector = applied(m[i], vector) + f[i]
        back = cotangent_ref[s, blocks - 1 : blocks]
        for i in range(blocks - 2, -1, -1):
            back = cotangent_ref[s, i : i + 1] + applied_transposed(m[i + 1], back)
        out_ref[s, :WIDTH] = total
        out_ref[s, WIDTH:] = jnp.concatenate(
            [vector, applied_transposed(m[0], back), jnp.zeros((6, WIDTH), F32)]
        )


def pair_kernel(pair_ref, out_ref):
    half = out_ref.shape[0]
    first_s = lax.axis_index("c") * half
    for k in range(half):
        first, second = pair_ref[0, first_s + k], pair_ref[1, first_s + k]
        one, two = two_parts(first[:WIDTH]), two_parts(second[:WIDTH])
        out_ref[k, :WIDTH] = product(two, one)
        out_ref[k, WIDTH : WIDTH + 1] = (
            applied(two, first[WIDTH : WIDTH + 1]) + second[WIDTH : WIDTH + 1]
        )
        out_ref[k, WIDTH + 1 : WIDTH + 2] = (
            applied_transposed(one, second[WIDTH + 1 : WIDTH + 2]) + first[WIDTH + 1 : WIDTH + 2]
        )
        out_ref[k, WIDTH + 2 :] = jnp.zeros((6, WIDTH), F32)


def keep(ref, k, matrix):
    ref[0, k], ref[1, k] = two_parts(matrix)


def kept(ref, k):
    return ref[0, k], ref[1, k]


def chain_kernel(lower_ref, upper_ref, chips_ref, outlet_ref, schur_ref, before_ref, after_ref, rows_ref, spread_ref):
    chips, half = chips_ref.shape[:2]
    first_s = lax.axis_index("c") * half
    y = lax.axis_index("y")
    row = lax.broadcasted_iota(jnp.int32, (8, WIDTH), 0)
    lane = lax.broadcasted_iota(jnp.int32, (8, WIDTH), 1)
    eye = (
        lax.broadcasted_iota(jnp.int32, (WIDTH, WIDTH), 0)
        == lax.broadcasted_iota(jnp.int32, (WIDTH, WIDTH), 1)
    ).astype(F32)
    nothing = jnp.zeros((1, WIDTH), F32)
    ids = jnp.zeros((8, WIDTH), jnp.int32)
    payload = [nothing] * 8
    for k in range(half):
        ids = jnp.where(lane == k, lower_ref[first_s + k], ids)
        ids = jnp.where(lane == half + k, upper_ref[first_s + k], ids)
        maps = [two_parts(chips_ref[i, k, :WIDTH]) for i in range(chips)]
        before, before_row = eye, nothing
        reached, reached_row = chips_ref[0, k, :WIDTH], chips_ref[0, k, WIDTH : WIDTH + 1]
        for i in range(1, chips):
            before = jnp.where(y == i, reached, before)
            before_row = jnp.where(y == i, reached_row, before_row)
            if i < chips - 1:
                reached = product(maps[i], reached)
            reached_row = applied(maps[i], reached_row) + chips_ref[i, k, WIDTH : WIDTH + 1]
        schur = outlet_ref[first_s + k]
        payload[k] = applied(schur, reached_row)
        after = schur
        upward, after_row = nothing, nothing
        for i in range(chips - 1, -1, -1):
            after = jnp.where(y == i, schur, after)
            after_row = jnp.where(y == i, upward, after_row)
            schur = product(schur, maps[i])
            upward = applied_transposed(maps[i], upward) + chips_ref[i, k, WIDTH + 1 : WIDTH + 2]
        payload[half + k] = upward
        keep(schur_ref, k, schur)
        keep(before_ref, k, before)
        keep(after_ref, k, after)
        rows_ref[k : k + 1] = before_row
        rows_ref[half + k : half + k + 1] = after_row
    rows_ref[2 * half :] = jnp.zeros((2, WIDTH), F32)
    full = jnp.where(row == 2 * half, ids.astype(F32), jnp.concatenate(payload))
    for i in range(spread_ref.shape[0]):
        spread_ref[i] = full


def build_kernel(ids_ref, table_ref, terms_ref, out_ref):
    dests = out_ref.shape[0]
    owned, rows = ids_ref.shape[0] // (2 * dests), table_ref.shape[1]
    half = owned // 2
    count = terms_ref.shape[0] * terms_ref.shape[1]
    x = lax.axis_index("x")
    terms = terms_ref[...].reshape(count, WIDTH)
    for step in range(dests):
        d = lax.rem(x + step, dests)
        out_ref[d, :count] = terms
        for tile in range(2 * owned):
            core, t = tile // owned, tile % owned
            side, k = (1, t) if t < half else (0, t - half)
            junction = ids_ref[(2 * step + side) * owned + core * half + k]
            basin = lax.div(junction, owned)
            line = lax.div(basin, dests)
            at = line * owned + (junction - basin * owned)
            here = basin - line * dests == x
            start = count + tile * rows
            out_ref[d, start : start + rows] = jnp.where(here, table_ref[at], 0.0)


def merge_kernel(picked_ref, out_ref):
    sides, rows = picked_ref.shape[:2]
    count = (out_ref.shape[0] - rows) // (sides - 1)
    for d in range(sides):
        out_ref[d * count : (d + 1) * count] = picked_ref[d, :count]
    total = picked_ref[0, count:]
    for d in range(1, sides):
        total = total + picked_ref[d, count:]
    out_ref[sides * count :] = total


def ends_kernel(both_ref, out_ref):
    tiles, rows = out_ref.shape[1:3]
    piece = (rows - 8) // 2
    first = both_ref.shape[1] - 2 * tiles * (piece + 8)
    c = lax.axis_index("c")
    for t in range(tiles):
        start = pl.multiple_of(first + (c * tiles + t) * (piece + 8), 8)
        full = jnp.concatenate(
            [both_ref[0, pl.ds(start, piece)], both_ref[1, pl.ds(start, piece)], both_ref[0, pl.ds(start + piece, 8)]]
        )
        for i in range(out_ref.shape[0]):
            out_ref[i, t] = full


def rule(above, below, half):
    row = lax.broadcasted_iota(jnp.int32, (8, WIDTH), 0)
    return jnp.where(row < half, above, jnp.where(row < 2 * half, below, -2))


def gathered(ids, values, pattern, half):
    total = jnp.sum(jnp.where(ids == pattern[None], values, 0.0), axis=0)
    inflow, outflow = total[0:1], total[half : half + 1]
    for k in range(1, half):
        inflow = inflow + total[k : k + 1]
        outflow = outflow + total[half + k : half + k + 1]
    return inflow, outflow


def step(lower_ref, upper_ref, ids, values, tiles, schur_ref, ends, base, spread_ref):
    half = schur_ref.shape[1]
    first_s = lax.axis_index("c") * half
    payload = [jnp.zeros((1, WIDTH), F32)] * 8
    for k in range(half):
        pattern = rule(upper_ref[first_s + k], lower_ref[first_s + k], half)
        inflow, outflow = gathered(ids, values, pattern, half)
        head = applied(kept(tiles, k), ends[k : k + 1] + inflow)
        relief = applied_transposed(
            kept(tiles, half + k), ends[half + k : half + k + 1] + outflow
        )
        schur = kept(schur_ref, k)
        payload[k] = base[k : k + 1] + applied(schur, head)
        payload[half + k] = base[half + k : half + k + 1] + applied_transposed(schur, relief)
    full = jnp.concatenate(payload)
    for i in range(spread_ref.shape[0]):
        spread_ref[i] = full


def first_step_kernel(
    lower_ref, upper_ref, terms_ref, ends_ref, schur_ref, base_ref, tiles_ref, ids_ref, rows_ref, spread_ref
):
    half = schur_ref.shape[1]
    piece = ends_ref.shape[2] - 8
    row = lax.broadcasted_iota(jnp.int32, (8, WIDTH), 0)
    lane = lax.broadcasted_iota(jnp.int32, (8, WIDTH), 1)
    values = terms_ref[:, : ids_ref.shape[0] * 4].reshape(-1, 8, WIDTH)
    chosen = jnp.where((row == lane) & (row < 2 * half), values[:, 2 * half : 2 * half + 1], 0.0)
    ids = jnp.sum(chosen, axis=2, keepdims=True).astype(jnp.int32)
    ids = jnp.broadcast_to(ids, values.shape)
    ids_ref[...] = ids
    for k in range(2 * half):
        keep(tiles_ref, k, jnp.concatenate([ends_ref[i, k, :piece] for i in range(ends_ref.shape[0])]))
    ends = [ends_ref[0, k, piece : piece + 1] for k in range(half)]
    ends += [ends_ref[0, half + k, piece + 1 : piece + 2] for k in range(half)]
    ends = jnp.concatenate(ends + [jnp.zeros((2, WIDTH), F32)])
    rows_ref[...] = ends
    step(lower_ref, upper_ref, ids, values, tiles_ref, schur_ref, ends, base_ref[0], spread_ref)


def step_kernel(
    lower_ref, upper_ref, terms_ref, ids_ref, tiles_ref, schur_ref, rows_ref, base_ref, spread_ref
):
    values = terms_ref[...].reshape(-1, 8, WIDTH)
    step(lower_ref, upper_ref, ids_ref[...], values, tiles_ref, schur_ref, rows_ref[...], base_ref[0], spread_ref)


def last_kernel(
    lower_ref, upper_ref, terms_ref, ids_ref, tiles_ref, rows_ref, before_ref, after_ref, passing_ref,
    inv_ref, residual_ref, cotangent_ref, sections_ref, adjoint_ref, shared_ref,
):
    half = before_ref.shape[1]
    owned = inv_ref.shape[0]
    first_s = lax.axis_index("c") * half
    first_j = (lax.axis_index("z") * lax.axis_size("x") + lax.axis_index("x")) * owned
    values = terms_ref[...].reshape(-1, 8, WIDTH)
    ids = ids_ref[...]
    shared_ref[2 * half :] = jnp.zeros((2, WIDTH), F32)
    for k in range(half):
        pattern = rule(upper_ref[first_s + k], lower_ref[first_s + k], half)
        inflow, outflow = gathered(ids, values, pattern, half)
        head = applied(kept(tiles_ref, k), rows_ref[k : k + 1] + inflow)
        relief = applied_transposed(
            kept(tiles_ref, half + k), rows_ref[half + k : half + k + 1] + outflow
        )
        shared_ref[k : k + 1] = applied(kept(before_ref, k), head) + passing_ref[k : k + 1]
        shared_ref[half + k : half + k + 1] = (
            applied_transposed(kept(after_ref, k), relief) + passing_ref[half + k : half + k + 1]
        )
    for k in range(owned):
        inflow, outflow = gathered(ids, values, rule(first_j + k, first_j + k, half), half)
        sections_ref[k : k + 1] = applied(inv_ref[k], residual_ref[k : k + 1] + inflow)
        adjoint_ref[k : k + 1] = cotangent_ref[k : k + 1] + outflow


def cells_kernel(shared_ref, pair_ref, high_ref, low_ref, forced_ref, cotangent_ref, update_ref, adjoint_ref):
    members, blocks = high_ref.shape[:2]
    half = members // 2
    c = lax.axis_index("c")
    for s in range(members):
        core, k = s // half, s % half
        enter = shared_ref[core, k : k + 1]
        leave = shared_ref[core, half + k : half + k + 1]
        other = pair_ref[1 - c, s]
        matrix = two_parts(other[:WIDTH])
        further = applied(matrix, enter) + other[WIDTH : WIDTH + 1]
        nearer = applied_transposed(matrix, leave) + other[WIDTH + 1 : WIDTH + 2]
        enter = jnp.where(c == 1, further, enter)
        leave = jnp.where(c == 0, nearer, leave)
        for i in range(blocks):
            enter = applied((high_ref[s, i], low_ref[s, i]), enter) + forced_ref[s, i : i + 1]
            update_ref[s, i : i + 1] = enter
        carried = cotangent_ref[s, blocks - 1 : blocks] + leave
        adjoint_ref[s, blocks - 1 : blocks] = carried
        for i in range(blocks - 2, -1, -1):
            carried = cotangent_ref[s, i : i + 1] + applied_transposed(
                (high_ref[s, i + 1], low_ref[s, i + 1]), carried
            )
            adjoint_ref[s, i : i + 1] = carried


def swap(spread, axis):
    return lax.all_to_all(spread, axis, 0, 0, tiled=False)


def over_x(values):
    return swap(jnp.broadcast_to(values[None], (lax.axis_size("x"),) + values.shape), "x")


def exchanged(spread):
    along_x = over_x(swap(spread, "z"))
    return lax.all_gather(along_x.reshape(-1, WIDTH), "c")


def shifted(values, places):
    n = lax.axis_size("x")
    return lax.ppermute(values, "x", [((i + places) % n, i) for i in range(n)])


def shards(
    reach_residual,
    chain_inv,
    chain_link,
    outlet_link,
    junction_inv,
    junction_residual,
    upper_junction,
    lower_junction,
    cell_cotangent,
    junction_cotangent,
):
    members, blocks, width = reach_residual.shape
    owned = junction_inv.shape[0]
    zs, xs, ys, cs = (lax.axis_size(a) for a in ("z", "x", "y", "c"))
    half = members // cs
    piece = width // (ys * cs)
    bf16 = jnp.bfloat16
    lower, upper = lower_junction, upper_junction

    own = jnp.stack([lower, upper])[None]
    beside = shifted(own, 1)

    part = run(
        table_kernel,
        array(owned, piece + 8, width),
        junction_inv, junction_residual, junction_cotangent,
        where=hbm, limit=60,
        scratch=[
            pltpu.VMEM((owned, piece, width), F32),
            pltpu.VMEM((owned, width), F32),
            pltpu.VMEM((owned, width), F32),
            pltpu.SemaphoreType.DMA((3,)),
        ],
    )
    table = lax.all_gather(part, "z").reshape(zs * owned, piece + 8, width)

    chain = (members, blocks, width, width)
    high, low, forced, local = run(
        local_kernel,
        [
            array(*chain, dtype=bf16),
            array(*chain, dtype=bf16),
            array(members, blocks, width),
            array(members, PACK, width),
        ],
        chain_inv, chain_link, reach_residual, cell_cotangent,
        where=hbm, limit=60, flops=2_000_000_000,
        scratch=[
            pltpu.VMEM(chain, F32),
            pltpu.VMEM(chain, F32),
            pltpu.VMEM((members, blocks, width), F32),
            pltpu.VMEM((members, blocks, width), F32),
            pltpu.SemaphoreType.DMA((2 + 2 * members,)),
        ],
    )
    local, beside = lax.optimization_barrier((local, beside))
    two = jnp.concatenate([own, beside])
    plane = jnp.concatenate([two, shifted(two, 2)]).reshape(-1)
    pair = lax.all_gather(local, "c")
    chips = lax.all_gather(run(pair_kernel, array(half, PACK, width), pair), "y")
    matrices = array(2, half, width, width, dtype=bf16)
    schur, before, after, passing, first = run(
        chain_kernel,
        [matrices, matrices, matrices, array(8, width), array(zs, 8, width)],
        lower, upper, chips, outlet_link, scalars=2,
    )

    count = zs * 8
    fetched = 2 * owned * (piece + 8)
    built = run(
        build_kernel, array(xs, count + fetched, width), plane, table, swap(first, "z"), scalars=1
    )
    merged = run(merge_kernel, array(xs * count + fetched, width), swap(built, "x"))
    both = lax.all_gather(merged, "c")
    ends = swap(run(ends_kernel, array(ys, owned, 2 * piece + 8, width), both), "y")
    tiles, ids, rows, spread = run(
        first_step_kernel,
        [
            array(2, 2 * half, width, width, dtype=bf16),
            array(cs * xs * zs, 8, width, dtype=jnp.int32),
            array(8, width),
            array(zs, 8, width),
        ],
        lower, upper, both, ends, schur, first, scalars=2,
    )
    terms = exchanged(spread)
    for sweep in range(2, SWEEPS):
        spread = run(
            step_kernel, array(zs, 8, width), lower, upper, terms, ids, tiles, schur, rows, first, scalars=2
        )
        terms = exchanged(spread)
    sections, adjoint, shared = run(
        last_kernel,
        [array(owned, width), array(owned, width), array(8, width)],
        lower, upper, terms, ids, tiles, rows, before, after, passing,
        junction_inv, junction_residual, junction_cotangent, scalars=2,
    )
    cell_update, cell_adjoint = run(
        cells_kernel,
        [array(members, blocks, width), array(members, blocks, width)],
        lax.all_gather(shared, "c"), pair, high, low, forced, cell_cotangent,
    )
    return (cell_update, sections, cell_adjoint, adjoint)


def solution(mesh):
    basins = mesh.shape["basin"]
    grid = Mesh(mesh.devices.reshape(basins // 4, 4, 4, 2), ("z", "x", "y", "c"))
    b, r = ("z", "x"), ("y", "c")
    return jax.shard_map(
        shards,
        mesh=grid,
        in_specs=(
            P(b, r, None),
            P(b, r, None, None),
            P(b, r, None, None),
            P(b, None, None),
            P(b, None, None),
            P(b, None),
            P(b),
            P(b),
            P(b, r, None),
            P(b, None),
        ),
        out_specs=(P(b, r, None), P(b, None), P(b, r, None), P(b, None)),
        check_vma=False,
    )
```

```python
import math

import jax
import jax.numpy as jnp
from jax import lax
from jax.experimental import pallas as pl
from jax.experimental.pallas import tpu as pltpu
from jax.sharding import Mesh, PartitionSpec as P

SWEEPS = 4
WIDTH = 128
PACK = WIDTH + 8
F32 = jnp.float32

smem = pl.BlockSpec(memory_space=pltpu.SMEM)
vmem = pl.BlockSpec(memory_space=pltpu.VMEM)
hbm = pl.BlockSpec(memory_space=pltpu.HBM)


def array(*shape, dtype=F32):
    return jax.ShapeDtypeStruct(shape, dtype)


def run(kernel, outs, *args, scalars=0, where=vmem, scratch=(), limit=40, flops=0):
    single = not isinstance(outs, list)
    shapes = [outs] if single else outs
    result = pl.pallas_call(
        kernel,
        out_shape=shapes,
        in_specs=[smem] * scalars + [where] * (len(args) - scalars),
        out_specs=[vmem] * len(shapes),
        scratch_shapes=scratch,
        compiler_params=pltpu.CompilerParams(vmem_limit_bytes=limit * 1024 * 1024),
        cost_estimate=pl.CostEstimate(flops=flops, bytes_accessed=flops // 100, transcendentals=0) if flops else None,
    )(*args)
    return result[0] if single else result


def two_parts(a):
    high = a.astype(jnp.bfloat16)
    return high, (a - high.astype(F32)).astype(jnp.bfloat16)


def dot(a, b, transposed=False):
    dims = (((1,), (1 if transposed else 0,)), ((), ()))
    return lax.dot_general(a, b, dims, preferred_element_type=F32)


def parts_of(a):
    return a if isinstance(a, tuple) else two_parts(a)


def product(a, b):
    (ah, al), (bh, bl) = parts_of(a), parts_of(b)
    return dot(ah, bh) + (dot(ah, bl) + dot(al, bh))


def along(vector, matrix, transposed):
    vh, vl = two_parts(vector)
    mh, ml = parts_of(matrix)
    return dot(vh, mh, transposed) + (dot(vl, mh, transposed) + dot(vh, ml, transposed))


def applied(matrix, row):
    return along(row, matrix, True)


def applied_transposed(matrix, row):
    return along(row, matrix, False)


def fetch(pairs, sems):
    copies = [pltpu.make_async_copy(src, dst, sems.at[i]) for i, (src, dst) in enumerate(pairs)]
    for copy in copies:
        copy.start()
    return copies


def table_kernel(inv_ref, residual_ref, cotangent_ref, out_ref, residual, cotangent, sems):
    copies = fetch(
        [
            (inv_ref, out_ref.at[:, :WIDTH]),
            (residual_ref, residual),
            (cotangent_ref, cotangent),
        ],
        sems,
    )
    copies[1].wait()
    copies[2].wait()
    for k in range(out_ref.shape[0]):
        out_ref[k, WIDTH:] = jnp.concatenate(
            [residual[k : k + 1], cotangent[k : k + 1], jnp.zeros((6, WIDTH), F32)]
        )
    copies[0].wait()


def slice_kernel(near_ref, out_ref, sems):
    piece = out_ref.shape[1] - 8
    start = pl.multiple_of(lax.axis_index("y") * piece, 8)
    copies = fetch(
        [
            (near_ref.at[:, pl.ds(start, piece)], out_ref.at[:, :piece]),
            (near_ref.at[:, WIDTH:], out_ref.at[:, piece:]),
        ],
        sems,
    )
    for copy in copies:
        copy.wait()


def local_kernel(
    inv_hbm, link_hbm, residual_hbm, cotangent_hbm, high_ref, low_ref, forced_ref, out_ref,
    inv_ref, link_ref, residual_ref, cotangent_ref, sems,
):
    members, blocks = inv_ref.shape[:2]
    pairs = [(residual_hbm, residual_ref), (cotangent_hbm, cotangent_ref)]
    for s in range(members):
        pairs += [(inv_hbm.at[s], inv_ref.at[s]), (link_hbm.at[s], link_ref.at[s])]
    copies = fetch(pairs, sems)
    copies[0].wait()
    copies[1].wait()
    for s in range(members):
        copies[2 + 2 * s].wait()
        copies[3 + 2 * s].wait()
        m, f = [], []
        for i in range(blocks):
            inverse = two_parts(inv_ref[s, i])
            m.append(two_parts(product(inverse, two_parts(link_ref[s, i]))))
            high_ref[s, i], low_ref[s, i] = m[i]
            f.append(applied(inverse, residual_ref[s, i : i + 1]))
            forced_ref[s, i : i + 1] = f[i]
        total, vector = m[0], f[0]
        for i in range(1, blocks):
            total = product(m[i], total if i == 1 else two_parts(total))
            vector = applied(m[i], vector) + f[i]
        back = cotangent_ref[s, blocks - 1 : blocks]
        for i in range(blocks - 2, -1, -1):
            back = cotangent_ref[s, i : i + 1] + applied_transposed(m[i + 1], back)
        out_ref[s, :WIDTH] = total
        out_ref[s, WIDTH:] = jnp.concatenate(
            [vector, applied_transposed(m[0], back), jnp.zeros((6, WIDTH), F32)]
        )


def pair_kernel(pair_ref, out_ref):
    half = out_ref.shape[0]
    first_s = lax.axis_index("c") * half
    for k in range(half):
        first, second = pair_ref[0, first_s + k], pair_ref[1, first_s + k]
        one, two = two_parts(first[:WIDTH]), two_parts(second[:WIDTH])
        out_ref[k, :WIDTH] = product(two, one)
        out_ref[k, WIDTH : WIDTH + 1] = (
            applied(two, first[WIDTH : WIDTH + 1]) + second[WIDTH : WIDTH + 1]
        )
        out_ref[k, WIDTH + 1 : WIDTH + 2] = (
            applied_transposed(one, second[WIDTH + 1 : WIDTH + 2]) + first[WIDTH + 1 : WIDTH + 2]
        )
        out_ref[k, WIDTH + 2 :] = jnp.zeros((6, WIDTH), F32)


def keep(ref, k, matrix):
    ref[0, k], ref[1, k] = two_parts(matrix)


def kept(ref, k):
    return ref[0, k], ref[1, k]


def chain_kernel(lower_ref, upper_ref, chips_ref, outlet_ref, schur_ref, before_ref, after_ref, rows_ref, spread_ref):
    chips, half = chips_ref.shape[:2]
    first_s = lax.axis_index("c") * half
    y = lax.axis_index("y")
    row = lax.broadcasted_iota(jnp.int32, (8, WIDTH), 0)
    lane = lax.broadcasted_iota(jnp.int32, (8, WIDTH), 1)
    eye = (
        lax.broadcasted_iota(jnp.int32, (WIDTH, WIDTH), 0)
        == lax.broadcasted_iota(jnp.int32, (WIDTH, WIDTH), 1)
    ).astype(F32)
    nothing = jnp.zeros((1, WIDTH), F32)
    ids = jnp.zeros((8, WIDTH), jnp.int32)
    payload = [nothing] * 8
    for k in range(half):
        ids = jnp.where(lane == k, lower_ref[first_s + k], ids)
        ids = jnp.where(lane == half + k, upper_ref[first_s + k], ids)
        maps = [two_parts(chips_ref[i, k, :WIDTH]) for i in range(chips)]
        before, before_row = eye, nothing
        reached, reached_row = chips_ref[0, k, :WIDTH], chips_ref[0, k, WIDTH : WIDTH + 1]
        for i in range(1, chips):
            before = jnp.where(y == i, reached, before)
            before_row = jnp.where(y == i, reached_row, before_row)
            if i < chips - 1:
                reached = product(maps[i], reached)
            reached_row = applied(maps[i], reached_row) + chips_ref[i, k, WIDTH : WIDTH + 1]
        schur = outlet_ref[first_s + k]
        payload[k] = applied(schur, reached_row)
        after = schur
        upward, after_row = nothing, nothing
        for i in range(chips - 1, -1, -1):
            after = jnp.where(y == i, schur, after)
            after_row = jnp.where(y == i, upward, after_row)
            schur = product(schur, maps[i])
            upward = applied_transposed(maps[i], upward) + chips_ref[i, k, WIDTH + 1 : WIDTH + 2]
        payload[half + k] = upward
        keep(schur_ref, k, schur)
        keep(before_ref, k, before)
        keep(after_ref, k, after)
        rows_ref[k : k + 1] = before_row
        rows_ref[half + k : half + k + 1] = after_row
    rows_ref[2 * half :] = jnp.zeros((2, WIDTH), F32)
    full = jnp.where(row == 2 * half, ids.astype(F32), jnp.concatenate(payload))
    for i in range(spread_ref.shape[0]):
        spread_ref[i] = full


def pick_kernel(ids_ref, table_ref, out_ref):
    dests, owned = out_ref.shape[:2]
    half = owned // 2
    x = lax.axis_index("x")
    first_s = lax.axis_index("c") * half
    for d in range(dests):
        for t in range(owned):
            side, k = (1, t) if t < half else (0, t - half)
            junction = ids_ref[(2 * d + side) * owned + first_s + k]
            basin = lax.div(junction, owned)
            line = lax.div(basin, dests)
            at = line * owned + (junction - basin * owned)
            here = basin - line * dests == x
            out_ref[d, t] = jnp.where(here, table_ref[at], 0.0)


def merge_kernel(picked_ref, out_ref):
    total = picked_ref[0]
    for d in range(1, picked_ref.shape[0]):
        total = total + picked_ref[d]
    rows = picked_ref.shape[2]
    out_ref[:, :rows] = total
    out_ref[:, rows:] = jnp.zeros((out_ref.shape[0], out_ref.shape[1] - rows, WIDTH), F32)


def rule(above, below, half):
    row = lax.broadcasted_iota(jnp.int32, (8, WIDTH), 0)
    return jnp.where(row < half, above, jnp.where(row < 2 * half, below, -2))


def gathered(ids, values, pattern, half):
    total = jnp.sum(jnp.where(ids == pattern[None], values, 0.0), axis=0)
    inflow, outflow = total[0:1], total[half : half + 1]
    for k in range(1, half):
        inflow = inflow + total[k : k + 1]
        outflow = outflow + total[half + k : half + k + 1]
    return inflow, outflow


def step(lower_ref, upper_ref, ids, values, tiles, schur_ref, ends, base, spread_ref):
    half = schur_ref.shape[1]
    first_s = lax.axis_index("c") * half
    payload = [jnp.zeros((1, WIDTH), F32)] * 8
    for k in range(half):
        pattern = rule(upper_ref[first_s + k], lower_ref[first_s + k], half)
        inflow, outflow = gathered(ids, values, pattern, half)
        head = applied(kept(tiles, k), ends[k : k + 1] + inflow)
        relief = applied_transposed(
            kept(tiles, half + k), ends[half + k : half + k + 1] + outflow
        )
        schur = kept(schur_ref, k)
        payload[k] = base[k : k + 1] + applied(schur, head)
        payload[half + k] = base[half + k : half + k + 1] + applied_transposed(schur, relief)
    full = jnp.concatenate(payload)
    for i in range(spread_ref.shape[0]):
        spread_ref[i] = full


def first_step_kernel(
    lower_ref, upper_ref, terms_ref, ends_ref, schur_ref, base_ref, tiles_ref, ids_ref, rows_ref, spread_ref
):
    half = schur_ref.shape[1]
    piece = WIDTH // ends_ref.shape[0]
    row = lax.broadcasted_iota(jnp.int32, (8, WIDTH), 0)
    lane = lax.broadcasted_iota(jnp.int32, (8, WIDTH), 1)
    values = terms_ref[...].reshape(-1, 8, WIDTH)
    chosen = jnp.where((row == lane) & (row < 2 * half), values[:, 2 * half : 2 * half + 1], 0.0)
    ids = jnp.sum(chosen, axis=2, keepdims=True).astype(jnp.int32)
    ids = jnp.broadcast_to(ids, values.shape)
    ids_ref[...] = ids
    for k in range(2 * half):
        keep(tiles_ref, k, jnp.concatenate([ends_ref[i, k, :piece] for i in range(ends_ref.shape[0])]))
    ends = [ends_ref[0, k, piece : piece + 1] for k in range(half)]
    ends += [ends_ref[0, half + k, piece + 1 : piece + 2] for k in range(half)]
    ends = jnp.concatenate(ends + [jnp.zeros((2, WIDTH), F32)])
    rows_ref[...] = ends
    step(lower_ref, upper_ref, ids, values, tiles_ref, schur_ref, ends, base_ref[0], spread_ref)


def step_kernel(
    lower_ref, upper_ref, terms_ref, ids_ref, tiles_ref, schur_ref, rows_ref, base_ref, spread_ref
):
    values = terms_ref[...].reshape(-1, 8, WIDTH)
    step(lower_ref, upper_ref, ids_ref[...], values, tiles_ref, schur_ref, rows_ref[...], base_ref[0], spread_ref)


def last_kernel(
    lower_ref, upper_ref, terms_ref, ids_ref, tiles_ref, rows_ref, before_ref, after_ref, passing_ref,
    inv_ref, residual_ref, cotangent_ref, sections_ref, adjoint_ref, shared_ref,
):
    half = before_ref.shape[1]
    owned = inv_ref.shape[0]
    first_s = lax.axis_index("c") * half
    first_j = (lax.axis_index(("zh", "zl")) * lax.axis_size("x") + lax.axis_index("x")) * owned
    values = terms_ref[...].reshape(-1, 8, WIDTH)
    ids = ids_ref[...]
    shared_ref[2 * half :] = jnp.zeros((2, WIDTH), F32)
    for k in range(half):
        pattern = rule(upper_ref[first_s + k], lower_ref[first_s + k], half)
        inflow, outflow = gathered(ids, values, pattern, half)
        head = applied(kept(tiles_ref, k), rows_ref[k : k + 1] + inflow)
        relief = applied_transposed(
            kept(tiles_ref, half + k), rows_ref[half + k : half + k + 1] + outflow
        )
        shared_ref[k : k + 1] = applied(kept(before_ref, k), head) + passing_ref[k : k + 1]
        shared_ref[half + k : half + k + 1] = (
            applied_transposed(kept(after_ref, k), relief) + passing_ref[half + k : half + k + 1]
        )
    for k in range(owned):
        inflow, outflow = gathered(ids, values, rule(first_j + k, first_j + k, half), half)
        sections_ref[k : k + 1] = applied(inv_ref[k], residual_ref[k : k + 1] + inflow)
        adjoint_ref[k : k + 1] = cotangent_ref[k : k + 1] + outflow


def cells_kernel(shared_ref, pair_ref, high_ref, low_ref, forced_ref, cotangent_ref, update_ref, adjoint_ref):
    members, blocks = high_ref.shape[:2]
    half = members // 2
    c = lax.axis_index("c")
    for s in range(members):
        core, k = s // half, s % half
        enter = shared_ref[core, k : k + 1]
        leave = shared_ref[core, half + k : half + k + 1]
        other = pair_ref[1 - c, s]
        matrix = two_parts(other[:WIDTH])
        further = applied(matrix, enter) + other[WIDTH : WIDTH + 1]
        nearer = applied_transposed(matrix, leave) + other[WIDTH + 1 : WIDTH + 2]
        enter = jnp.where(c == 1, further, enter)
        leave = jnp.where(c == 0, nearer, leave)
        for i in range(blocks):
            enter = applied((high_ref[s, i], low_ref[s, i]), enter) + forced_ref[s, i : i + 1]
            update_ref[s, i : i + 1] = enter
        carried = cotangent_ref[s, blocks - 1 : blocks] + leave
        adjoint_ref[s, blocks - 1 : blocks] = carried
        for i in range(blocks - 2, -1, -1):
            carried = cotangent_ref[s, i : i + 1] + applied_transposed(
                (high_ref[s, i + 1], low_ref[s, i + 1]), carried
            )
            adjoint_ref[s, i : i + 1] = carried


def swap(spread, axis):
    return lax.all_to_all(spread, axis, 0, 0, tiled=False)


def over_x(values):
    return swap(jnp.broadcast_to(values[None], (lax.axis_size("x"),) + values.shape), "x")


def exchanged(spread):
    along_x = over_x(swap(spread, ("zh", "zl")))
    return lax.all_gather(along_x.reshape(-1, WIDTH), "c")


def shards(
    reach_residual,
    chain_inv,
    chain_link,
    outlet_link,
    junction_inv,
    junction_residual,
    upper_junction,
    lower_junction,
    cell_cotangent,
    junction_cotangent,
):
    members, blocks, width = reach_residual.shape
    owned = junction_inv.shape[0]
    zs, xs, ys, cs = (lax.axis_size(a) for a in (("zh", "zl"), "x", "y", "c"))
    half = members // cs
    piece = width // ys
    bf16 = jnp.bfloat16
    lower, upper = lower_junction, upper_junction

    plane = over_x(jnp.stack([lower, upper])).reshape(-1)

    part = run(
        table_kernel,
        array(owned, PACK, width),
        junction_inv, junction_residual, junction_cotangent,
        where=hbm, limit=60,
        scratch=[
            pltpu.VMEM((owned, width), F32),
            pltpu.VMEM((owned, width), F32),
            pltpu.SemaphoreType.DMA((3,)),
        ],
    )
    near = lax.all_gather(part, "zl").reshape(-1, PACK, width)

    chain = (members, blocks, width, width)
    high, low, forced, local = run(
        local_kernel,
        [
            array(*chain, dtype=bf16),
            array(*chain, dtype=bf16),
            array(members, blocks, width),
            array(members, PACK, width),
        ],
        chain_inv, chain_link, reach_residual, cell_cotangent,
        where=hbm, limit=60, flops=2_000_000_000,
        scratch=[
            pltpu.VMEM(chain, F32),
            pltpu.VMEM(chain, F32),
            pltpu.VMEM((members, blocks, width), F32),
            pltpu.VMEM((members, blocks, width), F32),
            pltpu.SemaphoreType.DMA((2 + 2 * members,)),
        ],
    )
    pair = lax.all_gather(local, "c")
    chip = run(pair_kernel, array(half, PACK, width), pair)
    sliced = run(
        slice_kernel, array(near.shape[0], piece + 8, width), near,
        where=hbm, limit=60, scratch=[pltpu.SemaphoreType.DMA((2,))],
    )
    chip, sliced = lax.optimization_barrier((chip, sliced))
    table = lax.all_gather(sliced, "zh").reshape(zs * owned, piece + 8, width)
    chips, plane = lax.optimization_barrier((lax.all_gather(chip, "y"), plane))
    matrices = array(2, half, width, width, dtype=bf16)
    schur, before, after, passing, first = run(
        chain_kernel,
        [matrices, matrices, matrices, array(8, width), array(zs, 8, width)],
        lower, upper, chips, outlet_link, scalars=2,
    )

    picked = run(pick_kernel, array(xs, owned, piece + 8, width), plane, table, scalars=1)
    merged = run(merge_kernel, array(owned, 3 * piece, width), swap(picked, "x"))
    first, merged = lax.optimization_barrier((first, merged))
    ends = lax.all_gather(merged, "y")
    terms = exchanged(first)
    tiles, ids, rows, spread = run(
        first_step_kernel,
        [
            array(2, 2 * half, width, width, dtype=bf16),
            array(cs * xs * zs, 8, width, dtype=jnp.int32),
            array(8, width),
            array(zs, 8, width),
        ],
        lower, upper, terms, ends, schur, first, scalars=2,
    )
    terms = exchanged(spread)
    for sweep in range(2, SWEEPS):
        spread = run(
            step_kernel, array(zs, 8, width), lower, upper, terms, ids, tiles, schur, rows, first, scalars=2
        )
        terms = exchanged(spread)
    sections, adjoint, shared = run(
        last_kernel,
        [array(owned, width), array(owned, width), array(8, width)],
        lower, upper, terms, ids, tiles, rows, before, after, passing,
        junction_inv, junction_residual, junction_cotangent, scalars=2,
    )
    cell_update, cell_adjoint = run(
        cells_kernel,
        [array(members, blocks, width), array(members, blocks, width)],
        lax.all_gather(shared, "c"), pair, high, low, forced, cell_cotangent,
    )
    return (cell_update, sections, cell_adjoint, adjoint)


def solution(mesh):
    line = mesh.shape["basin"] // 4
    near = math.gcd(line, 4)
    shape = (line // near, near, 4, 4, 2)
    grid = Mesh(mesh.devices.reshape(shape), ("zh", "zl", "x", "y", "c"))
    b, r = ("zh", "zl", "x"), ("y", "c")
    return jax.shard_map(
        shards,
        mesh=grid,
        in_specs=(
            P(b, r, None),
            P(b, r, None, None),
            P(b, r, None, None),
            P(b, None, None),
            P(b, None, None),
            P(b, None),
            P(b),
            P(b),
            P(b, r, None),
            P(b, None),
        ),
        out_specs=(P(b, r, None), P(b, None), P(b, r, None), P(b, None)),
        check_vma=False,
    )
```

```python
import jax
import jax.numpy as jnp
from jax import lax
from jax.experimental import pallas as pl
from jax.experimental.pallas import tpu as pltpu
from jax.sharding import Mesh, PartitionSpec as P

SWEEPS = 4
WIDTH = 128
PACK = WIDTH + 8
F32 = jnp.float32

smem = pl.BlockSpec(memory_space=pltpu.SMEM)
vmem = pl.BlockSpec(memory_space=pltpu.VMEM)
hbm = pl.BlockSpec(memory_space=pltpu.HBM)


def array(*shape, dtype=F32):
    return jax.ShapeDtypeStruct(shape, dtype)


def run(kernel, outs, *args, scalars=0, where=vmem, scratch=(), limit=40, flops=0):
    single = not isinstance(outs, list)
    shapes = [outs] if single else outs
    result = pl.pallas_call(
        kernel,
        out_shape=shapes,
        in_specs=[smem] * scalars + [where] * (len(args) - scalars),
        out_specs=[vmem] * len(shapes),
        scratch_shapes=scratch,
        compiler_params=pltpu.CompilerParams(vmem_limit_bytes=limit * 1024 * 1024),
        cost_estimate=pl.CostEstimate(flops=flops, bytes_accessed=flops // 100, transcendentals=0) if flops else None,
    )(*args)
    return result[0] if single else result


def two_parts(a):
    high = a.astype(jnp.bfloat16)
    return high, (a - high.astype(F32)).astype(jnp.bfloat16)


def dot(a, b, transposed=False):
    dims = (((1,), (1 if transposed else 0,)), ((), ()))
    return lax.dot_general(a, b, dims, preferred_element_type=F32)


def parts_of(a):
    return a if isinstance(a, tuple) else two_parts(a)


def product(a, b):
    (ah, al), (bh, bl) = parts_of(a), parts_of(b)
    return dot(ah, bh) + (dot(ah, bl) + dot(al, bh))


def along(vector, matrix, transposed):
    vh, vl = two_parts(vector)
    mh, ml = parts_of(matrix)
    both = dot(jnp.concatenate([vh, vl]), mh, transposed)
    return both[0:1] + (both[1:2] + dot(vh, ml, transposed))


def applied(matrix, row):
    return along(row, matrix, True)


def applied_transposed(matrix, row):
    return along(row, matrix, False)


def fetch(pairs, sems):
    copies = [pltpu.make_async_copy(src, dst, sems.at[i]) for i, (src, dst) in enumerate(pairs)]
    for copy in copies:
        copy.start()
    return copies


def table_kernel(inv_ref, residual_ref, cotangent_ref, out_ref, residual, cotangent, sems):
    piece = out_ref.shape[1] - 8
    start = pl.multiple_of(lax.axis_index("y") * piece, 8)
    copies = fetch(
        [
            (inv_ref.at[:, pl.ds(start, piece)], out_ref.at[:, :piece]),
            (residual_ref, residual),
            (cotangent_ref, cotangent),
        ],
        sems,
    )
    for copy in copies[1:]:
        copy.wait()
    for k in range(out_ref.shape[0]):
        out_ref[k, piece:] = jnp.concatenate(
            [residual[k : k + 1], cotangent[k : k + 1], jnp.zeros((6, WIDTH), F32)]
        )
    copies[0].wait()


def local_kernel(
    inv_hbm, link_hbm, residual_hbm, cotangent_hbm, high_ref, low_ref, forced_ref, out_ref,
    inv_ref, link_ref, residual_ref, cotangent_ref, sems,
):
    members, blocks = inv_ref.shape[:2]
    pairs = [(residual_hbm, residual_ref), (cotangent_hbm, cotangent_ref)]
    for s in range(members):
        pairs += [(inv_hbm.at[s], inv_ref.at[s]), (link_hbm.at[s], link_ref.at[s])]
    copies = fetch(pairs, sems)
    copies[0].wait()
    copies[1].wait()
    for s in range(members):
        copies[2 + 2 * s].wait()
        copies[3 + 2 * s].wait()
        m, f = [], []
        for i in range(blocks):
            inverse = two_parts(inv_ref[s, i])
            m.append(two_parts(product(inverse, two_parts(link_ref[s, i]))))
            high_ref[s, i], low_ref[s, i] = m[i]
            f.append(applied(inverse, residual_ref[s, i : i + 1]))
            forced_ref[s, i : i + 1] = f[i]
        total, vector = m[0], f[0]
        for i in range(1, blocks):
            total = product(m[i], total if i == 1 else two_parts(total))
            vector = applied(m[i], vector) + f[i]
        back = cotangent_ref[s, blocks - 1 : blocks]
        for i in range(blocks - 2, -1, -1):
            back = cotangent_ref[s, i : i + 1] + applied_transposed(m[i + 1], back)
        out_ref[s, :WIDTH] = total
        out_ref[s, WIDTH:] = jnp.concatenate(
            [vector, applied_transposed(m[0], back), jnp.zeros((6, WIDTH), F32)]
        )


def pair_kernel(pair_ref, out_ref, other_ref, rows_ref):
    half = out_ref.shape[0]
    c = lax.axis_index("c")
    first_s = c * half
    for k in range(half):
        first, second = pair_ref[0, first_s + k], pair_ref[1, first_s + k]
        one, two = two_parts(first[:WIDTH]), two_parts(second[:WIDTH])
        out_ref[k, :WIDTH] = product(two, one)
        out_ref[k, WIDTH:] = jnp.concatenate(
            [
                applied(two, first[WIDTH : WIDTH + 1]) + second[WIDTH : WIDTH + 1],
                applied_transposed(one, second[WIDTH + 1 : WIDTH + 2])
                + first[WIDTH + 1 : WIDTH + 2],
                jnp.zeros((6, WIDTH), F32),
            ]
        )
    for s in range(other_ref.shape[1]):
        keep(other_ref, s, pair_ref[1 - c, s, :WIDTH])
        rows_ref[s] = pair_ref[1 - c, s, WIDTH:]


def keep(ref, k, matrix):
    ref[0, k], ref[1, k] = two_parts(matrix)


def kept(ref, k):
    return ref[0, k], ref[1, k]


def chain_kernel(lower_ref, upper_ref, chips_ref, outlet_ref, schur_ref, before_ref, after_ref, rows_ref, spread_ref):
    chips, half = chips_ref.shape[:2]
    first_s = lax.axis_index("c") * half
    y = lax.axis_index("y")
    row = lax.broadcasted_iota(jnp.int32, (8, WIDTH), 0)
    lane = lax.broadcasted_iota(jnp.int32, (8, WIDTH), 1)
    eye = (
        lax.broadcasted_iota(jnp.int32, (WIDTH, WIDTH), 0)
        == lax.broadcasted_iota(jnp.int32, (WIDTH, WIDTH), 1)
    ).astype(F32)
    nothing = jnp.zeros((1, WIDTH), F32)
    ids = jnp.zeros((8, WIDTH), jnp.int32)
    payload = [nothing] * 8
    for k in range(half):
        ids = jnp.where(lane == k, lower_ref[first_s + k], ids)
        ids = jnp.where(lane == half + k, upper_ref[first_s + k], ids)
        maps = [two_parts(chips_ref[i, k, :WIDTH]) for i in range(chips)]
        before, before_row = eye, nothing
        reached, reached_row = chips_ref[0, k, :WIDTH], chips_ref[0, k, WIDTH : WIDTH + 1]
        for i in range(1, chips):
            before = jnp.where(y == i, reached, before)
            before_row = jnp.where(y == i, reached_row, before_row)
            if i < chips - 1:
                reached = product(maps[i], reached)
            reached_row = applied(maps[i], reached_row) + chips_ref[i, k, WIDTH : WIDTH + 1]
        schur = outlet_ref[first_s + k]
        payload[k] = applied(schur, reached_row)
        after = schur
        upward, after_row = nothing, nothing
        for i in range(chips - 1, -1, -1):
            after = jnp.where(y == i, schur, after)
            after_row = jnp.where(y == i, upward, after_row)
            schur = product(schur, maps[i])
            upward = applied_transposed(maps[i], upward) + chips_ref[i, k, WIDTH + 1 : WIDTH + 2]
        payload[half + k] = upward
        keep(schur_ref, k, schur)
        keep(before_ref, k, before)
        keep(after_ref, k, after)
        rows_ref[k : k + 1] = before_row
        rows_ref[half + k : half + k + 1] = after_row
    rows_ref[2 * half :] = jnp.zeros((2, WIDTH), F32)
    full = jnp.where(row == 2 * half, ids.astype(F32), jnp.concatenate(payload))
    for i in range(spread_ref.shape[0]):
        spread_ref[i] = full


def pick_kernel(ids_ref, table_ref, out_ref, sems):
    dests, owned = out_ref.shape[:2]
    half = owned // 2
    x = lax.axis_index("x")
    pairs, here = [], []
    for d in range(dests):
        for t in range(owned):
            junction = ids_ref[d * owned + (t + half) % owned]
            basin = lax.div(junction, owned)
            line = lax.div(basin, dests)
            at = line * owned + (junction - basin * owned)
            here.append(basin - line * dests == x)
            pairs.append((table_ref.at[at], out_ref.at[d, t]))
    copies = fetch(pairs, sems)
    for copy in copies:
        copy.wait()
    for d in range(dests):
        for t in range(owned):
            out_ref[d, t] = jnp.where(here[d * owned + t], out_ref[d, t], 0.0)


def rule(above, below, half):
    row = lax.broadcasted_iota(jnp.int32, (8, WIDTH), 0)
    return jnp.where(row < half, above, jnp.where(row < 2 * half, below, -2))


def gathered(ids, values, pattern, half):
    total = jnp.sum(jnp.where(ids == pattern[None], values, 0.0), axis=0)
    inflow, outflow = total[0:1], total[half : half + 1]
    for k in range(1, half):
        inflow = inflow + total[k : k + 1]
        outflow = outflow + total[half + k : half + k + 1]
    return inflow, outflow


def spread_rows(payload, spread_ref):
    full = jnp.concatenate(payload)
    for i in range(spread_ref.shape[0]):
        spread_ref[i] = full


def step(lower_ref, upper_ref, ids, values, tiles, schur_ref, ends, base, spread_ref):
    half = schur_ref.shape[1]
    first_s = lax.axis_index("c") * half
    payload = [jnp.zeros((1, WIDTH), F32)] * 8
    for k in range(half):
        pattern = rule(upper_ref[first_s + k], lower_ref[first_s + k], half)
        inflow, outflow = gathered(ids, values, pattern, half)
        head = applied(kept(tiles, k), ends[k : k + 1] + inflow)
        relief = applied_transposed(
            kept(tiles, half + k), ends[half + k : half + k + 1] + outflow
        )
        schur = kept(schur_ref, k)
        payload[k] = base[k : k + 1] + applied(schur, head)
        payload[half + k] = base[half + k : half + k + 1] + applied_transposed(schur, relief)
    spread_rows(payload, spread_ref)


def partial_kernel(lower_ref, upper_ref, terms_ref, picked_ref, ids_ref, rows_ref, merged_ref, spread_ref, tile_ref):
    half = picked_ref.shape[1] // 2
    piece = WIDTH // spread_ref.shape[0]
    first_s = lax.axis_index("c") * half
    start = pl.multiple_of(lax.axis_index("y") * piece, 8)
    row = lax.broadcasted_iota(jnp.int32, (8, WIDTH), 0)
    lane = lax.broadcasted_iota(jnp.int32, (8, WIDTH), 1)
    values = terms_ref[...].reshape(-1, 8, WIDTH)
    chosen = jnp.where((row == lane) & (row < 2 * half), values[:, 2 * half : 2 * half + 1], 0.0)
    ids = jnp.sum(chosen, axis=2, keepdims=True).astype(jnp.int32)
    ids = jnp.broadcast_to(ids, values.shape)
    ids_ref[...] = ids
    merged = picked_ref[0]
    for d in range(1, picked_ref.shape[0]):
        merged = merged + picked_ref[d]
    merged_ref[:, : piece + 8] = merged
    merged_ref[:, piece + 8 :] = jnp.zeros(
        (2 * half, merged_ref.shape[1] - piece - 8, WIDTH), F32
    )
    tile_ref[...] = jnp.zeros(tile_ref.shape, F32)
    payload = [jnp.zeros((1, WIDTH), F32)] * 8
    ends = [jnp.zeros((1, WIDTH), F32)] * 8
    for k in range(half):
        pattern = rule(upper_ref[first_s + k], lower_ref[first_s + k], half)
        inflow, outflow = gathered(ids, values, pattern, half)
        ends[k] = merged[k, piece : piece + 1]
        ends[half + k] = merged[half + k, piece + 1 : piece + 2]
        tile_ref[k, pl.ds(start, piece)] = merged[k, :piece]
        tile_ref[half + k, pl.ds(start, piece)] = merged[half + k, :piece]
        payload[k] = applied(tile_ref[k], ends[k] + inflow)
        payload[half + k] = applied_transposed(tile_ref[half + k], ends[half + k] + outflow)
    rows_ref[...] = jnp.concatenate(ends)
    spread_rows(payload, spread_ref)


def second_kernel(parts_ref, schur_ref, base_ref, spread_ref):
    half = schur_ref.shape[1]
    total = parts_ref[0]
    for i in range(1, parts_ref.shape[0]):
        total = total + parts_ref[i]
    base = base_ref[0]
    payload = [jnp.zeros((1, WIDTH), F32)] * 8
    for k in range(half):
        schur = kept(schur_ref, k)
        payload[k] = base[k : k + 1] + applied(schur, total[k : k + 1])
        payload[half + k] = base[half + k : half + k + 1] + applied_transposed(
            schur, total[half + k : half + k + 1]
        )
    spread_rows(payload, spread_ref)


def third_kernel(
    lower_ref, upper_ref, terms_ref, ids_ref, ends_ref, schur_ref, rows_ref, base_ref, tiles_ref, spread_ref
):
    piece = WIDTH // ends_ref.shape[0]
    for k in range(tiles_ref.shape[1]):
        keep(tiles_ref, k, jnp.concatenate([ends_ref[i, k, :piece] for i in range(ends_ref.shape[0])]))
    values = terms_ref[...].reshape(-1, 8, WIDTH)
    step(lower_ref, upper_ref, ids_ref[...], values, tiles_ref, schur_ref, rows_ref[...], base_ref[0], spread_ref)


def step_kernel(
    lower_ref, upper_ref, terms_ref, ids_ref, tiles_ref, schur_ref, rows_ref, base_ref, spread_ref
):
    values = terms_ref[...].reshape(-1, 8, WIDTH)
    step(lower_ref, upper_ref, ids_ref[...], values, tiles_ref, schur_ref, rows_ref[...], base_ref[0], spread_ref)


def last_kernel(
    lower_ref, upper_ref, terms_ref, ids_ref, tiles_ref, rows_ref, before_ref, after_ref, passing_ref,
    inv_ref, residual_ref, cotangent_ref, sections_ref, adjoint_ref, shared_ref,
):
    half = before_ref.shape[1]
    owned = inv_ref.shape[0]
    first_s = lax.axis_index("c") * half
    first_j = (lax.axis_index("z") * lax.axis_size("x") + lax.axis_index("x")) * owned
    values = terms_ref[...].reshape(-1, 8, WIDTH)
    ids = ids_ref[...]
    shared_ref[2 * half :] = jnp.zeros((2, WIDTH), F32)
    for k in range(half):
        pattern = rule(upper_ref[first_s + k], lower_ref[first_s + k], half)
        inflow, outflow = gathered(ids, values, pattern, half)
        head = applied(kept(tiles_ref, k), rows_ref[k : k + 1] + inflow)
        relief = applied_transposed(
            kept(tiles_ref, half + k), rows_ref[half + k : half + k + 1] + outflow
        )
        shared_ref[k : k + 1] = applied(kept(before_ref, k), head) + passing_ref[k : k + 1]
        shared_ref[half + k : half + k + 1] = (
            applied_transposed(kept(after_ref, k), relief) + passing_ref[half + k : half + k + 1]
        )
    for k in range(owned):
        inflow, outflow = gathered(ids, values, rule(first_j + k, first_j + k, half), half)
        sections_ref[k : k + 1] = applied(inv_ref[k], residual_ref[k : k + 1] + inflow)
        adjoint_ref[k : k + 1] = cotangent_ref[k : k + 1] + outflow


def cells_kernel(shared_ref, other_ref, passing_ref, high_ref, low_ref, forced_ref, cotangent_ref, update_ref, adjoint_ref):
    members, blocks = high_ref.shape[:2]
    half = members // 2
    c = lax.axis_index("c")
    for s in range(members):
        core, k = s // half, s % half
        enter = shared_ref[core, k : k + 1]
        leave = shared_ref[core, half + k : half + k + 1]
        matrix = kept(other_ref, s)
        further = applied(matrix, enter) + passing_ref[s, 0:1]
        nearer = applied_transposed(matrix, leave) + passing_ref[s, 1:2]
        enter = jnp.where(c == 1, further, enter)
        leave = jnp.where(c == 0, nearer, leave)
        for i in range(blocks):
            enter = applied((high_ref[s, i], low_ref[s, i]), enter) + forced_ref[s, i : i + 1]
            update_ref[s, i : i + 1] = enter
        carried = cotangent_ref[s, blocks - 1 : blocks] + leave
        adjoint_ref[s, blocks - 1 : blocks] = carried
        for i in range(blocks - 2, -1, -1):
            carried = cotangent_ref[s, i : i + 1] + applied_transposed(
                (high_ref[s, i + 1], low_ref[s, i + 1]), carried
            )
            adjoint_ref[s, i : i + 1] = carried


def swap(spread, axis):
    return lax.all_to_all(spread, axis, 0, 0, tiled=False)


def over_x(values):
    return swap(jnp.broadcast_to(values[None], (lax.axis_size("x"),) + values.shape), "x")


def exchanged(spread):
    along_x = over_x(swap(spread, "z"))
    return lax.all_gather(along_x.reshape(-1, WIDTH), "c")


def shards(
    reach_residual,
    chain_inv,
    chain_link,
    outlet_link,
    junction_inv,
    junction_residual,
    upper_junction,
    lower_junction,
    cell_cotangent,
    junction_cotangent,
):
    members, blocks, width = reach_residual.shape
    owned = junction_inv.shape[0]
    zs, xs, ys, cs = (lax.axis_size(a) for a in ("z", "x", "y", "c"))
    half = members // cs
    piece = width // ys
    bf16 = jnp.bfloat16
    lower, upper = lower_junction, upper_junction

    part = run(
        table_kernel,
        array(owned, piece + 8, width),
        junction_inv, junction_residual, junction_cotangent,
        where=hbm, limit=60,
        scratch=[
            pltpu.VMEM((owned, width), F32),
            pltpu.VMEM((owned, width), F32),
            pltpu.SemaphoreType.DMA((3,)),
        ],
    )
    table = lax.all_gather(part, "z").reshape(zs * owned, piece + 8, width)

    chain = (members, blocks, width, width)
    high, low, forced, local = run(
        local_kernel,
        [
            array(*chain, dtype=bf16),
            array(*chain, dtype=bf16),
            array(members, blocks, width),
            array(members, PACK, width),
        ],
        chain_inv, chain_link, reach_residual, cell_cotangent,
        where=hbm, limit=60, flops=2_000_000_000,
        scratch=[
            pltpu.VMEM(chain, F32),
            pltpu.VMEM(chain, F32),
            pltpu.VMEM((members, blocks, width), F32),
            pltpu.VMEM((members, blocks, width), F32),
            pltpu.SemaphoreType.DMA((2 + 2 * members,)),
        ],
    )
    pair = lax.all_gather(local, "c")
    chip, other, other_rows = run(
        pair_kernel,
        [array(half, PACK, width), array(2, members, width, width, dtype=bf16), array(members, 8, width)],
        pair,
    )
    chips = lax.all_gather(chip, "y")
    matrices = array(2, half, width, width, dtype=bf16)
    schur, before, after, passing, first = run(
        chain_kernel,
        [matrices, matrices, matrices, array(8, width), array(zs, 8, width)],
        lower, upper, chips, outlet_link, scalars=2,
    )

    terms = exchanged(first)
    plane = lax.dynamic_slice(
        terms.reshape(cs, xs, zs, 8, width),
        (lax.axis_index("c"), 0, lax.axis_index("z"), 2 * half, 0),
        (1, xs, 1, 1, owned),
    ).reshape(-1).astype(jnp.int32)
    picked = run(
        pick_kernel, array(xs, owned, piece + 8, width), plane, table,
        scalars=1, where=hbm, limit=60, scratch=[pltpu.SemaphoreType.DMA((xs * owned,))],
    )
    ids, rows, merged, parts = run(
        partial_kernel,
        [
            array(cs * xs * zs, 8, width, dtype=jnp.int32),
            array(8, width),
            array(owned, 3 * piece, width),
            array(ys, 8, width),
        ],
        lower, upper, terms, swap(picked, "x"), scalars=2,
        scratch=[pltpu.VMEM((owned, width, width), F32)],
    )
    parts, merged = lax.optimization_barrier((parts, merged))
    ends = lax.all_gather(merged, "y")
    terms = exchanged(run(second_kernel, array(zs, 8, width), swap(parts, "y"), schur, first))
    tiles, spread = run(
        third_kernel,
        [array(2, 2 * half, width, width, dtype=bf16), array(zs, 8, width)],
        lower, upper, terms, ids, ends, schur, rows, first, scalars=2,
    )
    terms = exchanged(spread)
    for sweep in range(3, SWEEPS):
        spread = run(
            step_kernel, array(zs, 8, width), lower, upper, terms, ids, tiles, schur, rows, first, scalars=2
        )
        terms = exchanged(spread)
    sections, adjoint, shared = run(
        last_kernel,
        [array(owned, width), array(owned, width), array(8, width)],
        lower, upper, terms, ids, tiles, rows, before, after, passing,
        junction_inv, junction_residual, junction_cotangent, scalars=2,
    )
    cell_update, cell_adjoint = run(
        cells_kernel,
        [array(members, blocks, width), array(members, blocks, width)],
        lax.all_gather(shared, "c"), other, other_rows, high, low, forced, cell_cotangent,
    )
    return (cell_update, sections, cell_adjoint, adjoint)


def solution(mesh):
    basins = mesh.shape["basin"]
    grid = Mesh(mesh.devices.reshape(basins // 4, 4, 4, 2), ("z", "x", "y", "c"))
    b, r = ("z", "x"), ("y", "c")
    return jax.shard_map(
        shards,
        mesh=grid,
        in_specs=(
            P(b, r, None),
            P(b, r, None, None),
            P(b, r, None, None),
            P(b, None, None),
            P(b, None, None),
            P(b, None),
            P(b),
            P(b),
            P(b, r, None),
            P(b, None),
        ),
        out_specs=(P(b, r, None), P(b, None), P(b, r, None), P(b, None)),
        check_vma=False,
    )
```

```python
import functools

import jax
import jax.numpy as jnp
from jax import lax
from jax.experimental import pallas as pl
from jax.experimental.pallas import tpu as pltpu
from jax.sharding import Mesh, PartitionSpec as P

SWEEPS = 4
WIDTH = 128
PACK = WIDTH + 8
F32 = jnp.float32

smem = pl.BlockSpec(memory_space=pltpu.SMEM)
vmem = pl.BlockSpec(memory_space=pltpu.VMEM)
hbm = pl.BlockSpec(memory_space=pltpu.HBM)


def array(*shape, dtype=F32):
    return jax.ShapeDtypeStruct(shape, dtype)


def run(kernel, outs, *args, scalars=0, where=vmem, scratch=(), limit=40, flops=0):
    single = not isinstance(outs, list)
    shapes = [outs] if single else outs
    result = pl.pallas_call(
        kernel,
        out_shape=shapes,
        in_specs=[smem] * scalars + [where] * (len(args) - scalars),
        out_specs=[vmem] * len(shapes),
        scratch_shapes=scratch,
        compiler_params=pltpu.CompilerParams(vmem_limit_bytes=limit * 1024 * 1024),
        cost_estimate=pl.CostEstimate(flops=flops, bytes_accessed=flops // 100, transcendentals=0) if flops else None,
    )(*args)
    return result[0] if single else result


def two_parts(a):
    high = a.astype(jnp.bfloat16)
    return high, (a - high.astype(F32)).astype(jnp.bfloat16)


def dot(a, b, transposed=False):
    dims = (((1,), (1 if transposed else 0,)), ((), ()))
    return lax.dot_general(a, b, dims, preferred_element_type=F32)


def parts_of(a):
    return a if isinstance(a, tuple) else two_parts(a)


def product(a, b):
    (ah, al), (bh, bl) = parts_of(a), parts_of(b)
    return dot(ah, bh) + (dot(ah, bl) + dot(al, bh))


def along(vector, matrix, transposed):
    vh, vl = two_parts(vector)
    mh, ml = parts_of(matrix)
    both = dot(jnp.concatenate([vh, vl]), mh, transposed)
    return both[0:1] + (both[1:2] + dot(vh, ml, transposed))


def applied(matrix, row):
    return along(row, matrix, True)


def applied_transposed(matrix, row):
    return along(row, matrix, False)


def fetch(pairs, sems):
    copies = [pltpu.make_async_copy(src, dst, sems.at[i]) for i, (src, dst) in enumerate(pairs)]
    for copy in copies:
        copy.start()
    return copies


def table_kernel(inv_ref, residual_ref, cotangent_ref, out_ref, residual, cotangent, sems):
    piece = out_ref.shape[1] - 8
    start = pl.multiple_of(lax.axis_index("y") * piece, 8)
    copies = fetch(
        [
            (inv_ref.at[:, pl.ds(start, piece)], out_ref.at[:, :piece]),
            (residual_ref, residual),
            (cotangent_ref, cotangent),
        ],
        sems,
    )
    for copy in copies[1:]:
        copy.wait()
    for k in range(out_ref.shape[0]):
        out_ref[k, piece:] = jnp.concatenate(
            [residual[k : k + 1], cotangent[k : k + 1], jnp.zeros((6, WIDTH), F32)]
        )
    copies[0].wait()


def local_kernel(
    inv_hbm, link_hbm, residual_hbm, cotangent_hbm, maps_ref, vectors_ref, out_ref,
    inv_ref, link_ref, residual_ref, cotangent_ref, sems,
):
    members, blocks = inv_ref.shape[:2]
    pairs = [(residual_hbm, residual_ref), (cotangent_hbm, cotangent_ref)]
    for s in range(members):
        pairs += [(inv_hbm.at[s], inv_ref.at[s]), (link_hbm.at[s], link_ref.at[s])]
    copies = fetch(pairs, sems)
    copies[0].wait()
    copies[1].wait()
    for s in range(members):
        copies[2 + 2 * s].wait()
        copies[3 + 2 * s].wait()
        m, f = [], []
        for i in range(blocks):
            inverse = two_parts(inv_ref[s, i])
            m.append(two_parts(product(inverse, two_parts(link_ref[s, i]))))
            f.append(applied(inverse, residual_ref[s, i : i + 1]))
        rows = [jnp.zeros((1, WIDTH), F32)] * 8
        total, vector = m[0], f[0]
        for i in range(blocks):
            if i:
                result = product(m[i], total)
                total = two_parts(result)
                vector = applied(m[i], vector) + f[i]
            maps_ref[0, s, i], maps_ref[1, s, i] = total
            rows[i] = vector
        back = cotangent_ref[s, blocks - 1 : blocks]
        rows[2 * blocks - 1] = back
        suffix = None
        for i in range(blocks - 2, -1, -1):
            back = cotangent_ref[s, i : i + 1] + applied_transposed(m[i + 1], back)
            rows[blocks + i] = back
            suffix = m[i + 1] if suffix is None else two_parts(product(suffix, m[i + 1]))
            maps_ref[0, s, blocks + i], maps_ref[1, s, blocks + i] = suffix
        vectors_ref[s] = jnp.concatenate(rows)
        out_ref[s, :WIDTH] = result
        out_ref[s, WIDTH:] = jnp.concatenate(
            [vector, applied_transposed(m[0], back), jnp.zeros((6, WIDTH), F32)]
        )


def pair_kernel(pair_ref, out_ref, other_ref, rows_ref):
    half = out_ref.shape[0]
    c = lax.axis_index("c")
    first_s = c * half
    for k in range(half):
        first, second = pair_ref[0, first_s + k], pair_ref[1, first_s + k]
        one, two = two_parts(first[:WIDTH]), two_parts(second[:WIDTH])
        out_ref[k, :WIDTH] = product(two, one)
        out_ref[k, WIDTH:] = jnp.concatenate(
            [
                applied(two, first[WIDTH : WIDTH + 1]) + second[WIDTH : WIDTH + 1],
                applied_transposed(one, second[WIDTH + 1 : WIDTH + 2])
                + first[WIDTH + 1 : WIDTH + 2],
                jnp.zeros((6, WIDTH), F32),
            ]
        )
    for s in range(other_ref.shape[1]):
        keep(other_ref, s, pair_ref[1 - c, s, :WIDTH])
        rows_ref[s] = pair_ref[1 - c, s, WIDTH:]


def keep(ref, k, matrix):
    ref[0, k], ref[1, k] = two_parts(matrix)


def kept(ref, k):
    return ref[0, k], ref[1, k]


def chain_kernel(lower_ref, upper_ref, chips_ref, outlet_ref, schur_ref, before_ref, after_ref, rows_ref, spread_ref):
    chips, half = chips_ref.shape[:2]
    first_s = lax.axis_index("c") * half
    y = lax.axis_index("y")
    row = lax.broadcasted_iota(jnp.int32, (8, WIDTH), 0)
    lane = lax.broadcasted_iota(jnp.int32, (8, WIDTH), 1)
    eye = (
        lax.broadcasted_iota(jnp.int32, (WIDTH, WIDTH), 0)
        == lax.broadcasted_iota(jnp.int32, (WIDTH, WIDTH), 1)
    ).astype(F32)
    nothing = jnp.zeros((1, WIDTH), F32)
    ids = jnp.zeros((8, WIDTH), jnp.int32)
    payload = [nothing] * 8
    for k in range(half):
        ids = jnp.where(lane == k, lower_ref[first_s + k], ids)
        ids = jnp.where(lane == half + k, upper_ref[first_s + k], ids)
        maps = [two_parts(chips_ref[i, k, :WIDTH]) for i in range(chips)]
        before, before_row = eye, nothing
        reached, reached_row = chips_ref[0, k, :WIDTH], chips_ref[0, k, WIDTH : WIDTH + 1]
        for i in range(1, chips):
            before = jnp.where(y == i, reached, before)
            before_row = jnp.where(y == i, reached_row, before_row)
            if i < chips - 1:
                reached = product(maps[i], reached)
            reached_row = applied(maps[i], reached_row) + chips_ref[i, k, WIDTH : WIDTH + 1]
        schur = outlet_ref[first_s + k]
        payload[k] = applied(schur, reached_row)
        after = schur
        upward, after_row = nothing, nothing
        for i in range(chips - 1, -1, -1):
            after = jnp.where(y == i, schur, after)
            after_row = jnp.where(y == i, upward, after_row)
            schur = product(schur, maps[i])
            upward = applied_transposed(maps[i], upward) + chips_ref[i, k, WIDTH + 1 : WIDTH + 2]
        payload[half + k] = upward
        keep(schur_ref, k, schur)
        keep(before_ref, k, before)
        keep(after_ref, k, after)
        rows_ref[k : k + 1] = before_row
        rows_ref[half + k : half + k + 1] = after_row
    rows_ref[2 * half :] = jnp.zeros((2, WIDTH), F32)
    full = jnp.where(row == 2 * half, ids.astype(F32), jnp.concatenate(payload))
    for i in range(spread_ref.shape[0]):
        spread_ref[i] = full


def pick_kernel(ids_ref, table_ref, out_ref, sems):
    dests, owned = out_ref.shape[:2]
    half = owned // 2
    x, c = lax.axis_index("x"), lax.axis_index("c")
    pairs, here = [], []
    for d in range(dests):
        for t in range(owned):
            junction = ids_ref[(c * dests + d) * owned + (t + half) % owned]
            basin = lax.div(junction, owned)
            line = lax.div(basin, dests)
            at = line * owned + (junction - basin * owned)
            here.append(basin - line * dests == x)
            pairs.append((table_ref.at[at], out_ref.at[d, t]))
    copies = fetch(pairs, sems)
    for copy in copies:
        copy.wait()
    for d in range(dests):
        for t in range(owned):
            out_ref[d, t] = jnp.where(here[d * owned + t], out_ref[d, t], 0.0)


def rule(above, below, half):
    row = lax.broadcasted_iota(jnp.int32, (8, WIDTH), 0)
    return jnp.where(row < half, above, jnp.where(row < 2 * half, below, -2))


def gathered(ids, values, pattern, half):
    total = jnp.sum(jnp.where(ids == pattern[None], values, 0.0), axis=0)
    inflow, outflow = total[0:1], total[half : half + 1]
    for k in range(1, half):
        inflow = inflow + total[k : k + 1]
        outflow = outflow + total[half + k : half + k + 1]
    return inflow, outflow


def source_ids(values, half):
    row = lax.broadcasted_iota(jnp.int32, (8, WIDTH), 0)
    lane = lax.broadcasted_iota(jnp.int32, (8, WIDTH), 1)
    chosen = jnp.where((row == lane) & (row < 2 * half), values[:, 2 * half : 2 * half + 1], 0.0)
    ids = jnp.sum(chosen, axis=2, keepdims=True).astype(jnp.int32)
    return jnp.broadcast_to(ids, values.shape)


def sums_kernel(plane_ref, ids_ref, terms_ref, out_ref, *, half, cores, own):
    ids, values = ids_ref[...], terms_ref[...]
    sides = out_ref.shape[0] // cores
    owned = cores * half
    line = lax.axis_index("z") * sides
    nothing = jnp.zeros((1, WIDTH), F32)
    for d in range(out_ref.shape[0]):
        x, c = d // cores, d % cores
        at = (c * sides + x) * owned
        rows = [nothing] * out_ref.shape[1]
        for k in range(half):
            pattern = rule(plane_ref[at + half + k], plane_ref[at + k], half)
            rows[k], rows[half + k] = gathered(ids, values, pattern, half)
            if own:
                junction = (line + x) * owned + c * half + k
                pattern = rule(junction, junction, half)
                rows[8 + k], rows[8 + half + k] = gathered(ids, values, pattern, half)
        out_ref[d] = jnp.concatenate(rows)


def summed(parts_ref):
    total = parts_ref[0]
    for i in range(1, parts_ref.shape[0]):
        total = total + parts_ref[i]
    return total


def spread_rows(payload, spread_ref):
    full = jnp.concatenate(payload)
    for i in range(spread_ref.shape[0]):
        spread_ref[i] = full


def step(total, tiles_ref, schur_ref, ends, base, spread_ref):
    half = schur_ref.shape[1]
    payload = [jnp.zeros((1, WIDTH), F32)] * 8
    total = total + ends
    for k in range(half):
        other = half + k
        head, relief = total[k : k + 1], total[other : other + 1]
        if tiles_ref is not None:
            head = applied(kept(tiles_ref, k), head)
            relief = applied_transposed(kept(tiles_ref, other), relief)
        schur = kept(schur_ref, k)
        payload[k] = base[k : k + 1] + applied(schur, head)
        payload[other] = base[other : other + 1] + applied_transposed(schur, relief)
    spread_rows(payload, spread_ref)


def partial_kernel(lower_ref, upper_ref, terms_ref, picked_ref, ids_ref, rows_ref, merged_ref, spread_ref, tile_ref):
    half = picked_ref.shape[1] // 2
    piece = WIDTH // spread_ref.shape[0]
    first_s = lax.axis_index("c") * half
    start = pl.multiple_of(lax.axis_index("y") * piece, 8)
    values = terms_ref[...].reshape(-1, 8, WIDTH)
    ids = source_ids(values, half)
    count = ids_ref.shape[0] * 8
    column = pl.multiple_of(lax.axis_index("x") * count, 8)
    ids_ref[...] = source_ids(
        terms_ref[lax.axis_index("c"), pl.ds(column, count)].reshape(ids_ref.shape), half
    )
    merged = picked_ref[0]
    for d in range(1, picked_ref.shape[0]):
        merged = merged + picked_ref[d]
    merged_ref[:, : piece + 8] = merged
    merged_ref[:, piece + 8 :] = jnp.zeros(
        (2 * half, merged_ref.shape[1] - piece - 8, WIDTH), F32
    )
    tile_ref[...] = jnp.zeros(tile_ref.shape, F32)
    payload = [jnp.zeros((1, WIDTH), F32)] * 8
    ends = [jnp.zeros((1, WIDTH), F32)] * 8
    for k in range(half):
        pattern = rule(upper_ref[first_s + k], lower_ref[first_s + k], half)
        inflow, outflow = gathered(ids, values, pattern, half)
        ends[k] = merged[k, piece : piece + 1]
        ends[half + k] = merged[half + k, piece + 1 : piece + 2]
        tile_ref[k, pl.ds(start, piece)] = merged[k, :piece]
        tile_ref[half + k, pl.ds(start, piece)] = merged[half + k, :piece]
        payload[k] = applied(tile_ref[k], ends[k] + inflow)
        payload[half + k] = applied_transposed(tile_ref[half + k], ends[half + k] + outflow)
    rows_ref[...] = jnp.concatenate(ends)
    spread_rows(payload, spread_ref)


def second_kernel(parts_ref, schur_ref, base_ref, spread_ref):
    step(summed(parts_ref), None, schur_ref, 0.0, base_ref[0], spread_ref)


def third_kernel(parts_ref, ends_ref, schur_ref, rows_ref, base_ref, tiles_ref, spread_ref):
    piece = WIDTH // ends_ref.shape[0]
    for k in range(tiles_ref.shape[1]):
        keep(tiles_ref, k, jnp.concatenate([ends_ref[i, k, :piece] for i in range(ends_ref.shape[0])]))
    step(summed(parts_ref), tiles_ref, schur_ref, rows_ref[...], base_ref[0], spread_ref)


def step_kernel(parts_ref, tiles_ref, schur_ref, rows_ref, base_ref, spread_ref):
    step(summed(parts_ref), tiles_ref, schur_ref, rows_ref[...], base_ref[0], spread_ref)


def last_kernel(
    parts_ref, tiles_ref, rows_ref, before_ref, after_ref, passing_ref,
    inv_ref, residual_ref, cotangent_ref, shared_ref,
):
    half = before_ref.shape[1]
    c = lax.axis_index("c")
    total = summed(parts_ref)
    ends = total[:8] + rows_ref[...]
    out = [jnp.zeros((1, WIDTH), F32)] * 16
    for k in range(half):
        other = half + k
        head = applied(kept(tiles_ref, k), ends[k : k + 1])
        relief = applied_transposed(kept(tiles_ref, other), ends[other : other + 1])
        out[k] = applied(kept(before_ref, k), head) + passing_ref[k : k + 1]
        out[other] = applied_transposed(kept(after_ref, k), relief) + passing_ref[other : other + 1]
        residual = jnp.where(c == 1, residual_ref[other : other + 1], residual_ref[k : k + 1])
        cotangent = jnp.where(c == 1, cotangent_ref[other : other + 1], cotangent_ref[k : k + 1])
        out[8 + k] = applied(inv_ref[c * half + k], residual + total[8 + k : 9 + k])
        out[8 + other] = cotangent + total[8 + other : 9 + other]
    shared_ref[...] = jnp.concatenate(out)


def cells_kernel(
    shared_ref, other_ref, passing_ref, maps_ref, vectors_ref,
    update_ref, sections_ref, adjoint_ref, junction_ref,
):
    members, blocks = update_ref.shape[:2]
    half = members // 2
    c = lax.axis_index("c")
    for s in range(members):
        core, k = s // half, s % half
        sections_ref[s : s + 1] = shared_ref[core, 8 + k : 9 + k]
        junction_ref[s : s + 1] = shared_ref[core, 8 + half + k : 9 + half + k]
        enter = shared_ref[core, k : k + 1]
        leave = shared_ref[core, half + k : half + k + 1]
        matrix = kept(other_ref, s)
        further = applied(matrix, enter) + passing_ref[s, 0:1]
        nearer = applied_transposed(matrix, leave) + passing_ref[s, 1:2]
        enter = jnp.where(c == 1, further, enter)
        leave = jnp.where(c == 0, nearer, leave)
        rows, back = [], []
        for i in range(blocks):
            rows.append(
                applied((maps_ref[0, s, i], maps_ref[1, s, i]), enter) + vectors_ref[s, i : i + 1]
            )
            if i < blocks - 1:
                suffix = (maps_ref[0, s, blocks + i], maps_ref[1, s, blocks + i])
                change = applied_transposed(suffix, leave)
            else:
                change = leave
            back.append(change + vectors_ref[s, blocks + i : blocks + i + 1])
        update_ref[s] = jnp.concatenate(rows)
        adjoint_ref[s] = jnp.concatenate(back)


def swap(spread, axis):
    return lax.all_to_all(spread, axis, 0, 0, tiled=False)


def over_x(values):
    return swap(jnp.broadcast_to(values[None], (lax.axis_size("x"),) + values.shape), "x")


def exchanged(spread):
    along_x = over_x(swap(spread, "z"))
    return lax.all_gather(along_x.reshape(-1, WIDTH), "c")


def shards(
    reach_residual,
    chain_inv,
    chain_link,
    outlet_link,
    junction_inv,
    junction_residual,
    upper_junction,
    lower_junction,
    cell_cotangent,
    junction_cotangent,
):
    members, blocks, width = reach_residual.shape
    owned = junction_inv.shape[0]
    zs, xs, ys, cs = (lax.axis_size(a) for a in ("z", "x", "y", "c"))
    half = members // cs
    piece = width // ys
    bf16 = jnp.bfloat16
    lower, upper = lower_junction, upper_junction

    part = run(
        table_kernel,
        array(owned, piece + 8, width),
        junction_inv, junction_residual, junction_cotangent,
        where=hbm, limit=60,
        scratch=[
            pltpu.VMEM((owned, width), F32),
            pltpu.VMEM((owned, width), F32),
            pltpu.SemaphoreType.DMA((3,)),
        ],
    )
    table = lax.all_gather(part, "z").reshape(zs * owned, piece + 8, width)

    chain = (members, blocks, width, width)
    maps, vectors, local = run(
        local_kernel,
        [
            array(2, members, 2 * blocks - 1, width, width, dtype=bf16),
            array(members, 8, width),
            array(members, PACK, width),
        ],
        chain_inv, chain_link, reach_residual, cell_cotangent,
        where=hbm, limit=60, flops=2_000_000_000,
        scratch=[
            pltpu.VMEM(chain, F32),
            pltpu.VMEM(chain, F32),
            pltpu.VMEM((members, blocks, width), F32),
            pltpu.VMEM((members, blocks, width), F32),
            pltpu.SemaphoreType.DMA((2 + 2 * members,)),
        ],
    )
    pair = lax.all_gather(local, "c")
    chip, other, other_rows = run(
        pair_kernel,
        [array(half, PACK, width), array(2, members, width, width, dtype=bf16), array(members, 8, width)],
        pair,
    )
    chips = lax.all_gather(chip, "y")
    matrices = array(2, half, width, width, dtype=bf16)
    schur, before, after, passing, first = run(
        chain_kernel,
        [matrices, matrices, matrices, array(8, width), array(zs, 8, width)],
        lower, upper, chips, outlet_link, scalars=2,
    )

    terms = exchanged(first)
    plane = lax.dynamic_slice(
        terms.reshape(cs, xs, zs, 8, width),
        (0, 0, lax.axis_index("z"), 2 * half, 0),
        (cs, xs, 1, 1, owned),
    ).reshape(-1).astype(jnp.int32)
    picked = run(
        pick_kernel, array(xs, owned, piece + 8, width), plane, table,
        scalars=1, where=hbm, limit=60, scratch=[pltpu.SemaphoreType.DMA((xs * owned,))],
    )
    ids, rows, merged, parts = run(
        partial_kernel,
        [
            array(zs, 8, width, dtype=jnp.int32),
            array(8, width),
            array(owned, 3 * piece, width),
            array(ys, 8, width),
        ],
        lower, upper, terms, swap(picked, "x"), scalars=2,
        scratch=[pltpu.VMEM((owned, width, width), F32)],
    )
    parts, merged = lax.optimization_barrier((parts, merged))
    ends = lax.all_gather(merged, "y")
    sides = ("x", "c")

    def sums(spread, own):
        kernel = functools.partial(sums_kernel, half=half, cores=cs, own=own)
        shape = array(xs * cs, 16 if own else 8, width)
        return swap(run(kernel, shape, plane, ids, swap(spread, "z"), scalars=1), sides)

    spread = run(second_kernel, array(zs, 8, width), swap(parts, "y"), schur, first)
    tiles, spread = run(
        third_kernel,
        [array(2, 2 * half, width, width, dtype=bf16), array(zs, 8, width)],
        sums(spread, False), ends, schur, rows, first,
    )
    for sweep in range(3, SWEEPS):
        spread = run(
            step_kernel, array(zs, 8, width), sums(spread, False), tiles, schur, rows, first
        )
    shared = run(
        last_kernel, array(16, width), sums(spread, True), tiles, rows, before, after, passing,
        junction_inv, junction_residual, junction_cotangent,
    )
    cell_update, sections, cell_adjoint, adjoint = run(
        cells_kernel,
        [
            array(members, blocks, width), array(owned, width),
            array(members, blocks, width), array(owned, width),
        ],
        lax.all_gather(shared, "c"), other, other_rows, maps, vectors,
    )
    return (cell_update, sections, cell_adjoint, adjoint)


def solution(mesh):
    basins = mesh.shape["basin"]
    grid = Mesh(mesh.devices.reshape(basins // 4, 4, 4, 2), ("z", "x", "y", "c"))
    b, r = ("z", "x"), ("y", "c")
    return jax.shard_map(
        shards,
        mesh=grid,
        in_specs=(
            P(b, r, None),
            P(b, r, None, None),
            P(b, r, None, None),
            P(b, None, None),
            P(b, None, None),
            P(b, None),
            P(b),
            P(b),
            P(b, r, None),
            P(b, None),
        ),
        out_specs=(P(b, r, None), P(b, None), P(b, r, None), P(b, None)),
        check_vma=False,
    )
```

```python
import functools

import jax
import jax.numpy as jnp
from jax import lax
from jax.experimental import pallas as pl
from jax.experimental.pallas import tpu as pltpu
from jax.sharding import Mesh, PartitionSpec as P

SWEEPS = 4
WIDTH = 128
PACK = WIDTH + 8
F32 = jnp.float32

smem = pl.BlockSpec(memory_space=pltpu.SMEM)
vmem = pl.BlockSpec(memory_space=pltpu.VMEM)
hbm = pl.BlockSpec(memory_space=pltpu.HBM)


def array(*shape, dtype=F32):
    return jax.ShapeDtypeStruct(shape, dtype)


def run(kernel, outs, *args, scalars=0, where=vmem, scratch=(), limit=40, flops=0):
    single = not isinstance(outs, list)
    shapes = [outs] if single else outs
    result = pl.pallas_call(
        kernel,
        out_shape=shapes,
        in_specs=[smem] * scalars
        + (where if isinstance(where, list) else [where] * (len(args) - scalars)),
        out_specs=[vmem] * len(shapes),
        scratch_shapes=scratch,
        compiler_params=pltpu.CompilerParams(vmem_limit_bytes=limit * 1024 * 1024),
        cost_estimate=pl.CostEstimate(flops=flops, bytes_accessed=flops // 100, transcendentals=0) if flops else None,
    )(*args)
    return result[0] if single else result


def two_parts(a):
    high = a.astype(jnp.bfloat16)
    return high, (a - high.astype(F32)).astype(jnp.bfloat16)


def dot(a, b, transposed=False):
    dims = (((1,), (1 if transposed else 0,)), ((), ()))
    return lax.dot_general(a, b, dims, preferred_element_type=F32)


def parts_of(a):
    return a if isinstance(a, tuple) else two_parts(a)


def product(a, b):
    (ah, al), (bh, bl) = parts_of(a), parts_of(b)
    return dot(ah, bh) + (dot(ah, bl) + dot(al, bh))


def along(vector, matrix, transposed):
    vh, vl = two_parts(vector)
    mh, ml = parts_of(matrix)
    both = dot(jnp.concatenate([vh, vl]), mh, transposed)
    return both[0:1] + (both[1:2] + dot(vh, ml, transposed))


def applied(matrix, row):
    return along(row, matrix, True)


def applied_transposed(matrix, row):
    return along(row, matrix, False)


def fetch(pairs, sems):
    copies = [pltpu.make_async_copy(src, dst, sems.at[i]) for i, (src, dst) in enumerate(pairs)]
    for copy in copies:
        copy.start()
    return copies


def table_kernel(inv_ref, residual_ref, cotangent_ref, out_ref, residual, cotangent, sems):
    piece = out_ref.shape[1] - 8
    start = pl.multiple_of(lax.axis_index("y") * piece, 8)
    copies = fetch(
        [
            (inv_ref.at[:, pl.ds(start, piece)], out_ref.at[:, :piece]),
            (residual_ref, residual),
            (cotangent_ref, cotangent),
        ],
        sems,
    )
    for copy in copies[1:]:
        copy.wait()
    for k in range(out_ref.shape[0]):
        out_ref[k, piece:] = jnp.concatenate(
            [residual[k : k + 1], cotangent[k : k + 1], jnp.zeros((6, WIDTH), F32)]
        )
    copies[0].wait()


def local_kernel(
    inv_hbm, link_hbm, residual_hbm, cotangent_hbm, maps_ref, vectors_ref, out_ref,
    inv_ref, link_ref, residual_ref, cotangent_ref, sems,
):
    members, blocks = inv_ref.shape[:2]
    pairs = [(residual_hbm, residual_ref), (cotangent_hbm, cotangent_ref)]
    for s in range(members):
        pairs += [(inv_hbm.at[s], inv_ref.at[s]), (link_hbm.at[s], link_ref.at[s])]
    copies = fetch(pairs, sems)
    copies[0].wait()
    copies[1].wait()
    for s in range(members):
        copies[2 + 2 * s].wait()
        copies[3 + 2 * s].wait()
        m, f = [], []
        for i in range(blocks):
            inverse = two_parts(inv_ref[s, i])
            m.append(two_parts(product(inverse, two_parts(link_ref[s, i]))))
            f.append(applied(inverse, residual_ref[s, i : i + 1]))
        rows = [jnp.zeros((1, WIDTH), F32)] * 8
        total, vector = m[0], f[0]
        for i in range(blocks):
            if i:
                result = product(m[i], total)
                total = two_parts(result)
                vector = applied(m[i], vector) + f[i]
            maps_ref[0, s, i], maps_ref[1, s, i] = total
            rows[i] = vector
        back = cotangent_ref[s, blocks - 1 : blocks]
        rows[2 * blocks - 1] = back
        suffix = None
        for i in range(blocks - 2, -1, -1):
            back = cotangent_ref[s, i : i + 1] + applied_transposed(m[i + 1], back)
            rows[blocks + i] = back
            suffix = m[i + 1] if suffix is None else two_parts(product(suffix, m[i + 1]))
            maps_ref[0, s, blocks + i], maps_ref[1, s, blocks + i] = suffix
        vectors_ref[s] = jnp.concatenate(rows)
        out_ref[s, :WIDTH] = result
        out_ref[s, WIDTH:] = jnp.concatenate(
            [vector, applied_transposed(m[0], back), jnp.zeros((6, WIDTH), F32)]
        )


def pair_kernel(pair_ref, out_ref, other_ref, rows_ref):
    half = out_ref.shape[0]
    c = lax.axis_index("c")
    first_s = c * half
    for k in range(half):
        first, second = pair_ref[0, first_s + k], pair_ref[1, first_s + k]
        one, two = two_parts(first[:WIDTH]), two_parts(second[:WIDTH])
        out_ref[k, :WIDTH] = product(two, one)
        out_ref[k, WIDTH:] = jnp.concatenate(
            [
                applied(two, first[WIDTH : WIDTH + 1]) + second[WIDTH : WIDTH + 1],
                applied_transposed(one, second[WIDTH + 1 : WIDTH + 2])
                + first[WIDTH + 1 : WIDTH + 2],
                jnp.zeros((6, WIDTH), F32),
            ]
        )
    for s in range(other_ref.shape[1]):
        keep(other_ref, s, pair_ref[1 - c, s, :WIDTH])
        rows_ref[s] = pair_ref[1 - c, s, WIDTH:]


def keep(ref, k, matrix):
    ref[0, k], ref[1, k] = two_parts(matrix)


def kept(ref, k):
    return ref[0, k], ref[1, k]


def chain_kernel(lower_ref, upper_ref, chips_ref, outlet_ref, schur_ref, ways_ref, spread_ref):
    chips, half = chips_ref.shape[:2]
    first_s = lax.axis_index("c") * half
    y = lax.axis_index("y")
    row = lax.broadcasted_iota(jnp.int32, (8, WIDTH), 0)
    lane = lax.broadcasted_iota(jnp.int32, (8, WIDTH), 1)
    eye = (
        lax.broadcasted_iota(jnp.int32, (WIDTH, WIDTH), 0)
        == lax.broadcasted_iota(jnp.int32, (WIDTH, WIDTH), 1)
    ).astype(F32)
    nothing = jnp.zeros((1, WIDTH), F32)
    ids = jnp.zeros((8, WIDTH), jnp.int32)
    payload = [nothing] * 8
    for k in range(half):
        ids = jnp.where(lane == k, lower_ref[first_s + k], ids)
        ids = jnp.where(lane == half + k, upper_ref[first_s + k], ids)
        maps = [two_parts(chips_ref[i, k, :WIDTH]) for i in range(chips)]
        before, before_row = eye, nothing
        reached, reached_row = chips_ref[0, k, :WIDTH], chips_ref[0, k, WIDTH : WIDTH + 1]
        for i in range(1, chips):
            before = jnp.where(y == i, reached, before)
            before_row = jnp.where(y == i, reached_row, before_row)
            if i < chips - 1:
                reached = product(maps[i], reached)
            reached_row = applied(maps[i], reached_row) + chips_ref[i, k, WIDTH : WIDTH + 1]
        schur = outlet_ref[first_s + k]
        payload[k] = applied(schur, reached_row)
        after = schur
        upward, after_row = nothing, nothing
        for i in range(chips - 1, -1, -1):
            after = jnp.where(y == i, schur, after)
            after_row = jnp.where(y == i, upward, after_row)
            schur = product(schur, maps[i])
            upward = applied_transposed(maps[i], upward) + chips_ref[i, k, WIDTH + 1 : WIDTH + 2]
        payload[half + k] = upward
        keep(schur_ref, k, schur)
        for side, matrix, vector in ((0, before, before_row), (1, after, after_row)):
            ways_ref[side, k, :WIDTH] = matrix
            ways_ref[side, k, WIDTH:] = jnp.broadcast_to(vector, (8, WIDTH))
    full = jnp.where(row == 2 * half, ids.astype(F32), jnp.concatenate(payload))
    for i in range(spread_ref.shape[0]):
        spread_ref[i] = full


def join_kernel(ways_ref, other_ref, passing_ref, enter_ref, leave_ref, rows_ref):
    half = ways_ref.shape[2]
    c = lax.axis_index("c")
    for s in range(other_ref.shape[1]):
        core, k = s // half, s % half
        before, after = ways_ref[core, 0, k, :WIDTH], ways_ref[core, 1, k, :WIDTH]
        enter, leave = (ways_ref[core, side, k, WIDTH : WIDTH + 1] for side in (0, 1))
        matrix = kept(other_ref, s)
        further = applied(matrix, enter) + passing_ref[s, 0:1]
        nearer = applied_transposed(matrix, leave) + passing_ref[s, 1:2]
        keep(enter_ref, s, jnp.where(c == 1, product(matrix, before), before))
        keep(leave_ref, s, jnp.where(c == 0, product(after, matrix), after))
        rows_ref[s] = jnp.concatenate(
            [
                jnp.where(c == 1, further, enter),
                jnp.where(c == 0, nearer, leave),
                jnp.zeros((6, WIDTH), F32),
            ]
        )


def pick_kernel(ids_ref, table_ref, out_ref, sems):
    dests, owned = out_ref.shape[:2]
    half = owned // 2
    x, c = lax.axis_index("x"), lax.axis_index("c")
    pairs, here = [], []
    for d in range(dests):
        for t in range(owned):
            junction = ids_ref[(c * dests + d) * owned + (t + half) % owned]
            basin = lax.div(junction, owned)
            line = lax.div(basin, dests)
            at = line * owned + (junction - basin * owned)
            here.append(basin - line * dests == x)
            pairs.append((table_ref.at[at], out_ref.at[d, t]))
    copies = [
        pltpu.make_async_copy(source, target, sems.at[i])
        for i, (source, target) in enumerate(pairs)
    ]
    for copy, found, (_, target) in zip(copies, here, pairs):
        pl.when(found)(copy.start)

        @pl.when(jnp.logical_not(found))
        def _(target=target):
            target[...] = jnp.zeros(target.shape, F32)

    for copy, found in zip(copies, here):
        pl.when(found)(copy.wait)


def rule(above, below, half):
    row = lax.broadcasted_iota(jnp.int32, (8, WIDTH), 0)
    return jnp.where(row < half, above, jnp.where(row < 2 * half, below, -2))


def gathered(ids, values, pattern, half):
    total = jnp.sum(jnp.where(ids == pattern[None], values, 0.0), axis=0)
    inflow, outflow = total[0:1], total[half : half + 1]
    for k in range(1, half):
        inflow = inflow + total[k : k + 1]
        outflow = outflow + total[half + k : half + k + 1]
    return inflow, outflow


def source_ids(values, half):
    row = lax.broadcasted_iota(jnp.int32, (8, WIDTH), 0)
    lane = lax.broadcasted_iota(jnp.int32, (8, WIDTH), 1)
    chosen = jnp.where((row == lane) & (row < 2 * half), values[:, 2 * half : 2 * half + 1], 0.0)
    ids = jnp.sum(chosen, axis=2, keepdims=True).astype(jnp.int32)
    return jnp.broadcast_to(ids, values.shape)


def sums_kernel(plane_ref, ids_ref, terms_ref, out_ref, *, half, cores, own):
    ids, values = ids_ref[...], terms_ref[...]
    sides = out_ref.shape[0] // cores
    owned = cores * half
    line = lax.axis_index("z") * sides
    nothing = jnp.zeros((1, WIDTH), F32)
    for d in range(out_ref.shape[0]):
        x, c = d // cores, d % cores
        at = (c * sides + x) * owned
        rows = [nothing] * out_ref.shape[1]
        for k in range(half):
            pattern = rule(plane_ref[at + half + k], plane_ref[at + k], half)
            rows[k], rows[half + k] = gathered(ids, values, pattern, half)
            if own:
                junction = (line + x) * owned + c * half + k
                pattern = rule(junction, junction, half)
                rows[8 + k], rows[8 + half + k] = gathered(ids, values, pattern, half)
        out_ref[d] = jnp.concatenate(rows)


def sums_tiles_kernel(
    plane_ref, ids_ref, terms_ref, ends_hbm, out_ref, tiles_ref, ends_ref, sems, *, half, cores
):
    piece = ends_ref.shape[2]
    (copy,) = fetch([(ends_hbm.at[:, :, :piece], ends_ref)], sems)
    sums_kernel(plane_ref, ids_ref, terms_ref, out_ref, half=half, cores=cores, own=False)
    copy.wait()
    for k in range(tiles_ref.shape[1]):
        keep(tiles_ref, k, jnp.concatenate([ends_ref[i, k] for i in range(ends_ref.shape[0])]))


def summed(parts_ref):
    total = parts_ref[0]
    for i in range(1, parts_ref.shape[0]):
        total = total + parts_ref[i]
    return total


def spread_rows(payload, spread_ref):
    full = jnp.concatenate(payload)
    for i in range(spread_ref.shape[0]):
        spread_ref[i] = full


def step(total, tiles_ref, schur_ref, ends, base, spread_ref):
    half = schur_ref.shape[1]
    payload = [jnp.zeros((1, WIDTH), F32)] * 8
    total = total + ends
    for k in range(half):
        other = half + k
        head = applied(kept(tiles_ref, k), total[k : k + 1])
        relief = applied_transposed(kept(tiles_ref, other), total[other : other + 1])
        schur = kept(schur_ref, k)
        payload[k] = base[k : k + 1] + applied(schur, head)
        payload[other] = base[other : other + 1] + applied_transposed(schur, relief)
    spread_rows(payload, spread_ref)


def at_root(values):
    return jnp.where(lax.axis_index("y") == 0, values, 0.0)


def partial_kernel(
    lower_ref, upper_ref, terms_ref, picked_ref, schur_ref, first_ref,
    ids_ref, rows_ref, base_ref, merged_ref, spread_ref, tile_ref,
):
    half = picked_ref.shape[1] // 2
    piece = picked_ref.shape[2] - 8
    first_s = lax.axis_index("c") * half
    start = pl.multiple_of(lax.axis_index("y") * piece, 8)
    values = terms_ref[...].reshape(-1, 8, WIDTH)
    ids = source_ids(values, half)
    count = ids_ref.shape[0] * 8
    column = pl.multiple_of(lax.axis_index("x") * count, 8)
    ids_ref[...] = source_ids(
        terms_ref[lax.axis_index("c"), pl.ds(column, count)].reshape(ids_ref.shape), half
    )
    merged = picked_ref[0]
    for d in range(1, picked_ref.shape[0]):
        merged = merged + picked_ref[d]
    merged_ref[:, : piece + 8] = merged
    merged_ref[:, piece + 8 :] = jnp.zeros(
        (2 * half, merged_ref.shape[1] - piece - 8, WIDTH), F32
    )
    tile_ref[...] = jnp.zeros(tile_ref.shape, F32)
    base = at_root(first_ref[0])
    base_ref[...] = base
    payload = [jnp.zeros((1, WIDTH), F32)] * 8
    ends = [jnp.zeros((1, WIDTH), F32)] * 8
    for k in range(half):
        pattern = rule(upper_ref[first_s + k], lower_ref[first_s + k], half)
        inflow, outflow = gathered(ids, values, pattern, half)
        ends[k] = merged[k, piece : piece + 1]
        ends[half + k] = merged[half + k, piece + 1 : piece + 2]
        tile_ref[k, pl.ds(start, piece)] = merged[k, :piece]
        tile_ref[half + k, pl.ds(start, piece)] = merged[half + k, :piece]
        head = applied(tile_ref[k], ends[k] + inflow)
        relief = applied_transposed(tile_ref[half + k], ends[half + k] + outflow)
        schur = kept(schur_ref, k)
        payload[k] = base[k : k + 1] + applied(schur, head)
        payload[half + k] = base[half + k : half + k + 1] + applied_transposed(schur, relief)
    rows_ref[...] = at_root(jnp.concatenate(ends))
    spread_rows(payload, spread_ref)


def step_kernel(parts_ref, tiles_ref, schur_ref, rows_ref, base_ref, spread_ref):
    step(summed(parts_ref), tiles_ref, schur_ref, rows_ref[...], base_ref[...], spread_ref)


def last_kernel(
    parts_ref, tiles_ref, rows_ref, inv_ref, residual_ref, cotangent_ref, spread_ref
):
    half = tiles_ref.shape[1] // 2
    c = lax.axis_index("c")
    total = summed(parts_ref)
    ends = total[:8] + rows_ref[...]
    residuals, cotangents = at_root(residual_ref[...]), at_root(cotangent_ref[...])
    out = [jnp.zeros((1, WIDTH), F32)] * 16
    for k in range(half):
        other = half + k
        out[k] = applied(kept(tiles_ref, k), ends[k : k + 1])
        out[other] = applied_transposed(kept(tiles_ref, other), ends[other : other + 1])
        residual = jnp.where(c == 1, residuals[other : other + 1], residuals[k : k + 1])
        cotangent = jnp.where(c == 1, cotangents[other : other + 1], cotangents[k : k + 1])
        out[8 + k] = applied(inv_ref[c * half + k], residual + total[8 + k : 9 + k])
        out[8 + other] = cotangent + total[8 + other : 9 + other]
    spread_rows(out, spread_ref)


def cells_kernel(
    shared_ref, enter_ref, leave_ref, rows_ref, maps_ref, vectors_ref,
    update_ref, sections_ref, adjoint_ref, junction_ref,
):
    members, blocks = update_ref.shape[:2]
    half = members // 2
    shared = []
    for core in range(2):
        total = shared_ref[core]
        for i in range(core + 2, shared_ref.shape[0], 2):
            total = total + shared_ref[i]
        shared.append(total)
    for s in range(members):
        core, k = s // half, s % half
        sections_ref[s : s + 1] = shared[core][8 + k : 9 + k]
        junction_ref[s : s + 1] = shared[core][8 + half + k : 9 + half + k]
        enter = applied(kept(enter_ref, s), shared[core][k : k + 1]) + rows_ref[s, 0:1]
        leave = (
            applied_transposed(kept(leave_ref, s), shared[core][half + k : half + k + 1])
            + rows_ref[s, 1:2]
        )
        rows, back = [], []
        for i in range(blocks):
            rows.append(
                applied((maps_ref[0, s, i], maps_ref[1, s, i]), enter) + vectors_ref[s, i : i + 1]
            )
            if i < blocks - 1:
                suffix = (maps_ref[0, s, blocks + i], maps_ref[1, s, blocks + i])
                change = applied_transposed(suffix, leave)
            else:
                change = leave
            back.append(change + vectors_ref[s, blocks + i : blocks + i + 1])
        update_ref[s] = jnp.concatenate(rows)
        adjoint_ref[s] = jnp.concatenate(back)


def swap(spread, axis):
    return lax.all_to_all(spread, axis, 0, 0, tiled=False)


def over_x(values):
    return swap(jnp.broadcast_to(values[None], (lax.axis_size("x"),) + values.shape), "x")


def exchanged(spread):
    along_x = over_x(swap(spread, "z"))
    return lax.all_gather(along_x.reshape(-1, WIDTH), "c")


def shards(
    reach_residual,
    chain_inv,
    chain_link,
    outlet_link,
    junction_inv,
    junction_residual,
    upper_junction,
    lower_junction,
    cell_cotangent,
    junction_cotangent,
):
    members, blocks, width = reach_residual.shape
    owned = junction_inv.shape[0]
    zs, xs, ys, cs = (lax.axis_size(a) for a in ("z", "x", "y", "c"))
    half = members // cs
    piece = width // ys
    bf16 = jnp.bfloat16
    lower, upper = lower_junction, upper_junction

    part = run(
        table_kernel,
        array(owned, piece + 8, width),
        junction_inv, junction_residual, junction_cotangent,
        where=hbm, limit=60,
        scratch=[
            pltpu.VMEM((owned, width), F32),
            pltpu.VMEM((owned, width), F32),
            pltpu.SemaphoreType.DMA((3,)),
        ],
    )
    table = lax.all_gather(part, "z").reshape(zs * owned, piece + 8, width)

    chain = (members, blocks, width, width)
    maps, vectors, local = run(
        local_kernel,
        [
            array(2, members, 2 * blocks - 1, width, width, dtype=bf16),
            array(members, 8, width),
            array(members, PACK, width),
        ],
        chain_inv, chain_link, reach_residual, cell_cotangent,
        where=hbm, limit=60, flops=2_000_000_000,
        scratch=[
            pltpu.VMEM(chain, F32),
            pltpu.VMEM(chain, F32),
            pltpu.VMEM((members, blocks, width), F32),
            pltpu.VMEM((members, blocks, width), F32),
            pltpu.SemaphoreType.DMA((2 + 2 * members,)),
        ],
    )
    pair = lax.all_gather(local, "c")
    chip, other, other_rows = run(
        pair_kernel,
        [array(half, PACK, width), array(2, members, width, width, dtype=bf16), array(members, 8, width)],
        pair,
    )
    chips = lax.all_gather(chip, "y")
    matrices = array(2, half, width, width, dtype=bf16)
    schur, ways, first = run(
        chain_kernel,
        [matrices, array(2, half, PACK, width), array(zs, 8, width)],
        lower, upper, chips, outlet_link, scalars=2,
    )

    shared_map = array(2, members, width, width, dtype=bf16)
    joined = run(
        join_kernel,
        [shared_map, shared_map, array(members, 8, width)],
        lax.all_gather(ways, "c"), other, other_rows,
    )
    terms, joined = lax.optimization_barrier((exchanged(first), joined))
    plane = lax.dynamic_slice(
        terms.reshape(cs, xs, zs, 8, width),
        (0, 0, lax.axis_index("z"), 2 * half, 0),
        (cs, xs, 1, 1, owned),
    ).reshape(-1).astype(jnp.int32)
    picked = run(
        pick_kernel, array(xs, owned, piece + 8, width), plane, table,
        scalars=1, where=hbm, limit=60, scratch=[pltpu.SemaphoreType.DMA((xs * owned,))],
    )
    ids, rows, base, merged, spread = run(
        partial_kernel,
        [
            array(zs, 8, width, dtype=jnp.int32),
            array(8, width),
            array(8, width),
            array(owned, 3 * piece, width),
            array(zs, 8, width),
        ],
        lower, upper, terms, swap(picked, "x"), schur, first, scalars=2,
        scratch=[pltpu.VMEM((owned, width, width), F32)],
    )
    spread, merged = lax.optimization_barrier((spread, merged))
    ends = lax.all_gather(merged, "y")
    sides = ("x", "c")
    sizes = dict(half=half, cores=cs)
    sums, tiles = run(
        functools.partial(sums_tiles_kernel, **sizes),
        [array(xs * cs, 8, width), array(2, owned, width, width, dtype=bf16)],
        plane, ids, swap(spread, "z"), ends,
        scalars=1, where=[vmem, vmem, hbm], limit=60,
        scratch=[pltpu.VMEM((ys, owned, piece, width), F32), pltpu.SemaphoreType.DMA((1,))],
    )
    for sweep in range(2, SWEEPS):
        spread = run(
            step_kernel, array(zs, 8, width), swap(sums, sides), tiles, schur, rows, base
        )
        final = sweep == SWEEPS - 1
        sums = run(
            functools.partial(sums_kernel, own=final, **sizes),
            array(xs * cs, 16 if final else 8, width),
            plane, ids, swap(spread, "z"), scalars=1,
        )
    shared = run(
        last_kernel, array(ys * cs, 16, width), swap(sums, sides), tiles, rows,
        junction_inv, junction_residual, junction_cotangent,
    )
    cell_update, sections, cell_adjoint, adjoint = run(
        cells_kernel,
        [
            array(members, blocks, width), array(owned, width),
            array(members, blocks, width), array(owned, width),
        ],
        swap(shared, ("y", "c")), *joined, maps, vectors,
    )
    return (cell_update, sections, cell_adjoint, adjoint)


def solution(mesh):
    basins = mesh.shape["basin"]
    grid = Mesh(mesh.devices.reshape(basins // 4, 4, 4, 2), ("z", "x", "y", "c"))
    b, r = ("z", "x"), ("y", "c")
    return jax.shard_map(
        shards,
        mesh=grid,
        in_specs=(
            P(b, r, None),
            P(b, r, None, None),
            P(b, r, None, None),
            P(b, None, None),
            P(b, None, None),
            P(b, None),
            P(b),
            P(b),
            P(b, r, None),
            P(b, None),
        ),
        out_specs=(P(b, r, None), P(b, None), P(b, r, None), P(b, None)),
        check_vma=False,
    )
```

```python
import functools

import jax
import jax.numpy as jnp
from jax import lax
from jax.experimental import pallas as pl
from jax.experimental.pallas import tpu as pltpu
from jax.sharding import Mesh, PartitionSpec as P

SWEEPS = 4
WIDTH = 128
PACK = WIDTH + 8
F32 = jnp.float32

smem = pl.BlockSpec(memory_space=pltpu.SMEM)
vmem = pl.BlockSpec(memory_space=pltpu.VMEM)
hbm = pl.BlockSpec(memory_space=pltpu.HBM)


def array(*shape, dtype=F32):
    return jax.ShapeDtypeStruct(shape, dtype)


def run(kernel, outs, *args, scalars=0, where=vmem, scratch=(), limit=40, flops=0):
    single = not isinstance(outs, list)
    shapes = [outs] if single else outs
    result = pl.pallas_call(
        kernel,
        out_shape=shapes,
        in_specs=[smem] * scalars
        + (where if isinstance(where, list) else [where] * (len(args) - scalars)),
        out_specs=[vmem] * len(shapes),
        scratch_shapes=scratch,
        compiler_params=pltpu.CompilerParams(vmem_limit_bytes=limit * 1024 * 1024),
        cost_estimate=pl.CostEstimate(flops=flops, bytes_accessed=flops // 100, transcendentals=0) if flops else None,
    )(*args)
    return result[0] if single else result


def two_parts(a):
    high = a.astype(jnp.bfloat16)
    return high, (a - high.astype(F32)).astype(jnp.bfloat16)


def dot(a, b, transposed=False):
    dims = (((1,), (1 if transposed else 0,)), ((), ()))
    return lax.dot_general(a, b, dims, preferred_element_type=F32)


def parts_of(a):
    return a if isinstance(a, tuple) else two_parts(a)


def product(a, b):
    (ah, al), (bh, bl) = parts_of(a), parts_of(b)
    return dot(ah, bh) + (dot(ah, bl) + dot(al, bh))


def along(vector, matrix, transposed):
    vh, vl = two_parts(vector)
    mh, ml = parts_of(matrix)
    both = dot(jnp.concatenate([vh, vl]), mh, transposed)
    return both[0:1] + (both[1:2] + dot(vh, ml, transposed))


def applied(matrix, row):
    return along(row, matrix, True)


def applied_transposed(matrix, row):
    return along(row, matrix, False)


def fetch(pairs, sems):
    copies = [pltpu.make_async_copy(src, dst, sems.at[i]) for i, (src, dst) in enumerate(pairs)]
    for copy in copies:
        copy.start()
    return copies


def table_kernel(inv_ref, residual_ref, cotangent_ref, out_ref, residual, cotangent, sems):
    piece = out_ref.shape[1] - 8
    start = pl.multiple_of(lax.axis_index("y") * piece, 8)
    copies = fetch(
        [
            (inv_ref.at[:, pl.ds(start, piece)], out_ref.at[:, :piece]),
            (residual_ref, residual),
            (cotangent_ref, cotangent),
        ],
        sems,
    )
    for copy in copies[1:]:
        copy.wait()
    for k in range(out_ref.shape[0]):
        out_ref[k, piece:] = jnp.concatenate(
            [residual[k : k + 1], cotangent[k : k + 1], jnp.zeros((6, WIDTH), F32)]
        )
    copies[0].wait()


def local_kernel(
    inv_hbm, link_hbm, residual_hbm, cotangent_hbm, maps_ref, vectors_ref, out_ref,
    inv_ref, link_ref, residual_ref, cotangent_ref, sems,
):
    members, blocks = inv_ref.shape[:2]
    pairs = [(residual_hbm, residual_ref), (cotangent_hbm, cotangent_ref)]
    for s in range(members):
        pairs += [(inv_hbm.at[s], inv_ref.at[s]), (link_hbm.at[s], link_ref.at[s])]
    copies = fetch(pairs, sems)
    copies[0].wait()
    copies[1].wait()
    for s in range(members):
        copies[2 + 2 * s].wait()
        copies[3 + 2 * s].wait()
        m, f = [], []
        for i in range(blocks):
            inverse = two_parts(inv_ref[s, i])
            m.append(two_parts(product(inverse, two_parts(link_ref[s, i]))))
            f.append(applied(inverse, residual_ref[s, i : i + 1]))
        rows = [jnp.zeros((1, WIDTH), F32)] * 8
        total, vector = m[0], f[0]
        for i in range(blocks):
            if i:
                result = product(m[i], total)
                total = two_parts(result)
                vector = applied(m[i], vector) + f[i]
            maps_ref[0, s, i], maps_ref[1, s, i] = total
            rows[i] = vector
        back = cotangent_ref[s, blocks - 1 : blocks]
        rows[2 * blocks - 1] = back
        suffix = None
        for i in range(blocks - 2, -1, -1):
            back = cotangent_ref[s, i : i + 1] + applied_transposed(m[i + 1], back)
            rows[blocks + i] = back
            suffix = m[i + 1] if suffix is None else two_parts(product(suffix, m[i + 1]))
            maps_ref[0, s, blocks + i], maps_ref[1, s, blocks + i] = suffix
        vectors_ref[s] = jnp.concatenate(rows)
        out_ref[s, :WIDTH] = result
        out_ref[s, WIDTH:] = jnp.concatenate(
            [vector, applied_transposed(m[0], back), jnp.zeros((6, WIDTH), F32)]
        )


def pair_kernel(pair_ref, out_ref, other_ref, rows_ref):
    half = out_ref.shape[0]
    c = lax.axis_index("c")
    first_s = c * half
    for k in range(half):
        first, second = pair_ref[0, first_s + k], pair_ref[1, first_s + k]
        one, two = two_parts(first[:WIDTH]), two_parts(second[:WIDTH])
        out_ref[k, :WIDTH] = product(two, one)
        out_ref[k, WIDTH:] = jnp.concatenate(
            [
                applied(two, first[WIDTH : WIDTH + 1]) + second[WIDTH : WIDTH + 1],
                applied_transposed(one, second[WIDTH + 1 : WIDTH + 2])
                + first[WIDTH + 1 : WIDTH + 2],
                jnp.zeros((6, WIDTH), F32),
            ]
        )
    for s in range(other_ref.shape[1]):
        keep(other_ref, s, pair_ref[1 - c, s, :WIDTH])
        rows_ref[s] = pair_ref[1 - c, s, WIDTH:]


def keep(ref, k, matrix):
    ref[0, k], ref[1, k] = two_parts(matrix)


def kept(ref, k):
    return ref[0, k], ref[1, k]


def chain_kernel(lower_ref, upper_ref, chips_ref, outlet_ref, schur_ref, ways_ref, spread_ref):
    chips, half = chips_ref.shape[:2]
    first_s = lax.axis_index("c") * half
    y = lax.axis_index("y")
    row = lax.broadcasted_iota(jnp.int32, (8, WIDTH), 0)
    lane = lax.broadcasted_iota(jnp.int32, (8, WIDTH), 1)
    eye = (
        lax.broadcasted_iota(jnp.int32, (WIDTH, WIDTH), 0)
        == lax.broadcasted_iota(jnp.int32, (WIDTH, WIDTH), 1)
    ).astype(F32)
    nothing = jnp.zeros((1, WIDTH), F32)
    ids = jnp.zeros((8, WIDTH), jnp.int32)
    payload = [nothing] * 8
    for k in range(half):
        ids = jnp.where(lane == k, lower_ref[first_s + k], ids)
        ids = jnp.where(lane == half + k, upper_ref[first_s + k], ids)
        maps = [two_parts(chips_ref[i, k, :WIDTH]) for i in range(chips)]
        before, before_row = eye, nothing
        reached, reached_row = chips_ref[0, k, :WIDTH], chips_ref[0, k, WIDTH : WIDTH + 1]
        for i in range(1, chips):
            before = jnp.where(y == i, reached, before)
            before_row = jnp.where(y == i, reached_row, before_row)
            if i < chips - 1:
                reached = product(maps[i], reached)
            reached_row = applied(maps[i], reached_row) + chips_ref[i, k, WIDTH : WIDTH + 1]
        schur = outlet_ref[first_s + k]
        payload[k] = applied(schur, reached_row)
        after = schur
        upward, after_row = nothing, nothing
        for i in range(chips - 1, -1, -1):
            after = jnp.where(y == i, schur, after)
            after_row = jnp.where(y == i, upward, after_row)
            schur = product(schur, maps[i])
            upward = applied_transposed(maps[i], upward) + chips_ref[i, k, WIDTH + 1 : WIDTH + 2]
        payload[half + k] = upward
        keep(schur_ref, k, schur)
        for side, matrix, vector in ((0, before, before_row), (1, after, after_row)):
            ways_ref[side, k, :WIDTH] = matrix
            ways_ref[side, k, WIDTH:] = jnp.broadcast_to(vector, (8, WIDTH))
    full = jnp.where(row == 2 * half, ids.astype(F32), jnp.concatenate(payload))
    for i in range(spread_ref.shape[0]):
        spread_ref[i] = full


def join_kernel(ways_ref, other_ref, passing_ref, enter_ref, leave_ref, rows_ref):
    half = ways_ref.shape[2]
    c = lax.axis_index("c")
    for s in range(other_ref.shape[1]):
        core, k = s // half, s % half
        before, after = ways_ref[core, 0, k, :WIDTH], ways_ref[core, 1, k, :WIDTH]
        enter, leave = (ways_ref[core, side, k, WIDTH : WIDTH + 1] for side in (0, 1))
        matrix = kept(other_ref, s)
        further = applied(matrix, enter) + passing_ref[s, 0:1]
        nearer = applied_transposed(matrix, leave) + passing_ref[s, 1:2]
        keep(enter_ref, s, jnp.where(c == 1, product(matrix, before), before))
        keep(leave_ref, s, jnp.where(c == 0, product(after, matrix), after))
        rows_ref[s] = jnp.concatenate(
            [
                jnp.where(c == 1, further, enter),
                jnp.where(c == 0, nearer, leave),
                jnp.zeros((6, WIDTH), F32),
            ]
        )


def pick_kernel(ids_ref, table_ref, out_ref):
    dests, owned = out_ref.shape[:2]
    half = owned // 2
    x, c = lax.axis_index("x"), lax.axis_index("c")
    for d in range(dests):
        for t in range(owned):
            junction = ids_ref[(c * dests + d) * owned + (t + half) % owned]
            basin = lax.div(junction, owned)
            line = lax.div(basin, dests)
            at = line * owned + (junction - basin * owned)
            here = basin - line * dests == x
            out_ref[d, t] = jnp.where(here, table_ref[at], 0.0)


def rule(above, below, half):
    row = lax.broadcasted_iota(jnp.int32, (8, WIDTH), 0)
    return jnp.where(row < half, above, jnp.where(row < 2 * half, below, -2))


def gathered(ids, values, pattern, half):
    total = jnp.sum(jnp.where(ids == pattern[None], values, 0.0), axis=0)
    inflow, outflow = total[0:1], total[half : half + 1]
    for k in range(1, half):
        inflow = inflow + total[k : k + 1]
        outflow = outflow + total[half + k : half + k + 1]
    return inflow, outflow


def source_ids(values, half):
    row = lax.broadcasted_iota(jnp.int32, (8, WIDTH), 0)
    lane = lax.broadcasted_iota(jnp.int32, (8, WIDTH), 1)
    chosen = jnp.where((row == lane) & (row < 2 * half), values[:, 2 * half : 2 * half + 1], 0.0)
    ids = jnp.sum(chosen, axis=2, keepdims=True).astype(jnp.int32)
    return jnp.broadcast_to(ids, values.shape)


def sums_kernel(plane_ref, ids_ref, terms_ref, out_ref, *, half, cores, own):
    ids, values = ids_ref[...], terms_ref[...]
    sides = out_ref.shape[0] // cores
    owned = cores * half
    line = lax.axis_index("z") * sides
    nothing = jnp.zeros((1, WIDTH), F32)
    for d in range(out_ref.shape[0]):
        x, c = d // cores, d % cores
        at = (c * sides + x) * owned
        rows = [nothing] * out_ref.shape[1]
        for k in range(half):
            pattern = rule(plane_ref[at + half + k], plane_ref[at + k], half)
            rows[k], rows[half + k] = gathered(ids, values, pattern, half)
            if own:
                junction = (line + x) * owned + c * half + k
                pattern = rule(junction, junction, half)
                rows[8 + k], rows[8 + half + k] = gathered(ids, values, pattern, half)
        out_ref[d] = jnp.concatenate(rows)


def summed(parts_ref):
    total = parts_ref[0]
    for i in range(1, parts_ref.shape[0]):
        total = total + parts_ref[i]
    return total


def spread_rows(payload, spread_ref):
    full = jnp.concatenate(payload)
    for i in range(spread_ref.shape[0]):
        spread_ref[i] = full


def step(total, tiles_ref, schur_ref, ends, base, spread_ref):
    half = schur_ref.shape[1]
    payload = [jnp.zeros((1, WIDTH), F32)] * 8
    total = total + ends
    for k in range(half):
        other = half + k
        head = applied(kept(tiles_ref, k), total[k : k + 1])
        relief = applied_transposed(kept(tiles_ref, other), total[other : other + 1])
        schur = kept(schur_ref, k)
        payload[k] = base[k : k + 1] + applied(schur, head)
        payload[other] = base[other : other + 1] + applied_transposed(schur, relief)
    spread_rows(payload, spread_ref)


def at_root(values):
    return jnp.where(lax.axis_index("y") == 0, values, 0.0)


def flows_kernel(lower_ref, upper_ref, terms_ref, ids_ref, flows_ref):
    count = ids_ref.shape[0]
    half = flows_ref.shape[0] // 2 - 1
    first_s = lax.axis_index("c") * half
    values = terms_ref[...].reshape(-1, 8, WIDTH)
    ids = source_ids(values, half)
    column = pl.multiple_of(lax.axis_index("x") * count * 8, 8)
    ids_ref[...] = source_ids(
        terms_ref[lax.axis_index("c"), pl.ds(column, count * 8)].reshape(ids_ref.shape), half
    )
    rows = [jnp.zeros((1, WIDTH), F32)] * 8
    for k in range(half):
        pattern = rule(upper_ref[first_s + k], lower_ref[first_s + k], half)
        rows[k], rows[half + k] = gathered(ids, values, pattern, half)
    flows_ref[...] = jnp.concatenate(rows)


def partial_kernel(
    flows_ref, picked_ref, schur_ref, first_ref, rows_ref, base_ref, merged_ref, spread_ref, tile_ref
):
    half = picked_ref.shape[1] // 2
    piece = picked_ref.shape[2] - 8
    start = pl.multiple_of(lax.axis_index("y") * piece, 8)
    merged = picked_ref[0]
    for d in range(1, picked_ref.shape[0]):
        merged = merged + picked_ref[d]
    merged_ref[:, : piece + 8] = merged
    merged_ref[:, piece + 8 :] = jnp.zeros(
        (2 * half, merged_ref.shape[1] - piece - 8, WIDTH), F32
    )
    tile_ref[...] = jnp.zeros(tile_ref.shape, F32)
    base = at_root(first_ref[0])
    base_ref[...] = base
    payload = [jnp.zeros((1, WIDTH), F32)] * 8
    ends = [jnp.zeros((1, WIDTH), F32)] * 8
    for k in range(half):
        other = half + k
        ends[k] = merged[k, piece : piece + 1]
        ends[other] = merged[other, piece + 1 : piece + 2]
        tile_ref[k, pl.ds(start, piece)] = merged[k, :piece]
        tile_ref[other, pl.ds(start, piece)] = merged[other, :piece]
        head = applied(tile_ref[k], ends[k] + flows_ref[k : k + 1])
        relief = applied_transposed(tile_ref[other], ends[other] + flows_ref[other : other + 1])
        schur = kept(schur_ref, k)
        payload[k] = base[k : k + 1] + applied(schur, head)
        payload[other] = base[other : other + 1] + applied_transposed(schur, relief)
    rows_ref[...] = at_root(jnp.concatenate(ends))
    spread_rows(payload, spread_ref)


def tiles_step_kernel(parts_ref, ends_ref, schur_ref, rows_ref, base_ref, tiles_ref, spread_ref):
    piece = WIDTH // ends_ref.shape[0]
    for k in range(tiles_ref.shape[1]):
        keep(tiles_ref, k, jnp.concatenate([ends_ref[i, k, :piece] for i in range(ends_ref.shape[0])]))
    step_kernel(parts_ref, tiles_ref, schur_ref, rows_ref, base_ref, spread_ref)


def step_kernel(parts_ref, tiles_ref, schur_ref, rows_ref, base_ref, spread_ref):
    step(summed(parts_ref), tiles_ref, schur_ref, rows_ref[...], base_ref[...], spread_ref)


def last_kernel(
    parts_ref, tiles_ref, rows_ref, inv_ref, residual_ref, cotangent_ref, spread_ref
):
    half = tiles_ref.shape[1] // 2
    c = lax.axis_index("c")
    total = summed(parts_ref)
    ends = total[:8] + rows_ref[...]
    residuals, cotangents = at_root(residual_ref[...]), at_root(cotangent_ref[...])
    out = [jnp.zeros((1, WIDTH), F32)] * 16
    for k in range(half):
        other = half + k
        out[k] = applied(kept(tiles_ref, k), ends[k : k + 1])
        out[other] = applied_transposed(kept(tiles_ref, other), ends[other : other + 1])
        residual = jnp.where(c == 1, residuals[other : other + 1], residuals[k : k + 1])
        cotangent = jnp.where(c == 1, cotangents[other : other + 1], cotangents[k : k + 1])
        out[8 + k] = applied(inv_ref[c * half + k], residual + total[8 + k : 9 + k])
        out[8 + other] = cotangent + total[8 + other : 9 + other]
    spread_rows(out, spread_ref)


def cells_kernel(
    shared_ref, enter_ref, leave_ref, rows_ref, maps_ref, vectors_ref,
    update_ref, sections_ref, adjoint_ref, junction_ref,
):
    members, blocks = update_ref.shape[:2]
    half = members // 2
    shared = []
    for core in range(2):
        total = shared_ref[core]
        for i in range(core + 2, shared_ref.shape[0], 2):
            total = total + shared_ref[i]
        shared.append(total)
    for s in range(members):
        core, k = s // half, s % half
        sections_ref[s : s + 1] = shared[core][8 + k : 9 + k]
        junction_ref[s : s + 1] = shared[core][8 + half + k : 9 + half + k]
        enter = applied(kept(enter_ref, s), shared[core][k : k + 1]) + rows_ref[s, 0:1]
        leave = (
            applied_transposed(kept(leave_ref, s), shared[core][half + k : half + k + 1])
            + rows_ref[s, 1:2]
        )
        rows, back = [], []
        for i in range(blocks):
            rows.append(
                applied((maps_ref[0, s, i], maps_ref[1, s, i]), enter) + vectors_ref[s, i : i + 1]
            )
            if i < blocks - 1:
                suffix = (maps_ref[0, s, blocks + i], maps_ref[1, s, blocks + i])
                change = applied_transposed(suffix, leave)
            else:
                change = leave
            back.append(change + vectors_ref[s, blocks + i : blocks + i + 1])
        update_ref[s] = jnp.concatenate(rows)
        adjoint_ref[s] = jnp.concatenate(back)


def swap(spread, axis):
    return lax.all_to_all(spread, axis, 0, 0, tiled=False)


def over_x(values):
    return swap(jnp.broadcast_to(values[None], (lax.axis_size("x"),) + values.shape), "x")


def exchanged(spread):
    along_x = over_x(swap(spread, "z"))
    return lax.all_gather(along_x.reshape(-1, WIDTH), "c")


def shards(
    reach_residual,
    chain_inv,
    chain_link,
    outlet_link,
    junction_inv,
    junction_residual,
    upper_junction,
    lower_junction,
    cell_cotangent,
    junction_cotangent,
):
    members, blocks, width = reach_residual.shape
    owned = junction_inv.shape[0]
    zs, xs, ys, cs = (lax.axis_size(a) for a in ("z", "x", "y", "c"))
    half = members // cs
    piece = width // ys
    bf16 = jnp.bfloat16
    lower, upper = lower_junction, upper_junction

    part = run(
        table_kernel,
        array(owned, piece + 8, width),
        junction_inv, junction_residual, junction_cotangent,
        where=hbm, limit=60,
        scratch=[
            pltpu.VMEM((owned, width), F32),
            pltpu.VMEM((owned, width), F32),
            pltpu.SemaphoreType.DMA((3,)),
        ],
    )
    table = lax.all_gather(part, "z").reshape(zs * owned, piece + 8, width)

    chain = (members, blocks, width, width)
    maps, vectors, local = run(
        local_kernel,
        [
            array(2, members, 2 * blocks - 1, width, width, dtype=bf16),
            array(members, 8, width),
            array(members, PACK, width),
        ],
        chain_inv, chain_link, reach_residual, cell_cotangent,
        where=hbm, limit=60, flops=2_000_000_000,
        scratch=[
            pltpu.VMEM(chain, F32),
            pltpu.VMEM(chain, F32),
            pltpu.VMEM((members, blocks, width), F32),
            pltpu.VMEM((members, blocks, width), F32),
            pltpu.SemaphoreType.DMA((2 + 2 * members,)),
        ],
    )
    pair = lax.all_gather(local, "c")
    chip, other, other_rows = run(
        pair_kernel,
        [array(half, PACK, width), array(2, members, width, width, dtype=bf16), array(members, 8, width)],
        pair,
    )
    chips = lax.all_gather(chip, "y")
    matrices = array(2, half, width, width, dtype=bf16)
    schur, ways, first = run(
        chain_kernel,
        [matrices, array(2, half, PACK, width), array(zs, 8, width)],
        lower, upper, chips, outlet_link, scalars=2,
    )

    shared_map = array(2, members, width, width, dtype=bf16)
    joined = run(
        join_kernel,
        [shared_map, shared_map, array(members, 8, width)],
        lax.all_gather(ways, "c"), other, other_rows,
    )
    terms, joined = lax.optimization_barrier((exchanged(first), joined))
    plane = lax.dynamic_slice(
        terms.reshape(cs, xs, zs, 8, width),
        (0, 0, lax.axis_index("z"), 2 * half, 0),
        (cs, xs, 1, 1, owned),
    ).reshape(-1).astype(jnp.int32)
    ids, flows = run(
        flows_kernel,
        [array(zs, 8, width, dtype=jnp.int32), array(8, width)],
        lower, upper, terms, scalars=2,
    )
    plane, flows = lax.optimization_barrier((plane, flows))
    picked = run(pick_kernel, array(xs, owned, piece + 8, width), plane, table, scalars=1)
    rows, base, merged, spread = run(
        partial_kernel,
        [
            array(8, width),
            array(8, width),
            array(owned, 2 * piece + 24, width),
            array(zs, 8, width),
        ],
        flows, swap(picked, "x"), schur, first,
        scratch=[pltpu.VMEM((owned, width, width), F32)],
    )
    spread, merged = lax.optimization_barrier((spread, merged))
    ends = lax.all_gather(merged, "y")
    sides = ("x", "c")

    def sums(spread, own):
        kernel = functools.partial(sums_kernel, half=half, cores=cs, own=own)
        shape = array(xs * cs, 16 if own else 8, width)
        return swap(run(kernel, shape, plane, ids, swap(spread, "z"), scalars=1), sides)

    tiles, spread = run(
        tiles_step_kernel,
        [array(2, owned, width, width, dtype=bf16), array(zs, 8, width)],
        sums(spread, False), ends, schur, rows, base,
    )
    for sweep in range(3, SWEEPS):
        spread = run(
            step_kernel, array(zs, 8, width), sums(spread, False), tiles, schur, rows, base
        )
    shared = run(
        last_kernel, array(ys * cs, 16, width), sums(spread, True), tiles, rows,
        junction_inv, junction_residual, junction_cotangent,
    )
    cell_update, sections, cell_adjoint, adjoint = run(
        cells_kernel,
        [
            array(members, blocks, width), array(owned, width),
            array(members, blocks, width), array(owned, width),
        ],
        swap(shared, ("y", "c")), *joined, maps, vectors,
    )
    return (cell_update, sections, cell_adjoint, adjoint)


def solution(mesh):
    basins = mesh.shape["basin"]
    grid = Mesh(mesh.devices.reshape(basins // 4, 4, 4, 2), ("z", "x", "y", "c"))
    b, r = ("z", "x"), ("y", "c")
    return jax.shard_map(
        shards,
        mesh=grid,
        in_specs=(
            P(b, r, None),
            P(b, r, None, None),
            P(b, r, None, None),
            P(b, None, None),
            P(b, None, None),
            P(b, None),
            P(b),
            P(b),
            P(b, r, None),
            P(b, None),
        ),
        out_specs=(P(b, r, None), P(b, None), P(b, r, None), P(b, None)),
        check_vma=False,
    )
```

```python
import functools

import jax
import jax.numpy as jnp
from jax import lax
from jax.experimental import pallas as pl
from jax.experimental.pallas import tpu as pltpu
from jax.sharding import Mesh, PartitionSpec as P

SWEEPS = 4
WIDTH = 128
PACK = WIDTH + 8
F32 = jnp.float32

smem = pl.BlockSpec(memory_space=pltpu.SMEM)
vmem = pl.BlockSpec(memory_space=pltpu.VMEM)
hbm = pl.BlockSpec(memory_space=pltpu.HBM)


def array(*shape, dtype=F32):
    return jax.ShapeDtypeStruct(shape, dtype)


def run(kernel, outs, *args, scalars=0, where=vmem, scratch=(), limit=40, flops=0):
    single = not isinstance(outs, list)
    shapes = [outs] if single else outs
    result = pl.pallas_call(
        kernel,
        out_shape=shapes,
        in_specs=[smem] * scalars + [where] * (len(args) - scalars),
        out_specs=[vmem] * len(shapes),
        scratch_shapes=scratch,
        compiler_params=pltpu.CompilerParams(vmem_limit_bytes=limit * 1024 * 1024),
        cost_estimate=pl.CostEstimate(flops=flops, bytes_accessed=flops // 100, transcendentals=0) if flops else None,
    )(*args)
    return result[0] if single else result


def two_parts(a):
    high = a.astype(jnp.bfloat16)
    return high, (a - high.astype(F32)).astype(jnp.bfloat16)


def dot(a, b, transposed=False):
    dims = (((1,), (1 if transposed else 0,)), ((), ()))
    return lax.dot_general(a, b, dims, preferred_element_type=F32)


def parts_of(a):
    return a if isinstance(a, tuple) else two_parts(a)


def product(a, b):
    (ah, al), (bh, bl) = parts_of(a), parts_of(b)
    return dot(ah, bh) + (dot(ah, bl) + dot(al, bh))


def along(vector, matrix, transposed):
    vh, vl = two_parts(vector)
    mh, ml = parts_of(matrix)
    both = dot(jnp.concatenate([vh, vl]), mh, transposed)
    return both[0:1] + (both[1:2] + dot(vh, ml, transposed))


def applied(matrix, row):
    return along(row, matrix, True)


def applied_transposed(matrix, row):
    return along(row, matrix, False)


def fetch(pairs, sems):
    copies = [pltpu.make_async_copy(src, dst, sems.at[i]) for i, (src, dst) in enumerate(pairs)]
    for copy in copies:
        copy.start()
    return copies


def table_kernel(inv_ref, residual_ref, cotangent_ref, out_ref, residual, cotangent, sems):
    piece = out_ref.shape[1] - 8
    start = pl.multiple_of(lax.axis_index("y") * piece, 8)
    copies = fetch(
        [
            (inv_ref.at[:, pl.ds(start, piece)], out_ref.at[:, :piece]),
            (residual_ref, residual),
            (cotangent_ref, cotangent),
        ],
        sems,
    )
    for copy in copies[1:]:
        copy.wait()
    for k in range(out_ref.shape[0]):
        out_ref[k, piece:] = jnp.concatenate(
            [residual[k : k + 1], cotangent[k : k + 1], jnp.zeros((6, WIDTH), F32)]
        )
    copies[0].wait()


def local_kernel(
    inv_hbm, link_hbm, residual_hbm, cotangent_hbm, maps_ref, vectors_ref, out_ref,
    inv_ref, link_ref, residual_ref, cotangent_ref, sems,
):
    members, blocks = inv_ref.shape[:2]
    pairs = [(residual_hbm, residual_ref), (cotangent_hbm, cotangent_ref)]
    for s in range(members):
        pairs += [(inv_hbm.at[s], inv_ref.at[s]), (link_hbm.at[s], link_ref.at[s])]
    copies = fetch(pairs, sems)
    copies[0].wait()
    copies[1].wait()
    for s in range(members):
        copies[2 + 2 * s].wait()
        copies[3 + 2 * s].wait()
        m, f = [], []
        for i in range(blocks):
            inverse = two_parts(inv_ref[s, i])
            m.append(two_parts(product(inverse, two_parts(link_ref[s, i]))))
            f.append(applied(inverse, residual_ref[s, i : i + 1]))
        rows = [jnp.zeros((1, WIDTH), F32)] * 8
        total, vector = m[0], f[0]
        for i in range(blocks):
            if i:
                result = product(m[i], total)
                total = two_parts(result)
                vector = applied(m[i], vector) + f[i]
            maps_ref[0, s, i], maps_ref[1, s, i] = total
            rows[i] = vector
        back = cotangent_ref[s, blocks - 1 : blocks]
        rows[2 * blocks - 1] = back
        suffix = None
        for i in range(blocks - 2, -1, -1):
            back = cotangent_ref[s, i : i + 1] + applied_transposed(m[i + 1], back)
            rows[blocks + i] = back
            suffix = m[i + 1] if suffix is None else two_parts(product(suffix, m[i + 1]))
            maps_ref[0, s, blocks + i], maps_ref[1, s, blocks + i] = suffix
        vectors_ref[s] = jnp.concatenate(rows)
        out_ref[s, :WIDTH] = result
        out_ref[s, WIDTH:] = jnp.concatenate(
            [vector, applied_transposed(m[0], back), jnp.zeros((6, WIDTH), F32)]
        )


def pair_kernel(pair_ref, out_ref, other_ref, rows_ref):
    half = out_ref.shape[0]
    c = lax.axis_index("c")
    first_s = c * half
    for k in range(half):
        first, second = pair_ref[0, first_s + k], pair_ref[1, first_s + k]
        one, two = two_parts(first[:WIDTH]), two_parts(second[:WIDTH])
        out_ref[k, :WIDTH] = product(two, one)
        out_ref[k, WIDTH:] = jnp.concatenate(
            [
                applied(two, first[WIDTH : WIDTH + 1]) + second[WIDTH : WIDTH + 1],
                applied_transposed(one, second[WIDTH + 1 : WIDTH + 2])
                + first[WIDTH + 1 : WIDTH + 2],
                jnp.zeros((6, WIDTH), F32),
            ]
        )
    for s in range(other_ref.shape[1]):
        keep(other_ref, s, pair_ref[1 - c, s, :WIDTH])
        rows_ref[s] = pair_ref[1 - c, s, WIDTH:]


def keep(ref, k, matrix):
    ref[0, k], ref[1, k] = two_parts(matrix)


def kept(ref, k):
    return ref[0, k], ref[1, k]


def chain_kernel(lower_ref, upper_ref, chips_ref, outlet_ref, schur_ref, before_ref, after_ref, rows_ref, spread_ref):
    chips, half = chips_ref.shape[:2]
    first_s = lax.axis_index("c") * half
    y = lax.axis_index("y")
    row = lax.broadcasted_iota(jnp.int32, (8, WIDTH), 0)
    lane = lax.broadcasted_iota(jnp.int32, (8, WIDTH), 1)
    eye = (
        lax.broadcasted_iota(jnp.int32, (WIDTH, WIDTH), 0)
        == lax.broadcasted_iota(jnp.int32, (WIDTH, WIDTH), 1)
    ).astype(F32)
    nothing = jnp.zeros((1, WIDTH), F32)
    ids = jnp.zeros((8, WIDTH), jnp.int32)
    payload = [nothing] * 8
    for k in range(half):
        ids = jnp.where(lane == k, lower_ref[first_s + k], ids)
        ids = jnp.where(lane == half + k, upper_ref[first_s + k], ids)
        maps = [two_parts(chips_ref[i, k, :WIDTH]) for i in range(chips)]
        before, before_row = eye, nothing
        reached, reached_row = chips_ref[0, k, :WIDTH], chips_ref[0, k, WIDTH : WIDTH + 1]
        for i in range(1, chips):
            before = jnp.where(y == i, reached, before)
            before_row = jnp.where(y == i, reached_row, before_row)
            if i < chips - 1:
                reached = product(maps[i], reached)
            reached_row = applied(maps[i], reached_row) + chips_ref[i, k, WIDTH : WIDTH + 1]
        schur = outlet_ref[first_s + k]
        payload[k] = applied(schur, reached_row)
        after = schur
        upward, after_row = nothing, nothing
        for i in range(chips - 1, -1, -1):
            after = jnp.where(y == i, schur, after)
            after_row = jnp.where(y == i, upward, after_row)
            schur = product(schur, maps[i])
            upward = applied_transposed(maps[i], upward) + chips_ref[i, k, WIDTH + 1 : WIDTH + 2]
        payload[half + k] = upward
        keep(schur_ref, k, schur)
        keep(before_ref, k, before)
        keep(after_ref, k, after)
        rows_ref[k : k + 1] = before_row
        rows_ref[half + k : half + k + 1] = after_row
    rows_ref[2 * half :] = jnp.zeros((2, WIDTH), F32)
    full = jnp.where(row == 2 * half, ids.astype(F32), jnp.concatenate(payload))
    for i in range(spread_ref.shape[0]):
        spread_ref[i] = full


def pick_kernel(ids_ref, table_ref, out_ref):
    dests, owned = out_ref.shape[:2]
    half = owned // 2
    x, c = lax.axis_index("x"), lax.axis_index("c")
    for d in range(dests):
        for t in range(owned):
            junction = ids_ref[(c * dests + d) * owned + (t + half) % owned]
            basin = lax.div(junction, owned)
            line = lax.div(basin, dests)
            at = line * owned + (junction - basin * owned)
            here = basin - line * dests == x
            out_ref[d, t] = jnp.where(here, table_ref[at], 0.0)


def rule(above, below, half):
    row = lax.broadcasted_iota(jnp.int32, (8, WIDTH), 0)
    return jnp.where(row < half, above, jnp.where(row < 2 * half, below, -2))


def gathered(ids, values, pattern, half):
    total = jnp.sum(jnp.where(ids == pattern[None], values, 0.0), axis=0)
    inflow, outflow = total[0:1], total[half : half + 1]
    for k in range(1, half):
        inflow = inflow + total[k : k + 1]
        outflow = outflow + total[half + k : half + k + 1]
    return inflow, outflow


def source_ids(values, half):
    row = lax.broadcasted_iota(jnp.int32, (8, WIDTH), 0)
    lane = lax.broadcasted_iota(jnp.int32, (8, WIDTH), 1)
    chosen = jnp.where((row == lane) & (row < 2 * half), values[:, 2 * half : 2 * half + 1], 0.0)
    ids = jnp.sum(chosen, axis=2, keepdims=True).astype(jnp.int32)
    return jnp.broadcast_to(ids, values.shape)


def sums_kernel(plane_ref, ids_ref, terms_ref, out_ref, *, half, cores, own):
    ids, values = ids_ref[...], terms_ref[...]
    sides = out_ref.shape[0] // cores
    owned = cores * half
    line = lax.axis_index("z") * sides
    nothing = jnp.zeros((1, WIDTH), F32)
    for d in range(out_ref.shape[0]):
        x, c = d // cores, d % cores
        at = (c * sides + x) * owned
        rows = [nothing] * out_ref.shape[1]
        for k in range(half):
            pattern = rule(plane_ref[at + half + k], plane_ref[at + k], half)
            rows[k], rows[half + k] = gathered(ids, values, pattern, half)
            if own:
                junction = (line + x) * owned + c * half + k
                pattern = rule(junction, junction, half)
                rows[8 + k], rows[8 + half + k] = gathered(ids, values, pattern, half)
        out_ref[d] = jnp.concatenate(rows)


def summed(parts_ref):
    total = parts_ref[0]
    for i in range(1, parts_ref.shape[0]):
        total = total + parts_ref[i]
    return total


def spread_rows(payload, spread_ref):
    full = jnp.concatenate(payload)
    for i in range(spread_ref.shape[0]):
        spread_ref[i] = full


def step(total, tiles_ref, schur_ref, ends, base, spread_ref):
    half = schur_ref.shape[1]
    payload = [jnp.zeros((1, WIDTH), F32)] * 8
    total = total + ends
    for k in range(half):
        other = half + k
        head, relief = total[k : k + 1], total[other : other + 1]
        if tiles_ref is not None:
            head = applied(kept(tiles_ref, k), head)
            relief = applied_transposed(kept(tiles_ref, other), relief)
        schur = kept(schur_ref, k)
        payload[k] = base[k : k + 1] + applied(schur, head)
        payload[other] = base[other : other + 1] + applied_transposed(schur, relief)
    spread_rows(payload, spread_ref)


def flows_kernel(lower_ref, upper_ref, terms_ref, ids_ref, flows_ref):
    count = ids_ref.shape[0]
    half = flows_ref.shape[0] // 2 - 1
    first_s = lax.axis_index("c") * half
    values = terms_ref[...].reshape(-1, 8, WIDTH)
    ids = source_ids(values, half)
    column = pl.multiple_of(lax.axis_index("x") * count * 8, 8)
    ids_ref[...] = source_ids(
        terms_ref[lax.axis_index("c"), pl.ds(column, count * 8)].reshape(ids_ref.shape), half
    )
    rows = [jnp.zeros((1, WIDTH), F32)] * 8
    for k in range(half):
        pattern = rule(upper_ref[first_s + k], lower_ref[first_s + k], half)
        rows[k], rows[half + k] = gathered(ids, values, pattern, half)
    flows_ref[...] = jnp.concatenate(rows)


def partial_kernel(flows_ref, picked_ref, rows_ref, merged_ref, spread_ref, tile_ref):
    half = picked_ref.shape[1] // 2
    piece = picked_ref.shape[2] - 8
    start = pl.multiple_of(lax.axis_index("y") * piece, 8)
    merged = picked_ref[0]
    for d in range(1, picked_ref.shape[0]):
        merged = merged + picked_ref[d]
    merged_ref[:, : piece + 8] = merged
    merged_ref[:, piece + 8 :] = jnp.zeros(
        (2 * half, merged_ref.shape[1] - piece - 8, WIDTH), F32
    )
    tile_ref[...] = jnp.zeros(tile_ref.shape, F32)
    payload = [jnp.zeros((1, WIDTH), F32)] * 8
    ends = [jnp.zeros((1, WIDTH), F32)] * 8
    for k in range(half):
        other = half + k
        ends[k] = merged[k, piece : piece + 1]
        ends[other] = merged[other, piece + 1 : piece + 2]
        tile_ref[k, pl.ds(start, piece)] = merged[k, :piece]
        tile_ref[other, pl.ds(start, piece)] = merged[other, :piece]
        payload[k] = applied(tile_ref[k], ends[k] + flows_ref[k : k + 1])
        payload[other] = applied_transposed(
            tile_ref[other], ends[other] + flows_ref[other : other + 1]
        )
    rows_ref[...] = jnp.concatenate(ends)
    spread_rows(payload, spread_ref)


def second_kernel(parts_ref, schur_ref, base_ref, spread_ref):
    step(summed(parts_ref), None, schur_ref, 0.0, base_ref[0], spread_ref)


def third_kernel(parts_ref, ends_ref, schur_ref, rows_ref, base_ref, tiles_ref, spread_ref):
    piece = WIDTH // ends_ref.shape[0]
    for k in range(tiles_ref.shape[1]):
        keep(tiles_ref, k, jnp.concatenate([ends_ref[i, k, :piece] for i in range(ends_ref.shape[0])]))
    step(summed(parts_ref), tiles_ref, schur_ref, rows_ref[...], base_ref[0], spread_ref)


def step_kernel(parts_ref, tiles_ref, schur_ref, rows_ref, base_ref, spread_ref):
    step(summed(parts_ref), tiles_ref, schur_ref, rows_ref[...], base_ref[0], spread_ref)


def last_kernel(
    parts_ref, tiles_ref, rows_ref, before_ref, after_ref, passing_ref,
    inv_ref, residual_ref, cotangent_ref, shared_ref,
):
    half = before_ref.shape[1]
    c = lax.axis_index("c")
    total = summed(parts_ref)
    ends = total[:8] + rows_ref[...]
    out = [jnp.zeros((1, WIDTH), F32)] * 16
    for k in range(half):
        other = half + k
        head = applied(kept(tiles_ref, k), ends[k : k + 1])
        relief = applied_transposed(kept(tiles_ref, other), ends[other : other + 1])
        out[k] = applied(kept(before_ref, k), head) + passing_ref[k : k + 1]
        out[other] = applied_transposed(kept(after_ref, k), relief) + passing_ref[other : other + 1]
        residual = jnp.where(c == 1, residual_ref[other : other + 1], residual_ref[k : k + 1])
        cotangent = jnp.where(c == 1, cotangent_ref[other : other + 1], cotangent_ref[k : k + 1])
        out[8 + k] = applied(inv_ref[c * half + k], residual + total[8 + k : 9 + k])
        out[8 + other] = cotangent + total[8 + other : 9 + other]
    shared_ref[...] = jnp.concatenate(out)


def cells_kernel(
    shared_ref, other_ref, passing_ref, maps_ref, vectors_ref,
    update_ref, sections_ref, adjoint_ref, junction_ref,
):
    members, blocks = update_ref.shape[:2]
    half = members // 2
    c = lax.axis_index("c")
    for s in range(members):
        core, k = s // half, s % half
        sections_ref[s : s + 1] = shared_ref[core, 8 + k : 9 + k]
        junction_ref[s : s + 1] = shared_ref[core, 8 + half + k : 9 + half + k]
        enter = shared_ref[core, k : k + 1]
        leave = shared_ref[core, half + k : half + k + 1]
        matrix = kept(other_ref, s)
        further = applied(matrix, enter) + passing_ref[s, 0:1]
        nearer = applied_transposed(matrix, leave) + passing_ref[s, 1:2]
        enter = jnp.where(c == 1, further, enter)
        leave = jnp.where(c == 0, nearer, leave)
        rows, back = [], []
        for i in range(blocks):
            rows.append(
                applied((maps_ref[0, s, i], maps_ref[1, s, i]), enter) + vectors_ref[s, i : i + 1]
            )
            if i < blocks - 1:
                suffix = (maps_ref[0, s, blocks + i], maps_ref[1, s, blocks + i])
                change = applied_transposed(suffix, leave)
            else:
                change = leave
            back.append(change + vectors_ref[s, blocks + i : blocks + i + 1])
        update_ref[s] = jnp.concatenate(rows)
        adjoint_ref[s] = jnp.concatenate(back)


def swap(spread, axis):
    return lax.all_to_all(spread, axis, 0, 0, tiled=False)


def over_x(values):
    return swap(jnp.broadcast_to(values[None], (lax.axis_size("x"),) + values.shape), "x")


def exchanged(spread):
    along_x = over_x(swap(spread, "z"))
    return lax.all_gather(along_x.reshape(-1, WIDTH), "c")


def shards(
    reach_residual,
    chain_inv,
    chain_link,
    outlet_link,
    junction_inv,
    junction_residual,
    upper_junction,
    lower_junction,
    cell_cotangent,
    junction_cotangent,
):
    members, blocks, width = reach_residual.shape
    owned = junction_inv.shape[0]
    zs, xs, ys, cs = (lax.axis_size(a) for a in ("z", "x", "y", "c"))
    half = members // cs
    piece = width // ys
    bf16 = jnp.bfloat16
    lower, upper = lower_junction, upper_junction

    part = run(
        table_kernel,
        array(owned, piece + 8, width),
        junction_inv, junction_residual, junction_cotangent,
        where=hbm, limit=60,
        scratch=[
            pltpu.VMEM((owned, width), F32),
            pltpu.VMEM((owned, width), F32),
            pltpu.SemaphoreType.DMA((3,)),
        ],
    )
    table = lax.all_gather(part, "z").reshape(zs * owned, piece + 8, width)

    chain = (members, blocks, width, width)
    maps, vectors, local = run(
        local_kernel,
        [
            array(2, members, 2 * blocks - 1, width, width, dtype=bf16),
            array(members, 8, width),
            array(members, PACK, width),
        ],
        chain_inv, chain_link, reach_residual, cell_cotangent,
        where=hbm, limit=60, flops=2_000_000_000,
        scratch=[
            pltpu.VMEM(chain, F32),
            pltpu.VMEM(chain, F32),
            pltpu.VMEM((members, blocks, width), F32),
            pltpu.VMEM((members, blocks, width), F32),
            pltpu.SemaphoreType.DMA((2 + 2 * members,)),
        ],
    )
    pair = lax.all_gather(local, "c")
    chip, other, other_rows = run(
        pair_kernel,
        [array(half, PACK, width), array(2, members, width, width, dtype=bf16), array(members, 8, width)],
        pair,
    )
    chips = lax.all_gather(chip, "y")
    matrices = array(2, half, width, width, dtype=bf16)
    schur, before, after, passing, first = run(
        chain_kernel,
        [matrices, matrices, matrices, array(8, width), array(zs, 8, width)],
        lower, upper, chips, outlet_link, scalars=2,
    )

    terms = exchanged(first)
    plane = lax.dynamic_slice(
        terms.reshape(cs, xs, zs, 8, width),
        (0, 0, lax.axis_index("z"), 2 * half, 0),
        (cs, xs, 1, 1, owned),
    ).reshape(-1).astype(jnp.int32)
    ids, flows = run(
        flows_kernel,
        [array(zs, 8, width, dtype=jnp.int32), array(8, width)],
        lower, upper, terms, scalars=2,
    )
    plane, flows = lax.optimization_barrier((plane, flows))
    picked = run(pick_kernel, array(xs, owned, piece + 8, width), plane, table, scalars=1)
    rows, merged, parts = run(
        partial_kernel,
        [array(8, width), array(owned, 2 * piece + 24, width), array(ys, 8, width)],
        flows, swap(picked, "x"),
        scratch=[pltpu.VMEM((owned, width, width), F32)],
    )
    parts, merged = lax.optimization_barrier((parts, merged))
    ends = lax.all_gather(merged, "y")
    sides = ("x", "c")

    def sums(spread, own):
        kernel = functools.partial(sums_kernel, half=half, cores=cs, own=own)
        shape = array(xs * cs, 16 if own else 8, width)
        return swap(run(kernel, shape, plane, ids, swap(spread, "z"), scalars=1), sides)

    spread = run(second_kernel, array(zs, 8, width), swap(parts, "y"), schur, first)
    tiles, spread = run(
        third_kernel,
        [array(2, 2 * half, width, width, dtype=bf16), array(zs, 8, width)],
        sums(spread, False), ends, schur, rows, first,
    )
    for sweep in range(3, SWEEPS):
        spread = run(
            step_kernel, array(zs, 8, width), sums(spread, False), tiles, schur, rows, first
        )
    shared = run(
        last_kernel, array(16, width), sums(spread, True), tiles, rows, before, after, passing,
        junction_inv, junction_residual, junction_cotangent,
    )
    cell_update, sections, cell_adjoint, adjoint = run(
        cells_kernel,
        [
            array(members, blocks, width), array(owned, width),
            array(members, blocks, width), array(owned, width),
        ],
        lax.all_gather(shared, "c"), other, other_rows, maps, vectors,
    )
    return (cell_update, sections, cell_adjoint, adjoint)


def solution(mesh):
    basins = mesh.shape["basin"]
    grid = Mesh(mesh.devices.reshape(basins // 4, 4, 4, 2), ("z", "x", "y", "c"))
    b, r = ("z", "x"), ("y", "c")
    return jax.shard_map(
        shards,
        mesh=grid,
        in_specs=(
            P(b, r, None),
            P(b, r, None, None),
            P(b, r, None, None),
            P(b, None, None),
            P(b, None, None),
            P(b, None),
            P(b),
            P(b),
            P(b, r, None),
            P(b, None),
        ),
        out_specs=(P(b, r, None), P(b, None), P(b, r, None), P(b, None)),
        check_vma=False,
    )
```

```python
import functools

import jax
import jax.numpy as jnp
from jax import lax
from jax.experimental import pallas as pl
from jax.experimental.pallas import tpu as pltpu
from jax.sharding import Mesh, PartitionSpec as P

SWEEPS = 4
WIDTH = 128
PACK = WIDTH + 8
F32 = jnp.float32

smem = pl.BlockSpec(memory_space=pltpu.SMEM)
vmem = pl.BlockSpec(memory_space=pltpu.VMEM)
hbm = pl.BlockSpec(memory_space=pltpu.HBM)


def array(*shape, dtype=F32):
    return jax.ShapeDtypeStruct(shape, dtype)


def run(kernel, outs, *args, scalars=0, where=vmem, scratch=(), limit=40, flops=0):
    single = not isinstance(outs, list)
    shapes = [outs] if single else outs
    result = pl.pallas_call(
        kernel,
        out_shape=shapes,
        in_specs=[smem] * scalars + [where] * (len(args) - scalars),
        out_specs=[vmem] * len(shapes),
        scratch_shapes=scratch,
        compiler_params=pltpu.CompilerParams(vmem_limit_bytes=limit * 1024 * 1024),
        cost_estimate=pl.CostEstimate(flops=flops, bytes_accessed=flops // 100, transcendentals=0) if flops else None,
    )(*args)
    return result[0] if single else result


def two_parts(a):
    high = a.astype(jnp.bfloat16)
    return high, (a - high.astype(F32)).astype(jnp.bfloat16)


def dot(a, b, transposed=False):
    dims = (((1,), (1 if transposed else 0,)), ((), ()))
    return lax.dot_general(a, b, dims, preferred_element_type=F32)


def parts_of(a):
    return a if isinstance(a, tuple) else two_parts(a)


def product(a, b):
    (ah, al), (bh, bl) = parts_of(a), parts_of(b)
    return dot(ah, bh) + (dot(ah, bl) + dot(al, bh))


def along(vector, matrix, transposed):
    vh, vl = two_parts(vector)
    mh, ml = parts_of(matrix)
    both = dot(jnp.concatenate([vh, vl]), mh, transposed)
    return both[0:1] + (both[1:2] + dot(vh, ml, transposed))


def applied(matrix, row):
    return along(row, matrix, True)


def applied_transposed(matrix, row):
    return along(row, matrix, False)


def fetch(pairs, sems):
    copies = [pltpu.make_async_copy(src, dst, sems.at[i]) for i, (src, dst) in enumerate(pairs)]
    for copy in copies:
        copy.start()
    return copies


def table_kernel(inv_ref, residual_ref, cotangent_ref, out_ref, residual, cotangent, sems):
    piece = out_ref.shape[1] - 8
    start = pl.multiple_of(lax.axis_index("y") * piece, 8)
    copies = fetch(
        [
            (inv_ref.at[:, pl.ds(start, piece)], out_ref.at[:, :piece]),
            (residual_ref, residual),
            (cotangent_ref, cotangent),
        ],
        sems,
    )
    for copy in copies[1:]:
        copy.wait()
    for k in range(out_ref.shape[0]):
        out_ref[k, piece:] = jnp.concatenate(
            [residual[k : k + 1], cotangent[k : k + 1], jnp.zeros((6, WIDTH), F32)]
        )
    copies[0].wait()


def local_kernel(
    inv_hbm, link_hbm, residual_hbm, cotangent_hbm, maps_ref, vectors_ref, out_ref,
    inv_ref, link_ref, residual_ref, cotangent_ref, sems,
):
    members, blocks = inv_ref.shape[:2]
    pairs = [(residual_hbm, residual_ref), (cotangent_hbm, cotangent_ref)]
    for s in range(members):
        pairs += [(inv_hbm.at[s], inv_ref.at[s]), (link_hbm.at[s], link_ref.at[s])]
    copies = fetch(pairs, sems)
    copies[0].wait()
    copies[1].wait()
    for s in range(members):
        copies[2 + 2 * s].wait()
        copies[3 + 2 * s].wait()
        m, f = [], []
        for i in range(blocks):
            inverse = two_parts(inv_ref[s, i])
            m.append(two_parts(product(inverse, two_parts(link_ref[s, i]))))
            f.append(applied(inverse, residual_ref[s, i : i + 1]))
        rows = [jnp.zeros((1, WIDTH), F32)] * 8
        total, vector = m[0], f[0]
        for i in range(blocks):
            if i:
                result = product(m[i], total)
                total = two_parts(result)
                vector = applied(m[i], vector) + f[i]
            maps_ref[0, s, i], maps_ref[1, s, i] = total
            rows[i] = vector
        back = cotangent_ref[s, blocks - 1 : blocks]
        rows[2 * blocks - 1] = back
        suffix = None
        for i in range(blocks - 2, -1, -1):
            back = cotangent_ref[s, i : i + 1] + applied_transposed(m[i + 1], back)
            rows[blocks + i] = back
            suffix = m[i + 1] if suffix is None else two_parts(product(suffix, m[i + 1]))
            maps_ref[0, s, blocks + i], maps_ref[1, s, blocks + i] = suffix
        vectors_ref[s] = jnp.concatenate(rows)
        out_ref[s, :WIDTH] = result
        out_ref[s, WIDTH:] = jnp.concatenate(
            [vector, applied_transposed(m[0], back), jnp.zeros((6, WIDTH), F32)]
        )


def pair_kernel(pair_ref, out_ref, other_ref, rows_ref):
    half = out_ref.shape[0]
    c = lax.axis_index("c")
    first_s = c * half
    for k in range(half):
        first, second = pair_ref[0, first_s + k], pair_ref[1, first_s + k]
        one, two = two_parts(first[:WIDTH]), two_parts(second[:WIDTH])
        out_ref[k, :WIDTH] = product(two, one)
        out_ref[k, WIDTH:] = jnp.concatenate(
            [
                applied(two, first[WIDTH : WIDTH + 1]) + second[WIDTH : WIDTH + 1],
                applied_transposed(one, second[WIDTH + 1 : WIDTH + 2])
                + first[WIDTH + 1 : WIDTH + 2],
                jnp.zeros((6, WIDTH), F32),
            ]
        )
    for s in range(other_ref.shape[1]):
        keep(other_ref, s, pair_ref[1 - c, s, :WIDTH])
        rows_ref[s] = pair_ref[1 - c, s, WIDTH:]


def keep(ref, k, matrix):
    ref[0, k], ref[1, k] = two_parts(matrix)


def kept(ref, k):
    return ref[0, k], ref[1, k]


def chain_kernel(lower_ref, upper_ref, chips_ref, outlet_ref, schur_ref, before_ref, after_ref, rows_ref, spread_ref):
    chips, half = chips_ref.shape[:2]
    first_s = lax.axis_index("c") * half
    y = lax.axis_index("y")
    row = lax.broadcasted_iota(jnp.int32, (8, WIDTH), 0)
    lane = lax.broadcasted_iota(jnp.int32, (8, WIDTH), 1)
    eye = (
        lax.broadcasted_iota(jnp.int32, (WIDTH, WIDTH), 0)
        == lax.broadcasted_iota(jnp.int32, (WIDTH, WIDTH), 1)
    ).astype(F32)
    nothing = jnp.zeros((1, WIDTH), F32)
    ids = jnp.zeros((8, WIDTH), jnp.int32)
    payload = [nothing] * 8
    for k in range(half):
        ids = jnp.where(lane == k, lower_ref[first_s + k], ids)
        ids = jnp.where(lane == half + k, upper_ref[first_s + k], ids)
        maps = [two_parts(chips_ref[i, k, :WIDTH]) for i in range(chips)]
        before, before_row = eye, nothing
        reached, reached_row = chips_ref[0, k, :WIDTH], chips_ref[0, k, WIDTH : WIDTH + 1]
        for i in range(1, chips):
            before = jnp.where(y == i, reached, before)
            before_row = jnp.where(y == i, reached_row, before_row)
            if i < chips - 1:
                reached = product(maps[i], reached)
            reached_row = applied(maps[i], reached_row) + chips_ref[i, k, WIDTH : WIDTH + 1]
        schur = outlet_ref[first_s + k]
        payload[k] = applied(schur, reached_row)
        after = schur
        upward, after_row = nothing, nothing
        for i in range(chips - 1, -1, -1):
            after = jnp.where(y == i, schur, after)
            after_row = jnp.where(y == i, upward, after_row)
            schur = product(schur, maps[i])
            upward = applied_transposed(maps[i], upward) + chips_ref[i, k, WIDTH + 1 : WIDTH + 2]
        payload[half + k] = upward
        keep(schur_ref, k, schur)
        keep(before_ref, k, before)
        keep(after_ref, k, after)
        rows_ref[k : k + 1] = before_row
        rows_ref[half + k : half + k + 1] = after_row
    rows_ref[2 * half :] = jnp.zeros((2, WIDTH), F32)
    full = jnp.where(row == 2 * half, ids.astype(F32), jnp.concatenate(payload))
    for i in range(spread_ref.shape[0]):
        spread_ref[i] = full


def pick_kernel(ids_ref, table_ref, out_ref):
    dests = out_ref.shape[0]
    piece = table_ref.shape[1] - 8
    owned = (out_ref.shape[1] - 8) // piece
    half = owned // 2
    x, c = lax.axis_index("x"), lax.axis_index("c")
    for d in range(dests):
        ends = []
        for t in range(owned):
            junction = ids_ref[(c * dests + d) * owned + (t + half) % owned]
            basin = lax.div(junction, owned)
            line = lax.div(basin, dests)
            at = line * owned + (junction - basin * owned)
            here = basin - line * dests == x
            found = jnp.where(here, table_ref[at], 0.0)
            out_ref[d, t * piece : (t + 1) * piece] = found[:piece]
            row = piece + (0 if t < half else 1)
            ends.append(found[row : row + 1])
        out_ref[d, owned * piece :] = jnp.concatenate(ends + [jnp.zeros((2, WIDTH), F32)])


def rule(above, below, half):
    row = lax.broadcasted_iota(jnp.int32, (8, WIDTH), 0)
    return jnp.where(row < half, above, jnp.where(row < 2 * half, below, -2))


def gathered(ids, values, pattern, half):
    total = jnp.sum(jnp.where(ids == pattern[None], values, 0.0), axis=0)
    inflow, outflow = total[0:1], total[half : half + 1]
    for k in range(1, half):
        inflow = inflow + total[k : k + 1]
        outflow = outflow + total[half + k : half + k + 1]
    return inflow, outflow


def source_ids(values, half):
    row = lax.broadcasted_iota(jnp.int32, (8, WIDTH), 0)
    lane = lax.broadcasted_iota(jnp.int32, (8, WIDTH), 1)
    chosen = jnp.where((row == lane) & (row < 2 * half), values[:, 2 * half : 2 * half + 1], 0.0)
    ids = jnp.sum(chosen, axis=2, keepdims=True).astype(jnp.int32)
    return jnp.broadcast_to(ids, values.shape)


def sums_kernel(plane_ref, ids_ref, terms_ref, out_ref, *, half, cores, own):
    ids, values = ids_ref[...], terms_ref[...]
    sides = out_ref.shape[0] // cores
    owned = cores * half
    line = lax.axis_index("z") * sides
    nothing = jnp.zeros((1, WIDTH), F32)
    for d in range(out_ref.shape[0]):
        x, c = d // cores, d % cores
        at = (c * sides + x) * owned
        rows = [nothing] * out_ref.shape[1]
        for k in range(half):
            pattern = rule(plane_ref[at + half + k], plane_ref[at + k], half)
            rows[k], rows[half + k] = gathered(ids, values, pattern, half)
            if own:
                junction = (line + x) * owned + c * half + k
                pattern = rule(junction, junction, half)
                rows[8 + k], rows[8 + half + k] = gathered(ids, values, pattern, half)
        out_ref[d] = jnp.concatenate(rows)


def summed(parts_ref):
    total = parts_ref[0]
    for i in range(1, parts_ref.shape[0]):
        total = total + parts_ref[i]
    return total


def spread_rows(payload, spread_ref):
    full = jnp.concatenate(payload)
    for i in range(spread_ref.shape[0]):
        spread_ref[i] = full


def step(total, tiles_ref, schur_ref, ends, base, spread_ref):
    half = schur_ref.shape[1]
    payload = [jnp.zeros((1, WIDTH), F32)] * 8
    total = total + ends
    for k in range(half):
        other = half + k
        head, relief = total[k : k + 1], total[other : other + 1]
        if tiles_ref is not None:
            head = applied(kept(tiles_ref, k), head)
            relief = applied_transposed(kept(tiles_ref, other), relief)
        schur = kept(schur_ref, k)
        payload[k] = base[k : k + 1] + applied(schur, head)
        payload[other] = base[other : other + 1] + applied_transposed(schur, relief)
    spread_rows(payload, spread_ref)


def flows_kernel(lower_ref, upper_ref, terms_ref, ids_ref, flows_ref):
    count = ids_ref.shape[0]
    half = flows_ref.shape[0] // 2 - 1
    first_s = lax.axis_index("c") * half
    values = terms_ref[...].reshape(-1, 8, WIDTH)
    ids = source_ids(values, half)
    column = pl.multiple_of(lax.axis_index("x") * count * 8, 8)
    ids_ref[...] = source_ids(
        terms_ref[lax.axis_index("c"), pl.ds(column, count * 8)].reshape(ids_ref.shape), half
    )
    rows = [jnp.zeros((1, WIDTH), F32)] * 8
    for k in range(half):
        pattern = rule(upper_ref[first_s + k], lower_ref[first_s + k], half)
        rows[k], rows[half + k] = gathered(ids, values, pattern, half)
    flows_ref[...] = jnp.concatenate(rows)


def partial_kernel(flows_ref, picked_ref, rows_ref, merged_ref, spread_ref, tile_ref):
    owned = merged_ref.shape[0]
    half = owned // 2
    piece = (picked_ref.shape[1] - 8) // owned
    start = pl.multiple_of(lax.axis_index("y") * piece, 8)
    merged = picked_ref[0]
    for d in range(1, picked_ref.shape[0]):
        merged = merged + picked_ref[d]
    ends = merged[owned * piece :]
    rows_ref[...] = ends
    merged_ref[:, piece:] = jnp.zeros((owned, merged_ref.shape[1] - piece, WIDTH), F32)
    tile_ref[...] = jnp.zeros(tile_ref.shape, F32)
    for k in range(owned):
        rows = merged[k * piece : (k + 1) * piece]
        merged_ref[k, :piece] = rows
        tile_ref[k, pl.ds(start, piece)] = rows
    full = ends + flows_ref[...]
    payload = [jnp.zeros((1, WIDTH), F32)] * 8
    for k in range(half):
        other = half + k
        payload[k] = applied(tile_ref[k], full[k : k + 1])
        payload[other] = applied_transposed(tile_ref[other], full[other : other + 1])
    spread_rows(payload, spread_ref)


def second_kernel(parts_ref, schur_ref, base_ref, spread_ref):
    step(summed(parts_ref), None, schur_ref, 0.0, base_ref[0], spread_ref)


def third_kernel(parts_ref, ends_ref, schur_ref, rows_ref, base_ref, tiles_ref, spread_ref):
    piece = WIDTH // ends_ref.shape[0]
    for k in range(tiles_ref.shape[1]):
        keep(tiles_ref, k, jnp.concatenate([ends_ref[i, k, :piece] for i in range(ends_ref.shape[0])]))
    step(summed(parts_ref), tiles_ref, schur_ref, rows_ref[...], base_ref[0], spread_ref)


def step_kernel(parts_ref, tiles_ref, schur_ref, rows_ref, base_ref, spread_ref):
    step(summed(parts_ref), tiles_ref, schur_ref, rows_ref[...], base_ref[0], spread_ref)


def last_kernel(
    parts_ref, tiles_ref, rows_ref, before_ref, after_ref, passing_ref,
    inv_ref, residual_ref, cotangent_ref, shared_ref,
):
    half = before_ref.shape[1]
    c = lax.axis_index("c")
    total = summed(parts_ref)
    ends = total[:8] + rows_ref[...]
    out = [jnp.zeros((1, WIDTH), F32)] * 16
    for k in range(half):
        other = half + k
        head = applied(kept(tiles_ref, k), ends[k : k + 1])
        relief = applied_transposed(kept(tiles_ref, other), ends[other : other + 1])
        out[k] = applied(kept(before_ref, k), head) + passing_ref[k : k + 1]
        out[other] = applied_transposed(kept(after_ref, k), relief) + passing_ref[other : other + 1]
        residual = jnp.where(c == 1, residual_ref[other : other + 1], residual_ref[k : k + 1])
        cotangent = jnp.where(c == 1, cotangent_ref[other : other + 1], cotangent_ref[k : k + 1])
        out[8 + k] = applied(inv_ref[c * half + k], residual + total[8 + k : 9 + k])
        out[8 + other] = cotangent + total[8 + other : 9 + other]
    shared_ref[...] = jnp.concatenate(out)


def cells_kernel(
    shared_ref, other_ref, passing_ref, maps_ref, vectors_ref,
    update_ref, sections_ref, adjoint_ref, junction_ref,
):
    members, blocks = update_ref.shape[:2]
    half = members // 2
    c = lax.axis_index("c")
    for s in range(members):
        core, k = s // half, s % half
        sections_ref[s : s + 1] = shared_ref[core, 8 + k : 9 + k]
        junction_ref[s : s + 1] = shared_ref[core, 8 + half + k : 9 + half + k]
        enter = shared_ref[core, k : k + 1]
        leave = shared_ref[core, half + k : half + k + 1]
        matrix = kept(other_ref, s)
        further = applied(matrix, enter) + passing_ref[s, 0:1]
        nearer = applied_transposed(matrix, leave) + passing_ref[s, 1:2]
        enter = jnp.where(c == 1, further, enter)
        leave = jnp.where(c == 0, nearer, leave)
        rows, back = [], []
        for i in range(blocks):
            rows.append(
                applied((maps_ref[0, s, i], maps_ref[1, s, i]), enter) + vectors_ref[s, i : i + 1]
            )
            if i < blocks - 1:
                suffix = (maps_ref[0, s, blocks + i], maps_ref[1, s, blocks + i])
                change = applied_transposed(suffix, leave)
            else:
                change = leave
            back.append(change + vectors_ref[s, blocks + i : blocks + i + 1])
        update_ref[s] = jnp.concatenate(rows)
        adjoint_ref[s] = jnp.concatenate(back)


def swap(spread, axis):
    return lax.all_to_all(spread, axis, 0, 0, tiled=False)


def over_x(values):
    return swap(jnp.broadcast_to(values[None], (lax.axis_size("x"),) + values.shape), "x")


def exchanged(spread):
    along_x = over_x(swap(spread, "z"))
    return lax.all_gather(along_x.reshape(-1, WIDTH), "c")


def shards(
    reach_residual,
    chain_inv,
    chain_link,
    outlet_link,
    junction_inv,
    junction_residual,
    upper_junction,
    lower_junction,
    cell_cotangent,
    junction_cotangent,
):
    members, blocks, width = reach_residual.shape
    owned = junction_inv.shape[0]
    zs, xs, ys, cs = (lax.axis_size(a) for a in ("z", "x", "y", "c"))
    half = members // cs
    piece = width // ys
    bf16 = jnp.bfloat16
    lower, upper = lower_junction, upper_junction

    part = run(
        table_kernel,
        array(owned, piece + 8, width),
        junction_inv, junction_residual, junction_cotangent,
        where=hbm, limit=60,
        scratch=[
            pltpu.VMEM((owned, width), F32),
            pltpu.VMEM((owned, width), F32),
            pltpu.SemaphoreType.DMA((3,)),
        ],
    )
    table = lax.all_gather(part, "z").reshape(zs * owned, piece + 8, width)

    chain = (members, blocks, width, width)
    maps, vectors, local = run(
        local_kernel,
        [
            array(2, members, 2 * blocks - 1, width, width, dtype=bf16),
            array(members, 8, width),
            array(members, PACK, width),
        ],
        chain_inv, chain_link, reach_residual, cell_cotangent,
        where=hbm, limit=60, flops=2_000_000_000,
        scratch=[
            pltpu.VMEM(chain, F32),
            pltpu.VMEM(chain, F32),
            pltpu.VMEM((members, blocks, width), F32),
            pltpu.VMEM((members, blocks, width), F32),
            pltpu.SemaphoreType.DMA((2 + 2 * members,)),
        ],
    )
    pair = lax.all_gather(local, "c")
    chip, other, other_rows = run(
        pair_kernel,
        [array(half, PACK, width), array(2, members, width, width, dtype=bf16), array(members, 8, width)],
        pair,
    )
    chips = lax.all_gather(chip, "y")
    matrices = array(2, half, width, width, dtype=bf16)
    schur, before, after, passing, first = run(
        chain_kernel,
        [matrices, matrices, matrices, array(8, width), array(zs, 8, width)],
        lower, upper, chips, outlet_link, scalars=2,
    )

    terms = exchanged(first)
    plane = lax.dynamic_slice(
        terms.reshape(cs, xs, zs, 8, width),
        (0, 0, lax.axis_index("z"), 2 * half, 0),
        (cs, xs, 1, 1, owned),
    ).reshape(-1).astype(jnp.int32)
    ids, flows = run(
        flows_kernel,
        [array(zs, 8, width, dtype=jnp.int32), array(8, width)],
        lower, upper, terms, scalars=2,
    )
    plane, flows = lax.optimization_barrier((plane, flows))
    picked = run(pick_kernel, array(xs, owned * piece + 8, width), plane, table, scalars=1)
    rows, merged, parts = run(
        partial_kernel,
        [array(8, width), array(owned, 2 * piece + 24, width), array(ys, 8, width)],
        flows, swap(picked, "x"),
        scratch=[pltpu.VMEM((owned, width, width), F32)],
    )
    parts, merged = lax.optimization_barrier((parts, merged))
    ends = lax.all_gather(merged, "y")
    sides = ("x", "c")

    def sums(spread, own):
        kernel = functools.partial(sums_kernel, half=half, cores=cs, own=own)
        shape = array(xs * cs, 16 if own else 8, width)
        return swap(run(kernel, shape, plane, ids, swap(spread, "z"), scalars=1), sides)

    spread = run(second_kernel, array(zs, 8, width), swap(parts, "y"), schur, first)
    tiles, spread = run(
        third_kernel,
        [array(2, 2 * half, width, width, dtype=bf16), array(zs, 8, width)],
        sums(spread, False), ends, schur, rows, first,
    )
    for sweep in range(3, SWEEPS):
        spread = run(
            step_kernel, array(zs, 8, width), sums(spread, False), tiles, schur, rows, first
        )
    shared = run(
        last_kernel, array(16, width), sums(spread, True), tiles, rows, before, after, passing,
        junction_inv, junction_residual, junction_cotangent,
    )
    cell_update, sections, cell_adjoint, adjoint = run(
        cells_kernel,
        [
            array(members, blocks, width), array(owned, width),
            array(members, blocks, width), array(owned, width),
        ],
        lax.all_gather(shared, "c"), other, other_rows, maps, vectors,
    )
    return (cell_update, sections, cell_adjoint, adjoint)


def solution(mesh):
    basins = mesh.shape["basin"]
    grid = Mesh(mesh.devices.reshape(basins // 4, 4, 4, 2), ("z", "x", "y", "c"))
    b, r = ("z", "x"), ("y", "c")
    return jax.shard_map(
        shards,
        mesh=grid,
        in_specs=(
            P(b, r, None),
            P(b, r, None, None),
            P(b, r, None, None),
            P(b, None, None),
            P(b, None, None),
            P(b, None),
            P(b),
            P(b),
            P(b, r, None),
            P(b, None),
        ),
        out_specs=(P(b, r, None), P(b, None), P(b, r, None), P(b, None)),
        check_vma=False,
    )
```
